32 devices in a mesh: groups: 2 (over x), tensor: 16 (over z, y, core).
Axes of the slice: x: 2, y: 2, z: 4, core: 2. Of those that a mesh axis runs over, the one named last changes fastest.
Arguments:
- attended: bfloat16 [512, 8192], P('groups', 'tensor'), parts along dimension 0, may hold values from -6 to 6
- out_weight: bfloat16 [8192, 8192], P('tensor'), may hold values from -0.09375 to 0.09375
- adapter_down: bfloat16 [32, 8192, 64], P(('groups', 'tensor')), parts along dimension 0, may hold values from -0.0625 to 0.0625
- adapter_up: bfloat16 [32, 64, 8192], P(('groups', 'tensor')), parts along dimension 0, may hold values from -0.75 to 0.75
- row_adapter: int32 [512], P('groups'), parts along dimension 0, may hold values from 0 to 15, as said below
- adapter_slot: int32 [32], P('groups'), parts along dimension 0, may hold values from 0 to 15, as said below
Outputs:
- projected: bfloat16 [512, 8192], P('groups', 'tensor'), parts along dimension 0
The draws below stay inside these ranges and needn't reach their ends.
There are 2 independent parts, one for each index of `groups`. The reference program is written for one: setup_inputs(seed, part) draws one part's arguments, and reference() takes and returns one part's arrays. A program takes and returns all parts, laid end to end along the dimension named above; an argument that names none is the same for every part. Nothing has to cross between parts.
Inputs may be any that keep to these rules, and one draw needn't show every extreme that they name: adapter_slot is a permutation: adapter a is stored at position adapter_slot[a]; positions s with equal s // 1 lie on one device of the tensor axis. `row_adapter`: at most 32 rows have adapters stored on one device of the tensor axis, and exactly 32 on some device.
All inputs are finite; a program needn't handle non-finite values.
Results may differ from the reference program's by a relative error of at most 0.0046.
Values may be sent and summed in bfloat16 or wider, within the bound.
No kernel may reach another device: no remote copies, remote signals or barrier semaphores. Data moves between devices by JAX's collectives and lax.ppermute only.
A program may use at most 192 MiB of HBM per device.

```python
import jax
import jax.numpy as jnp
from jax import lax

D = 8192
RANK = 64
ADP_DEV = 1
ADAPTERS = 16
ROWS = 256
CAP = 32
N_TENSOR = 16


def shared_routing(key):
    key_perm, key_score, key_hot, key_local, key_order = jax.random.split(key, 5)
    placed = jax.random.permutation(key_perm, ADAPTERS).astype(jnp.int32)
    total_slots = N_TENSOR * CAP
    slot_ids = jnp.arange(total_slots, dtype=jnp.int32)
    scores = jax.random.randint(key_score, (total_slots,), 0, 2 ** 18, dtype=jnp.int32) * total_slots + slot_ids
    hot_owner = jax.random.randint(key_hot, (), 0, N_TENSOR, dtype=jnp.int32)
    scores = jnp.where(slot_ids // CAP == hot_owner, slot_ids - total_slots, scores)
    chosen = jnp.argsort(scores, stable=True)[:ROWS].astype(jnp.int32)
    owners = chosen // CAP
    local_index = jax.random.randint(key_local, (ROWS,), 0, ADP_DEV, dtype=jnp.int32)
    stored = owners * ADP_DEV + local_index
    inverse = jnp.argsort(placed).astype(jnp.int32)
    row_ids = inverse[stored]
    shuffle = jax.random.permutation(key_order, ROWS).astype(jnp.int32)
    return (placed, row_ids[shuffle])


def draw_row_adapter(key, part):
    placed, row_ids = shared_routing(key)
    return row_ids


def draw_adapter_slot(key, part):
    placed, row_ids = shared_routing(key)
    return placed


def with_spikes(result, rng, source, target, shards_of, factor):
    def block_of(dim):
        return (jnp.arange(result.shape[dim]) // (result.shape[dim] // shards_of)).reshape((-1,) + (1,) * (result.ndim - 1 - dim))

    one_side = jax.random.permutation(rng, shards_of)[block_of(target)]
    other_side = (block_of(target) + shards_of // 2) % shards_of
    return jnp.where((block_of(source) == one_side) | (block_of(source) == other_side), factor * result, result)


def levels(stream_key, extent, cuts, smallest, top_value):
    gain, own = 1.0, jax.random.fold_in(stream_key, 6)
    for position, shards_of in cuts:
        steps = jnp.exp(jax.random.uniform(jax.random.fold_in(own, position), (shards_of,), jnp.float32, smallest / len(cuts), top_value / len(cuts)))
        gain = gain * jnp.repeat(steps, extent[position] // shards_of).reshape([-1 if axis == position else 1 for axis in range(len(extent))])
    return gain


def normal_values(own_key, dims, width, most, shards=(), kind=jnp.bfloat16):
    factor_of = levels(own_key, dims, shards, -0.22, 0.18) if shards else 1.0
    result = jax.random.normal(own_key, dims, jnp.float32) * width * factor_of
    return jnp.minimum(jnp.maximum(result, -most), most).astype(kind)


def bell_draw_with(own_key, shape, spread, limit, pieces, heavy, held_as=jnp.bfloat16):
    entries = spread * jax.random.normal(own_key, shape, jnp.float32)
    if pieces:
        entries = entries * levels(own_key, shape, pieces, -0.22, 0.18)
    return jnp.clip(with_spikes(entries, jax.random.fold_in(own_key, 3), *heavy), -limit, limit).astype(held_as)


def setup_inputs(seed: int = 0, part: int = 0) -> dict:
    arg_keys = jax.random.split(jax.random.key(seed), 7)
    part_keys = jax.random.split(jax.random.fold_in(arg_keys[6], part), 7)
    return {
        "attended": normal_values(part_keys[0], (ROWS, D), 1.0, 6.0, ((1, 16),)),
        "out_weight": bell_draw_with(arg_keys[1], (D, D), D ** -0.5, 0.09375, ((0, 16),), (0, 1, 16, 2.0)),
        "adapter_down": normal_values(part_keys[2], (ADAPTERS, D, RANK), D ** -0.5, 0.0625, ((0, 16),)),
        "adapter_up": normal_values(part_keys[3], (ADAPTERS, RANK, D), RANK ** -0.5, 0.75, ((0, 16),)),
        "row_adapter": draw_row_adapter(jax.random.fold_in(jax.random.fold_in(arg_keys[6], part), 71), part),
        "adapter_slot": draw_adapter_slot(jax.random.fold_in(jax.random.fold_in(arg_keys[6], part), 71), part),
    }


def reference(attended, out_weight, adapter_down, adapter_up, row_adapter, adapter_slot):
    storage = adapter_slot[row_adapter]
    base_out = jnp.dot(attended, out_weight, preferred_element_type=jnp.float32)

    def one_row(row_item):
        vector, slot_index = row_item
        shrunk = jnp.dot(vector[None, :], adapter_down[slot_index], preferred_element_type=jnp.float32).astype(jnp.bfloat16)
        grown = jnp.dot(shrunk, adapter_up[slot_index], preferred_element_type=jnp.float32).astype(jnp.bfloat16)
        return grown[0]

    delta_out = lax.map(one_row, (attended, storage))
    return (base_out + delta_out.astype(jnp.float32)).astype(jnp.bfloat16)
```

```python
import functools

import jax
import jax.numpy as jnp
from jax import lax
from jax.experimental import pallas as pl
from jax.experimental.pallas import tpu as pltpu
from jax.sharding import PartitionSpec as P

CAP = 32
VMEM = pltpu.VMEM
SMEM = pltpu.SMEM


def params(mib):
    return pltpu.CompilerParams(vmem_limit_bytes=mib * 1024 * 1024)


def cost(flops, moved):
    return pl.CostEstimate(flops=flops, bytes_accessed=moved, transcendentals=0)


def swap(value, mask, count):
    return lax.ppermute(value, "tensor", [(t, t ^ mask) for t in range(count)])


def route_kernel(count, me_ref, slot_ref, row_ref, attended_ref, outgoing_ref, picks_ref):
    rows = attended_ref.shape[0]
    ids = row_ref[...]
    owner = jnp.zeros_like(ids)
    for a in range(slot_ref.shape[0]):
        owner = jnp.where(ids == a, slot_ref[a], owner)
    hot = (lax.broadcasted_iota(jnp.int32, (count, rows), 0) == owner).astype(jnp.float32)
    earlier = (
        lax.broadcasted_iota(jnp.int32, (rows, rows), 0)
        < lax.broadcasted_iota(jnp.int32, (rows, rows), 1)
    ).astype(jnp.bfloat16)
    ahead = jnp.dot(hot.astype(jnp.bfloat16), earlier, preferred_element_type=jnp.float32)
    place = jnp.sum(ahead * hot, axis=0, keepdims=True).astype(jnp.int32)
    target = owner * CAP + place
    slots = lax.broadcasted_iota(jnp.int32, (count * CAP, rows), 0)
    select = (slots == target).astype(jnp.bfloat16)
    outgoing_ref[...] = jnp.dot(
        select, attended_ref[...], preferred_element_type=jnp.float32
    ).astype(jnp.bfloat16)
    me = me_ref[0]
    local = lax.broadcasted_iota(jnp.int32, (CAP, rows), 0)
    picks_ref[:CAP, :] = (local + me * CAP == target).astype(jnp.bfloat16)
    picks_ref[CAP:, :] = (local + (me ^ 1) * CAP == target).astype(jnp.bfloat16)


def route(me, adapter_slot, row_adapter, attended, count):
    rows, width = attended.shape
    return pl.pallas_call(
        functools.partial(route_kernel, count),
        out_shape=(
            jax.ShapeDtypeStruct((count * CAP, width), jnp.bfloat16),
            jax.ShapeDtypeStruct((2 * CAP, rows), jnp.bfloat16),
        ),
        in_specs=[
            pl.BlockSpec(memory_space=SMEM),
            pl.BlockSpec(memory_space=SMEM),
            pl.BlockSpec(memory_space=VMEM),
            pl.BlockSpec(memory_space=VMEM),
        ],
        out_specs=(pl.BlockSpec(memory_space=VMEM), pl.BlockSpec(memory_space=VMEM)),
        compiler_params=params(16),
        cost_estimate=cost(2 * count * CAP * rows * width, 2 * (count * CAP + rows) * width),
        name="route",
    )(me, adapter_slot, row_adapter[None, :], attended)


def away_kernel(me_ref, attended_ref, weight_ref, out_ref):
    out_ref[0] = jnp.dot(
        attended_ref[...], weight_ref[...], preferred_element_type=jnp.float32
    ).astype(jnp.bfloat16)


def away(me, attended, out_weight, kz, width):
    rows, depth = attended.shape
    return pl.pallas_call(
        away_kernel,
        out_shape=jax.ShapeDtypeStruct((2, rows, width), jnp.bfloat16),
        grid_spec=pltpu.PrefetchScalarGridSpec(
            num_scalar_prefetch=1,
            grid=(2,),
            in_specs=[
                pl.BlockSpec((rows, depth), lambda i, me: (0, 0)),
                pl.BlockSpec((depth, width), lambda i, me: (0, me[0] ^ (kz * 4 + i * 2 + 1))),
            ],
            out_specs=pl.BlockSpec((1, rows, width), lambda i, me: (i, 0, 0)),
        ),
        compiler_params=params(16),
        cost_estimate=cost(4 * rows * depth * width, 4 * depth * width + 4 * rows * width),
        name="away",
    )(me, attended, out_weight)


def adapter_kernel(count, me_ref, arrived_ref, down_ref, up_ref, near_ref, far_ref):
    width = arrived_ref.shape[2]
    total = jnp.zeros((CAP, down_ref.shape[0]), jnp.float32)
    for t in range(count):
        total += lax.dot_general(
            arrived_ref[t],
            down_ref[:, t * width : (t + 1) * width],
            (((1,), (1,)), ((), ())),
            preferred_element_type=jnp.float32,
        )
    shrunk = total.astype(jnp.bfloat16)
    for m in range(count):
        start = pl.multiple_of((me_ref[0] ^ m) * width, width)
        grown = jnp.dot(
            shrunk, up_ref[:, pl.ds(start, width)], preferred_element_type=jnp.float32
        ).astype(jnp.bfloat16)
        if m % 2:
            far_ref[m // 2] = grown
        else:
            near_ref[m // 2] = grown


def adapter(me, arrived, down, up):
    count, cap, width = arrived.shape
    half = jax.ShapeDtypeStruct((count // 2, cap, width), jnp.bfloat16)
    vmem = pl.BlockSpec(memory_space=VMEM)
    return pl.pallas_call(
        functools.partial(adapter_kernel, count),
        out_shape=(half, half),
        in_specs=[pl.BlockSpec(memory_space=SMEM), vmem, vmem, vmem],
        out_specs=(vmem, vmem),
        compiler_params=params(24),
        cost_estimate=cost(4 * cap * down.size, 2 * (down.size + up.size + 2 * arrived.size)),
        name="adapter",
    )(me, arrived, down, up)


def pair_kernel(
    me_ref, attended_ref, stay_w_ref, go_w_ref, other_ref, picks_ref, near_ref, far_ref, stay_ref, go_ref
):
    def block(weight_ref, j):
        total = jnp.dot(attended_ref[...], weight_ref[...], preferred_element_type=jnp.float32)
        own = lax.dot_general(
            picks_ref[:CAP, :], near_ref[j], (((0,), (0,)), ((), ())), preferred_element_type=jnp.float32
        )
        others = lax.dot_general(
            picks_ref[CAP:, :], far_ref[j], (((0,), (0,)), ((), ())), preferred_element_type=jnp.float32
        )
        return total + other_ref[j].astype(jnp.float32) + (own + others)

    go_ref[...] = block(go_w_ref, 1).astype(jnp.bfloat16)
    stay_ref[...] = block(stay_w_ref, 0)


def pair(me, attended, out_weight, other, picks, near, far, kz):
    rows, depth = attended.shape
    width = other.shape[2]
    cap = near.shape[1]
    whole = lambda i, me: (0, 0)
    return pl.pallas_call(
        pair_kernel,
        out_shape=(
            jax.ShapeDtypeStruct((rows, width), jnp.float32),
            jax.ShapeDtypeStruct((rows, width), jnp.bfloat16),
        ),
        grid_spec=pltpu.PrefetchScalarGridSpec(
            num_scalar_prefetch=1,
            grid=(1,),
            in_specs=[
                pl.BlockSpec((rows, depth), whole),
                pl.BlockSpec((depth, width), lambda i, me: (0, me[0] ^ (kz * 4))),
                pl.BlockSpec((depth, width), lambda i, me: (0, me[0] ^ (kz * 4 + 2))),
                pl.BlockSpec((2, rows, width), lambda i, me: (0, 0, 0)),
                pl.BlockSpec((2 * cap, rows), whole),
                pl.BlockSpec((2, cap, width), lambda i, me: (kz, 0, 0)),
                pl.BlockSpec((2, cap, width), lambda i, me: (kz, 0, 0)),
            ],
            out_specs=(pl.BlockSpec((rows, width), whole), pl.BlockSpec((rows, width), whole)),
        ),
        compiler_params=params(24),
        cost_estimate=cost(4 * rows * depth * width, 4 * depth * width + 12 * rows * width),
        name="pair",
    )(me, attended, out_weight, out_weight, other, picks, near, far)


def staged(attended, out_weight, adapter_down, adapter_up, row_adapter, adapter_slot):
    count = lax.axis_size("tensor")
    me = lax.axis_index("tensor").astype(jnp.int32)[None]
    width = out_weight.shape[1] // count
    outgoing, picks = route(me, adapter_slot, row_adapter, attended, count)
    arrived = lax.all_to_all(
        outgoing.reshape(count, CAP, outgoing.shape[1]), "tensor", split_axis=0, concat_axis=0, tiled=True
    )
    order = (3, 2, 1, 0)
    others = {kz: swap(away(me, attended, out_weight, kz, width), 1, count) for kz in order}
    near, far = adapter(me, arrived, jnp.swapaxes(adapter_down, 1, 2)[0], adapter_up[0])
    far = swap(far, 1, count)
    total = None
    for kz in order:
        stay, go = pair(me, attended, out_weight, others[kz], picks, near, far, kz)
        came = swap(go, 2, count)
        both = stay + came.astype(jnp.float32)
        if kz:
            both = swap(both.astype(jnp.bfloat16), 4 * kz, count).astype(jnp.float32)
        total = both if total is None else total + both
    return total.astype(jnp.bfloat16)


def general(attended, out_weight, adapter_down, adapter_up, row_adapter, adapter_slot):
    tensor_size = lax.axis_size("tensor")
    device = lax.axis_index("tensor")
    row_count = attended.shape[0]
    held_count = adapter_down.shape[0]
    storage = adapter_slot[row_adapter]
    partial_value = jnp.dot(attended, out_weight, preferred_element_type=jnp.float32)
    base_out = lax.psum_scatter(partial_value, "tensor", scatter_dimension=1, tiled=True)
    owner_of = storage // held_count
    local_index = storage % held_count
    owner_hot = (owner_of[:, None] == jnp.arange(tensor_size, dtype=jnp.int32)[None, :]).astype(
        jnp.int32
    )
    position = jnp.sum(jnp.cumsum(owner_hot, axis=0) * owner_hot, axis=1) - 1
    target = owner_of * CAP + position
    slot_row = (
        jnp.full((tensor_size * CAP,), row_count, jnp.int32)
        .at[target]
        .set(jnp.arange(row_count, dtype=jnp.int32))
    )
    padded = jnp.concatenate([attended, jnp.zeros((1, attended.shape[1]), attended.dtype)], axis=0)
    outgoing = padded[slot_row]
    arrived = lax.all_to_all(outgoing, "tensor", split_axis=0, concat_axis=1, tiled=True)
    own_slots = lax.dynamic_slice_in_dim(slot_row, device * CAP, CAP)
    slot_local = jnp.concatenate([local_index, jnp.zeros((1,), jnp.int32)])[own_slots]
    selector = (slot_local[None, :] == jnp.arange(held_count, dtype=jnp.int32)[:, None]).astype(
        jnp.float32
    )
    all_shrunk = jnp.einsum(
        "cd,adk->ack", arrived, adapter_down, preferred_element_type=jnp.float32
    )
    shrunk = jnp.sum(all_shrunk * selector[:, :, None], axis=0).astype(jnp.bfloat16)
    picked = (selector[:, :, None] * shrunk[None].astype(jnp.float32)).astype(jnp.bfloat16)
    expanded = jnp.einsum(
        "ack,akd->cd", picked, adapter_up, preferred_element_type=jnp.float32
    ).astype(jnp.bfloat16)
    returned = lax.all_to_all(expanded, "tensor", split_axis=1, concat_axis=0, tiled=True)
    delta_out = returned[target]
    return (base_out + delta_out.astype(jnp.float32)).astype(jnp.bfloat16)


def shards(*arrays):
    if lax.axis_size("tensor") == 16 and arrays[2].shape[0] == 1:
        return staged(*arrays)
    return general(*arrays)


def solution(mesh):
    placed = (
        P("groups", "tensor"),
        P("tensor", None),
        P(("groups", "tensor"), None, None),
        P(("groups", "tensor"), None, None),
        P("groups"),
        P("groups"),
    )
    return jax.shard_map(
        shards, mesh=mesh, in_specs=placed, out_specs=P("groups", "tensor"), check_vma=False
    )
```

```python
import functools

import jax
import jax.numpy as jnp
from jax import lax
from jax.experimental import pallas as pl
from jax.experimental.pallas import tpu as pltpu
from jax.sharding import PartitionSpec as P

CAP = 32
IN_VMEM = pl.BlockSpec(memory_space=pltpu.VMEM)
IN_HBM = pl.BlockSpec(memory_space=pltpu.HBM)
DMA = pltpu.SemaphoreType.DMA


def params(mib):
    return pltpu.CompilerParams(vmem_limit_bytes=mib * 1024 * 1024)


def cost(flops, moved):
    return pl.CostEstimate(flops=flops, bytes_accessed=moved, transcendentals=0)


def shape(dims, dtype=jnp.bfloat16):
    return jax.ShapeDtypeStruct(dims, dtype)


def dot(a, b):
    return jnp.dot(a, b, preferred_element_type=jnp.float32)


def swap(value, mask):
    count = lax.axis_size("tensor")
    return lax.ppermute(value, "tensor", [(t, t ^ mask) for t in range(count)])


def route_kernel(chips, slot_hbm, row_ref, own_ref, other_ref, target_ref, *rest):
    out_refs, slot_ref, slot_sem = rest[:chips], rest[chips], rest[chips + 1]
    rows, width = own_ref.shape
    me = lax.axis_index("tensor")
    core = me % 2
    fetch = pltpu.make_async_copy(slot_hbm, slot_ref, slot_sem)
    fetch.start()
    fetch.wait()
    ids = row_ref[...]
    owner = jnp.zeros_like(ids)
    for a in range(slot_ref.shape[0]):
        owner = jnp.where(ids == a, slot_ref[a], owner)
    hot = (lax.broadcasted_iota(jnp.int32, (2 * chips, rows), 0) == owner).astype(jnp.float32)
    earlier = (
        lax.broadcasted_iota(jnp.int32, (rows, rows), 0)
        < lax.broadcasted_iota(jnp.int32, (rows, rows), 1)
    ).astype(jnp.bfloat16)
    ahead = dot(hot.astype(jnp.bfloat16), earlier)
    place = jnp.sum(ahead * hot, axis=0, keepdims=True).astype(jnp.int32)
    target = owner * CAP + place
    target_ref[...] = target
    j = lax.broadcasted_iota(jnp.int32, (chips * CAP, rows), 0)
    slots = (me ^ ((j // CAP) * 2)) * CAP + j % CAP
    select = (slots == target).astype(jnp.bfloat16)
    own = dot(select, own_ref[...]).astype(jnp.bfloat16)
    other = dot(select, other_ref[...]).astype(jnp.bfloat16)
    for m in range(chips):
        out_refs[m][:, pl.ds(pl.multiple_of(core * width, width), width)] = own[m * CAP : (m + 1) * CAP]
        out_refs[m][:, pl.ds(pl.multiple_of((1 - core) * width, width), width)] = other[
            m * CAP : (m + 1) * CAP
        ]


def route(adapter_slot, row_adapter, own, other):
    rows, width = own.shape
    chips = lax.axis_size("tensor") // 2
    found = pl.pallas_call(
        functools.partial(route_kernel, chips),
        out_shape=[shape((1, rows), jnp.int32)] + [shape((CAP, 2 * width))] * chips,
        in_specs=[IN_HBM, IN_VMEM, IN_VMEM, IN_VMEM],
        out_specs=[IN_VMEM] * (chips + 1),
        scratch_shapes=[pltpu.SMEM(adapter_slot.shape, jnp.int32), DMA(())],
        compiler_params=params(16),
        cost_estimate=cost(4 * chips * CAP * rows * width, 8 * chips * CAP * width),
        name="route",
    )(adapter_slot, row_adapter[None, :], own, other)
    return found[0], found[1:]


def product_kernel(chip_masks, attended_hbm, weight_hbm, away_ref, stay_ref, attended_ref, weight_ref, sems):
    width = stay_ref.shape[2]
    me = lax.axis_index("tensor")
    core, chip = me % 2, me // 2
    fetches = [pltpu.make_async_copy(attended_hbm, attended_ref, sems.at[len(chip_masks)])]
    for i, m in enumerate(chip_masks):
        start = pl.multiple_of((chip ^ m) * 2 * width, 2 * width)
        fetches.append(
            pltpu.make_async_copy(weight_hbm.at[:, pl.ds(start, 2 * width)], weight_ref.at[i], sems.at[i])
        )
    for fetch in fetches:
        fetch.start()
    fetches[0].wait()
    for i in range(len(chip_masks)):
        fetches[i + 1].wait()
        there = pl.ds(pl.multiple_of((1 - core) * width, width), width)
        here = pl.ds(pl.multiple_of(core * width, width), width)
        away_ref[i] = dot(attended_ref[...], weight_ref[i, :, there]).astype(jnp.bfloat16)
        stay_ref[i] = dot(attended_ref[...], weight_ref[i, :, here])


def product(attended, out_weight, chip_masks):
    rows, depth = attended.shape
    width = out_weight.shape[1] // lax.axis_size("tensor")
    n = len(chip_masks)
    return pl.pallas_call(
        functools.partial(product_kernel, chip_masks),
        out_shape=(shape((n, rows, width)), shape((n, rows, width), jnp.float32)),
        in_specs=[IN_HBM, IN_HBM],
        out_specs=(IN_VMEM, IN_VMEM),
        scratch_shapes=[
            pltpu.VMEM((rows, depth), jnp.bfloat16),
            pltpu.VMEM((n, depth, 2 * width), jnp.bfloat16),
            DMA((n + 1,)),
        ],
        compiler_params=params(24),
        cost_estimate=cost(4 * n * rows * depth * width, n * (4 * depth * width + 6 * rows * width)),
        name="product",
    )(attended, out_weight)


def shrink_kernel(down_ref, *refs):
    arrived_refs, out_ref = refs[:-1], refs[-1]
    chip = lax.axis_index("tensor") // 2
    total = jnp.zeros(out_ref.shape, jnp.float32)
    for m, arrived_ref in enumerate(arrived_refs):
        width = arrived_ref.shape[1]
        start = pl.multiple_of((chip ^ m) * width, width)
        total += lax.dot_general(
            arrived_ref[...],
            down_ref[:, pl.ds(start, width)],
            (((1,), (1,)), ((), ())),
            preferred_element_type=jnp.float32,
        )
    out_ref[...] = total.astype(jnp.bfloat16)


def shrink(down, arrived):
    return pl.pallas_call(
        shrink_kernel,
        out_shape=shape((CAP, down.shape[0])),
        in_specs=[IN_VMEM] * (1 + len(arrived)),
        out_specs=IN_VMEM,
        compiler_params=params(16),
        cost_estimate=cost(2 * CAP * down.size, 2 * down.size),
        name="shrink",
    )(down, *arrived)


def grow_kernel(shrunk_ref, shrunk_other_ref, up_ref, up_other_ref, *out_refs):
    me = lax.axis_index("tensor")
    for m, out_ref in enumerate(out_refs):
        width = out_ref.shape[1]
        block = pl.ds(pl.multiple_of((me ^ (2 * m)) * width, width), width)
        out_ref[:CAP, :] = dot(shrunk_ref[...], up_ref[:, block]).astype(jnp.bfloat16)
        out_ref[CAP:, :] = dot(shrunk_other_ref[...], up_other_ref[:, block]).astype(jnp.bfloat16)


def grow(shrunk, shrunk_other, up, up_other):
    count = lax.axis_size("tensor")
    width = up.shape[1] // count
    return pl.pallas_call(
        grow_kernel,
        out_shape=[shape((2 * CAP, width))] * (count // 2),
        in_specs=[IN_VMEM] * 4,
        out_specs=[IN_VMEM] * (count // 2),
        compiler_params=params(16),
        cost_estimate=cost(2 * CAP * up.size, 4 * up.size),
        name="grow",
    )(shrunk, shrunk_other, up, up_other)


def finish_kernel(target_ref, base_ref, *refs):
    grown_refs, out_ref = refs[:-1], refs[-1]
    rows = base_ref.shape[0]
    me = lax.axis_index("tensor")
    j = lax.broadcasted_iota(jnp.int32, (2 * CAP, rows), 0)
    delta = jnp.zeros(out_ref.shape, jnp.float32)
    for m, grown_ref in enumerate(grown_refs):
        slots = (me ^ (2 * m) ^ (j // CAP)) * CAP + j % CAP
        pick = (slots == target_ref[...]).astype(jnp.bfloat16)
        delta += lax.dot_general(
            pick, grown_ref[...], (((0,), (0,)), ((), ())), preferred_element_type=jnp.float32
        )
    out_ref[...] = (base_ref[...] + delta).astype(jnp.bfloat16)


def finish(target, base, grown):
    return pl.pallas_call(
        finish_kernel,
        out_shape=shape(base.shape),
        in_specs=[IN_VMEM] * (2 + len(grown)),
        out_specs=IN_VMEM,
        compiler_params=params(16),
        cost_estimate=cost(4 * CAP * len(grown) * base.size, 8 * base.size),
        name="finish",
    )(target, base, *grown)


def staged(attended, out_weight, adapter_down, adapter_up, row_adapter, adapter_slot):
    f32 = jnp.float32
    up, down = adapter_up[0], jnp.swapaxes(adapter_down, 1, 2)[0]
    attended_other = swap(attended, 1)
    away7, stay7 = product(attended, out_weight, (7,))
    came7 = swap(away7, 1)
    target, outgoing = route(adapter_slot, row_adapter, attended, attended_other)
    arrived = {m: swap(outgoing[m], 2 * m) for m in (7, 6, 5, 4, 3, 2, 1)}
    arrived[0] = outgoing[0]
    up_other = swap(up, 1)
    go3 = (stay7[0] + came7[0].astype(f32)).astype(jnp.bfloat16)
    y3 = swap(go3, 2)
    away_far, stay_far = product(attended, out_weight, (5, 3, 1))
    came_far = swap(away_far, 1)
    away_near, stay_near = product(attended, out_weight, (6, 4, 2, 0))
    came_near = swap(away_near, 1)
    ys = [y3]
    for i in range(3):
        go = (stay_far[i] + came_far[i].astype(f32)).astype(jnp.bfloat16)
        ys.append(swap(go, 2))
    sides = [stay_near[i] + came_near[i].astype(f32) + ys[i].astype(f32) for i in range(4)]
    from3 = swap(sides[0].astype(jnp.bfloat16), 4)
    from2 = swap((sides[1] + from3.astype(f32)).astype(jnp.bfloat16), 8)
    from1 = swap(sides[2].astype(jnp.bfloat16), 4)
    shrunk = shrink(down, [arrived[m] for m in range(8)])
    shrunk_other = swap(shrunk, 1)
    grown = grow(shrunk, shrunk_other, up, up_other)
    back = [grown[0]] + [None] * 7
    for m in (7, 6, 5, 4, 3, 2, 1):
        back[m] = swap(grown[m], 2 * m)
    base = sides[3] + from1.astype(f32) + from2.astype(f32)
    return finish(target, base, back)


def general(attended, out_weight, adapter_down, adapter_up, row_adapter, adapter_slot):
    tensor_size = lax.axis_size("tensor")
    device = lax.axis_index("tensor")
    row_count = attended.shape[0]
    held_count = adapter_down.shape[0]
    storage = adapter_slot[row_adapter]
    partial_value = jnp.dot(attended, out_weight, preferred_element_type=jnp.float32)
    base_out = lax.psum_scatter(partial_value, "tensor", scatter_dimension=1, tiled=True)
    owner_of = storage // held_count
    local_index = storage % held_count
    owner_hot = (owner_of[:, None] == jnp.arange(tensor_size, dtype=jnp.int32)[None, :]).astype(
        jnp.int32
    )
    position = jnp.sum(jnp.cumsum(owner_hot, axis=0) * owner_hot, axis=1) - 1
    target = owner_of * CAP + position
    slot_row = (
        jnp.full((tensor_size * CAP,), row_count, jnp.int32)
        .at[target]
        .set(jnp.arange(row_count, dtype=jnp.int32))
    )
    padded = jnp.concatenate([attended, jnp.zeros((1, attended.shape[1]), attended.dtype)], axis=0)
    outgoing = padded[slot_row]
    arrived = lax.all_to_all(outgoing, "tensor", split_axis=0, concat_axis=1, tiled=True)
    own_slots = lax.dynamic_slice_in_dim(slot_row, device * CAP, CAP)
    slot_local = jnp.concatenate([local_index, jnp.zeros((1,), jnp.int32)])[own_slots]
    selector = (slot_local[None, :] == jnp.arange(held_count, dtype=jnp.int32)[:, None]).astype(
        jnp.float32
    )
    all_shrunk = jnp.einsum(
        "cd,adk->ack", arrived, adapter_down, preferred_element_type=jnp.float32
    )
    shrunk = jnp.sum(all_shrunk * selector[:, :, None], axis=0).astype(jnp.bfloat16)
    picked = (selector[:, :, None] * shrunk[None].astype(jnp.float32)).astype(jnp.bfloat16)
    expanded = jnp.einsum(
        "ack,akd->cd", picked, adapter_up, preferred_element_type=jnp.float32
    ).astype(jnp.bfloat16)
    returned = lax.all_to_all(expanded, "tensor", split_axis=1, concat_axis=0, tiled=True)
    delta_out = returned[target]
    return (base_out + delta_out.astype(jnp.float32)).astype(jnp.bfloat16)


def shards(*arrays):
    if lax.axis_size("tensor") == 16 and arrays[2].shape[0] == 1:
        return staged(*arrays)
    return general(*arrays)


def solution(mesh):
    placed = (
        P("groups", "tensor"),
        P("tensor", None),
        P(("groups", "tensor"), None, None),
        P(("groups", "tensor"), None, None),
        P("groups"),
        P("groups"),
    )
    return jax.shard_map(
        shards, mesh=mesh, in_specs=placed, out_specs=P("groups", "tensor"), check_vma=False
    )
```

```python
import functools

import jax
import jax.numpy as jnp
from jax import lax
from jax.experimental import pallas as pl
from jax.experimental.pallas import tpu as pltpu
from jax.sharding import PartitionSpec as P

CAP = 32
IN_VMEM = pl.BlockSpec(memory_space=pltpu.VMEM)
IN_HBM = pl.BlockSpec(memory_space=pltpu.HBM)
DMA = pltpu.SemaphoreType.DMA


def params(mib):
    return pltpu.CompilerParams(vmem_limit_bytes=mib * 1024 * 1024)


def cost(flops, moved):
    return pl.CostEstimate(flops=flops, bytes_accessed=moved, transcendentals=0)


def shape(dims, dtype=jnp.bfloat16):
    return jax.ShapeDtypeStruct(dims, dtype)


def dot(a, b):
    return jnp.dot(a, b, preferred_element_type=jnp.float32)


def swap(value, mask):
    count = lax.axis_size("tensor")
    return lax.ppermute(value, "tensor", [(t, t ^ mask) for t in range(count)])


def route_kernel(chips, slot_hbm, row_ref, own_ref, other_ref, target_ref, *rest):
    out_refs, slot_ref, slot_sem = rest[:chips], rest[chips], rest[chips + 1]
    rows, width = own_ref.shape
    me = lax.axis_index("tensor")
    core = me % 2
    fetch = pltpu.make_async_copy(slot_hbm, slot_ref, slot_sem)
    fetch.start()
    fetch.wait()
    ids = row_ref[...]
    owner = jnp.zeros_like(ids)
    for a in range(slot_ref.shape[0]):
        owner = jnp.where(ids == a, slot_ref[a], owner)
    hot = (lax.broadcasted_iota(jnp.int32, (2 * chips, rows), 0) == owner).astype(jnp.float32)
    earlier = (
        lax.broadcasted_iota(jnp.int32, (rows, rows), 0)
        < lax.broadcasted_iota(jnp.int32, (rows, rows), 1)
    ).astype(jnp.bfloat16)
    ahead = dot(hot.astype(jnp.bfloat16), earlier)
    place = jnp.sum(ahead * hot, axis=0, keepdims=True).astype(jnp.int32)
    target = owner * CAP + place
    target_ref[...] = target
    j = lax.broadcasted_iota(jnp.int32, (chips * CAP, rows), 0)
    slots = (me ^ ((j // CAP) * 2)) * CAP + j % CAP
    select = (slots == target).astype(jnp.bfloat16)
    own = dot(select, own_ref[...]).astype(jnp.bfloat16)
    other = dot(select, other_ref[...]).astype(jnp.bfloat16)
    for m in range(chips):
        out_refs[m][:, pl.ds(pl.multiple_of(core * width, width), width)] = own[m * CAP : (m + 1) * CAP]
        out_refs[m][:, pl.ds(pl.multiple_of((1 - core) * width, width), width)] = other[
            m * CAP : (m + 1) * CAP
        ]


def route(adapter_slot, row_adapter, own, other):
    rows, width = own.shape
    chips = lax.axis_size("tensor") // 2
    found = pl.pallas_call(
        functools.partial(route_kernel, chips),
        out_shape=[shape((1, rows), jnp.int32)] + [shape((CAP, 2 * width))] * chips,
        in_specs=[IN_HBM, IN_VMEM, IN_VMEM, IN_VMEM],
        out_specs=[IN_VMEM] * (chips + 1),
        scratch_shapes=[pltpu.SMEM(adapter_slot.shape, jnp.int32), DMA(())],
        compiler_params=params(16),
        cost_estimate=cost(4 * chips * CAP * rows * width, 8 * chips * CAP * width),
        name="route",
    )(adapter_slot, row_adapter[None, :], own, other)
    return found[0], found[1:]


def product_kernel(attended_ref, weight_ref, away_ref, stay_ref):
    chips, rows, width = stay_ref.shape
    me = lax.axis_index("tensor")
    for m in reversed(range(chips)):
        there = pl.ds(pl.multiple_of((me ^ (2 * m + 1)) * width, width), width)
        here = pl.ds(pl.multiple_of((me ^ (2 * m)) * width, width), width)
        away_ref[m] = dot(attended_ref[...], weight_ref[:, there]).astype(jnp.bfloat16)
        stay_ref[m] = dot(attended_ref[...], weight_ref[:, here])


def product(attended, out_weight):
    rows, depth = attended.shape
    chips = lax.axis_size("tensor") // 2
    width = out_weight.shape[1] // (2 * chips)
    return pl.pallas_call(
        product_kernel,
        out_shape=(shape((chips, rows, width)), shape((chips, rows, width), jnp.float32)),
        in_specs=[IN_VMEM, IN_VMEM],
        out_specs=(IN_VMEM, IN_VMEM),
        compiler_params=params(24),
        cost_estimate=cost(2 * rows * out_weight.size, 2 * out_weight.size + 6 * chips * rows * width),
        name="product",
    )(attended, out_weight)


def adapter_kernel(chip_masks, down_ref, up_ref, *refs):
    arrived_refs, near_ref, far_ref = refs[:-2], refs[-2], refs[-1]
    me = lax.axis_index("tensor")
    total = jnp.zeros((CAP, down_ref.shape[0]), jnp.float32)
    for m, arrived_ref in zip(chip_masks, arrived_refs):
        width = arrived_ref.shape[1]
        start = pl.multiple_of(((me // 2) ^ m) * width, width)
        total += lax.dot_general(
            arrived_ref[...],
            down_ref[:, pl.ds(start, width)],
            (((1,), (1,)), ((), ())),
            preferred_element_type=jnp.float32,
        )
    shrunk = total.astype(jnp.bfloat16)
    width = near_ref.shape[2]
    for m in range(len(arrived_refs)):
        near = pl.multiple_of((me ^ (2 * m)) * width, width)
        far = pl.multiple_of((me ^ (2 * m + 1)) * width, width)
        near_ref[m] = dot(shrunk, up_ref[:, pl.ds(near, width)]).astype(jnp.bfloat16)
        far_ref[m] = dot(shrunk, up_ref[:, pl.ds(far, width)]).astype(jnp.bfloat16)


def adapter(down, up, arrived):
    chips = len(arrived)
    half = shape((chips, CAP, up.shape[1] // (2 * chips)))
    return pl.pallas_call(
        functools.partial(adapter_kernel, tuple(arrived)),
        out_shape=(half, half),
        in_specs=[IN_VMEM] * (2 + chips),
        out_specs=(IN_VMEM, IN_VMEM),
        compiler_params=params(16),
        cost_estimate=cost(40 * 10**9, 128 * down.size),
        name="adapter",
    )(down, up, *arrived.values())


def join_kernel(chip_masks, target_ref, stay_ref, came_ref, near_ref, far_ref, *out_refs):
    rows = target_ref.shape[1]
    me = lax.axis_index("tensor")
    j = lax.broadcasted_iota(jnp.int32, (CAP, rows), 0)
    over = (((0,), (0,)), ((), ()))
    near_pick = (me * CAP + j == target_ref[...]).astype(jnp.bfloat16)
    far_pick = ((me ^ 1) * CAP + j == target_ref[...]).astype(jnp.bfloat16)
    for m, out_ref in zip(chip_masks, out_refs):
        total = stay_ref[m] + came_ref[m].astype(jnp.float32)
        total += lax.dot_general(near_pick, near_ref[m], over, preferred_element_type=jnp.float32)
        total += lax.dot_general(far_pick, far_ref[m], over, preferred_element_type=jnp.float32)
        out_ref[...] = total.astype(out_ref.dtype)


def join(target, stay, came, near, far, chip_masks, dtype):
    n, (rows, width) = len(chip_masks), stay.shape[1:]
    return pl.pallas_call(
        functools.partial(join_kernel, chip_masks),
        out_shape=[shape((rows, width), dtype)] * n,
        in_specs=[IN_VMEM] * 5,
        out_specs=[IN_VMEM] * n,
        compiler_params=params(24),
        cost_estimate=cost(4 * n * CAP * rows * width, 10 * n * rows * width),
        name="join",
    )(target, stay, came, near, far)


def staged(attended, out_weight, adapter_down, adapter_up, row_adapter, adapter_slot):
    f32, bf16 = jnp.float32, jnp.bfloat16
    up, down = adapter_up[0], jnp.swapaxes(adapter_down, 1, 2)[0]
    target, outgoing = route(adapter_slot, row_adapter, attended, swap(attended, 1))
    arrived = {m: swap(outgoing[m], 2 * m) for m in (1, 2, 4, 5, 6, 7, 3)}
    arrived[0] = outgoing[0]
    away, stay = product(attended, out_weight)
    came = swap(away, 1)
    near, far = adapter(down, up, arrived)
    far = swap(far, 1)
    (go3,) = join(target, stay, came, near, far, (7,), bf16)
    go2, go1, go0 = join(target, stay, came, near, far, (5, 3, 1), bf16)
    y3, y2, y1, y0 = swap(go3, 2), swap(go2, 2), swap(go1, 2), swap(go0, 2)
    side3, side2, side1, side0 = join(target, stay, came, near, far, (6, 4, 2, 0), f32)
    z3 = swap((side3 + y3.astype(f32)).astype(bf16), 4)
    z2 = swap((side2 + y2.astype(f32) + z3.astype(f32)).astype(bf16), 8)
    z1 = swap((side1 + y1.astype(f32)).astype(bf16), 4)
    total = side0 + y0.astype(f32) + z1.astype(f32) + z2.astype(f32)
    return total.astype(bf16)


def general(attended, out_weight, adapter_down, adapter_up, row_adapter, adapter_slot):
    tensor_size = lax.axis_size("tensor")
    device = lax.axis_index("tensor")
    row_count = attended.shape[0]
    held_count = adapter_down.shape[0]
    storage = adapter_slot[row_adapter]
    partial_value = jnp.dot(attended, out_weight, preferred_element_type=jnp.float32)
    base_out = lax.psum_scatter(partial_value, "tensor", scatter_dimension=1, tiled=True)
    owner_of = storage // held_count
    local_index = storage % held_count
    owner_hot = (owner_of[:, None] == jnp.arange(tensor_size, dtype=jnp.int32)[None, :]).astype(
        jnp.int32
    )
    position = jnp.sum(jnp.cumsum(owner_hot, axis=0) * owner_hot, axis=1) - 1
    target = owner_of * CAP + position
    slot_row = (
        jnp.full((tensor_size * CAP,), row_count, jnp.int32)
        .at[target]
        .set(jnp.arange(row_count, dtype=jnp.int32))
    )
    padded = jnp.concatenate([attended, jnp.zeros((1, attended.shape[1]), attended.dtype)], axis=0)
    outgoing = padded[slot_row]
    arrived = lax.all_to_all(outgoing, "tensor", split_axis=0, concat_axis=1, tiled=True)
    own_slots = lax.dynamic_slice_in_dim(slot_row, device * CAP, CAP)
    slot_local = jnp.concatenate([local_index, jnp.zeros((1,), jnp.int32)])[own_slots]
    selector = (slot_local[None, :] == jnp.arange(held_count, dtype=jnp.int32)[:, None]).astype(
        jnp.float32
    )
    all_shrunk = jnp.einsum(
        "cd,adk->ack", arrived, adapter_down, preferred_element_type=jnp.float32
    )
    shrunk = jnp.sum(all_shrunk * selector[:, :, None], axis=0).astype(jnp.bfloat16)
    picked = (selector[:, :, None] * shrunk[None].astype(jnp.float32)).astype(jnp.bfloat16)
    expanded = jnp.einsum(
        "ack,akd->cd", picked, adapter_up, preferred_element_type=jnp.float32
    ).astype(jnp.bfloat16)
    returned = lax.all_to_all(expanded, "tensor", split_axis=1, concat_axis=0, tiled=True)
    delta_out = returned[target]
    return (base_out + delta_out.astype(jnp.float32)).astype(jnp.bfloat16)


def shards(*arrays):
    if lax.axis_size("tensor") == 16 and arrays[2].shape[0] == 1:
        return staged(*arrays)
    return general(*arrays)


def solution(mesh):
    placed = (
        P("groups", "tensor"),
        P("tensor", None),
        P(("groups", "tensor"), None, None),
        P(("groups", "tensor"), None, None),
        P("groups"),
        P("groups"),
    )
    return jax.shard_map(
        shards, mesh=mesh, in_specs=placed, out_specs=P("groups", "tensor"), check_vma=False
    )
```

```python
import functools

import jax
import jax.numpy as jnp
from jax import lax
from jax.experimental import pallas as pl
from jax.experimental.pallas import tpu as pltpu
from jax.sharding import PartitionSpec as P

CAP = 32
IN_VMEM = pl.BlockSpec(memory_space=pltpu.VMEM)
IN_HBM = pl.BlockSpec(memory_space=pltpu.HBM)
DMA = pltpu.SemaphoreType.DMA


def params(mib):
    return pltpu.CompilerParams(vmem_limit_bytes=mib * 1024 * 1024)


def cost(flops, moved):
    return pl.CostEstimate(flops=flops, bytes_accessed=moved, transcendentals=0)


def shape(dims, dtype=jnp.bfloat16):
    return jax.ShapeDtypeStruct(dims, dtype)


def dot(a, b):
    return jnp.dot(a, b, preferred_element_type=jnp.float32)


def swap(value, mask):
    count = lax.axis_size("tensor")
    return lax.ppermute(value, "tensor", [(t, t ^ mask) for t in range(count)])


def route_kernel(chips, slot_hbm, row_ref, own_ref, other_ref, after_ref, target_ref, *rest):
    out_refs, slot_ref, slot_sem = rest[:chips], rest[chips], rest[chips + 1]
    rows, width = own_ref.shape
    me = lax.axis_index("tensor")
    core = me % 2
    fetch = pltpu.make_async_copy(slot_hbm, slot_ref, slot_sem)
    fetch.start()
    fetch.wait()
    ids = row_ref[...]
    owner = jnp.zeros_like(ids)
    for a in range(slot_ref.shape[0]):
        owner = jnp.where(ids == a, slot_ref[a], owner)
    hot = (lax.broadcasted_iota(jnp.int32, (2 * chips, rows), 0) == owner).astype(jnp.float32)
    earlier = (
        lax.broadcasted_iota(jnp.int32, (rows, rows), 0)
        < lax.broadcasted_iota(jnp.int32, (rows, rows), 1)
    ).astype(jnp.bfloat16)
    ahead = dot(hot.astype(jnp.bfloat16), earlier)
    place = jnp.sum(ahead * hot, axis=0, keepdims=True).astype(jnp.int32)
    target = owner * CAP + place
    target_ref[...] = target
    j = lax.broadcasted_iota(jnp.int32, (chips * CAP, rows), 0)
    slots = (me ^ ((j // CAP) * 2)) * CAP + j % CAP
    select = (slots == target).astype(jnp.bfloat16)
    own = dot(select, own_ref[...]).astype(jnp.bfloat16)
    other = dot(select, other_ref[...]).astype(jnp.bfloat16)
    for m in range(chips):
        out_refs[m][:, pl.ds(pl.multiple_of(core * width, width), width)] = own[m * CAP : (m + 1) * CAP]
        out_refs[m][:, pl.ds(pl.multiple_of((1 - core) * width, width), width)] = other[
            m * CAP : (m + 1) * CAP
        ]


def route(adapter_slot, row_adapter, own, other, after):
    rows, width = own.shape
    chips = lax.axis_size("tensor") // 2
    found = pl.pallas_call(
        functools.partial(route_kernel, chips),
        out_shape=[shape((1, rows), jnp.int32)] + [shape((CAP, 2 * width))] * chips,
        in_specs=[IN_HBM, IN_VMEM, IN_VMEM, IN_VMEM, IN_VMEM],
        out_specs=[IN_VMEM] * (chips + 1),
        scratch_shapes=[pltpu.SMEM(adapter_slot.shape, jnp.int32), DMA(())],
        compiler_params=params(16),
        cost_estimate=cost(4 * chips * CAP * rows * width, 8 * chips * CAP * width),
        name="route",
    )(adapter_slot, row_adapter[None, :], own, other, after)
    return found[0], found[1:]


def product_kernel(attended_hbm, weight_hbm, away_ref, stay_ref, token_ref, attended_ref, weight_ref, sems):
    chips, rows, width = stay_ref.shape
    me = lax.axis_index("tensor")
    core, chip = me % 2, me // 2
    order = tuple(reversed(range(chips)))
    fetches = [pltpu.make_async_copy(attended_hbm, attended_ref, sems.at[chips])]
    for m in order:
        start = pl.multiple_of((chip ^ m) * 2 * width, 2 * width)
        fetches.append(
            pltpu.make_async_copy(weight_hbm.at[:, pl.ds(start, 2 * width)], weight_ref.at[m], sems.at[m])
        )
    for fetch in fetches:
        fetch.start()
    token_ref[...] = jnp.zeros(token_ref.shape, token_ref.dtype)
    fetches[0].wait()
    there = pl.ds(pl.multiple_of((1 - core) * width, width), width)
    here = pl.ds(pl.multiple_of(core * width, width), width)
    for i, m in enumerate(order):
        fetches[i + 1].wait()
        away_ref[m] = dot(attended_ref[...], weight_ref[m, :, there]).astype(jnp.bfloat16)
        stay_ref[m] = dot(attended_ref[...], weight_ref[m, :, here])


def product(attended, out_weight):
    rows, depth = attended.shape
    chips = lax.axis_size("tensor") // 2
    width = out_weight.shape[1] // (2 * chips)
    return pl.pallas_call(
        product_kernel,
        out_shape=(
            shape((chips, rows, width)),
            shape((chips, rows, width), jnp.float32),
            shape((8, 128), jnp.float32),
        ),
        in_specs=[IN_HBM, IN_HBM],
        out_specs=(IN_VMEM, IN_VMEM, IN_VMEM),
        scratch_shapes=[
            pltpu.VMEM((rows, depth), jnp.bfloat16),
            pltpu.VMEM((chips, depth, 2 * width), jnp.bfloat16),
            DMA((chips + 1,)),
        ],
        compiler_params=params(48),
        cost_estimate=cost(2 * rows * out_weight.size, 2 * out_weight.size + 6 * chips * rows * width),
        name="product",
    )(attended, out_weight)


def adapter_kernel(chip_masks, down_ref, up_ref, *refs):
    arrived_refs, near_ref, far_ref = refs[:-2], refs[-2], refs[-1]
    me = lax.axis_index("tensor")
    total = jnp.zeros((CAP, down_ref.shape[0]), jnp.float32)
    for m, arrived_ref in zip(chip_masks, arrived_refs):
        width = arrived_ref.shape[1]
        start = pl.multiple_of(((me // 2) ^ m) * width, width)
        total += lax.dot_general(
            arrived_ref[...],
            down_ref[:, pl.ds(start, width)],
            (((1,), (1,)), ((), ())),
            preferred_element_type=jnp.float32,
        )
    shrunk = total.astype(jnp.bfloat16)
    width = near_ref.shape[2]
    for m in range(len(arrived_refs)):
        near = pl.multiple_of((me ^ (2 * m)) * width, width)
        far = pl.multiple_of((me ^ (2 * m + 1)) * width, width)
        near_ref[m] = dot(shrunk, up_ref[:, pl.ds(near, width)]).astype(jnp.bfloat16)
        far_ref[m] = dot(shrunk, up_ref[:, pl.ds(far, width)]).astype(jnp.bfloat16)


def adapter(down, up, arrived):
    chips = len(arrived)
    half = shape((chips, CAP, up.shape[1] // (2 * chips)))
    return pl.pallas_call(
        functools.partial(adapter_kernel, tuple(arrived)),
        out_shape=(half, half),
        in_specs=[IN_VMEM] * (2 + chips),
        out_specs=(IN_VMEM, IN_VMEM),
        compiler_params=params(16),
        cost_estimate=cost(40 * 10**9, 128 * down.size),
        name="adapter",
    )(down, up, *arrived.values())


def join_kernel(chip_masks, target_ref, stay_ref, came_ref, near_ref, far_ref, *out_refs):
    rows = target_ref.shape[1]
    me = lax.axis_index("tensor")
    j = lax.broadcasted_iota(jnp.int32, (CAP, rows), 0)
    over = (((0,), (0,)), ((), ()))
    near_pick = (me * CAP + j == target_ref[...]).astype(jnp.bfloat16)
    far_pick = ((me ^ 1) * CAP + j == target_ref[...]).astype(jnp.bfloat16)
    for m, out_ref in zip(chip_masks, out_refs):
        total = stay_ref[m] + came_ref[m].astype(jnp.float32)
        total += lax.dot_general(near_pick, near_ref[m], over, preferred_element_type=jnp.float32)
        total += lax.dot_general(far_pick, far_ref[m], over, preferred_element_type=jnp.float32)
        out_ref[...] = total.astype(out_ref.dtype)


def join(target, stay, came, near, far, chip_masks, dtype):
    n, (rows, width) = len(chip_masks), stay.shape[1:]
    return pl.pallas_call(
        functools.partial(join_kernel, chip_masks),
        out_shape=[shape((rows, width), dtype)] * n,
        in_specs=[IN_VMEM] * 5,
        out_specs=[IN_VMEM] * n,
        compiler_params=params(24),
        cost_estimate=cost(4 * n * CAP * rows * width, 10 * n * rows * width),
        name="join",
    )(target, stay, came, near, far)


def later_kernel(side_ref, came_ref, after_ref, out_ref):
    out_ref[...] = (side_ref[...] + came_ref[...].astype(jnp.float32)).astype(jnp.bfloat16)


def later(side, came, after):
    return pl.pallas_call(
        later_kernel,
        out_shape=shape(side.shape),
        in_specs=[IN_VMEM] * 3,
        out_specs=IN_VMEM,
        compiler_params=params(16),
        cost_estimate=cost(2 * side.size, 8 * side.size),
        name="later",
    )(side, came, after)


def staged(attended, out_weight, adapter_down, adapter_up, row_adapter, adapter_slot):
    f32, bf16 = jnp.float32, jnp.bfloat16
    up, down = adapter_up[0], jnp.swapaxes(adapter_down, 1, 2)[0]
    attended_other = swap(attended, 1)
    away, stay, token = product(attended, out_weight)
    came = swap(away, 1)
    target, outgoing = route(adapter_slot, row_adapter, attended, attended_other, token)
    arrived = {m: swap(outgoing[m], 2 * m) for m in (1, 2, 4, 5, 6, 7, 3)}
    arrived[0] = outgoing[0]
    near, far = adapter(down, up, arrived)
    far = swap(far, 1)
    (go3,) = join(target, stay, came, near, far, (7,), bf16)
    go2, go1, go0 = join(target, stay, came, near, far, (5, 3, 1), bf16)
    y3, y2, y1, y0 = swap(go3, 2), swap(go2, 2), swap(go1, 2), swap(go0, 2)
    side3, side2, side1, side0 = join(target, stay, came, near, far, (6, 4, 2, 0), f32)
    z3 = swap((side3 + y3.astype(f32)).astype(bf16), 4)
    sum2 = (side2 + y2.astype(f32) + z3.astype(f32)).astype(bf16)
    z2 = swap(sum2, 8)
    z1 = swap(later(side1, y1, sum2), 4)
    total = side0 + y0.astype(f32) + z1.astype(f32) + z2.astype(f32)
    return total.astype(bf16)


def general(attended, out_weight, adapter_down, adapter_up, row_adapter, adapter_slot):
    tensor_size = lax.axis_size("tensor")
    device = lax.axis_index("tensor")
    row_count = attended.shape[0]
    held_count = adapter_down.shape[0]
    storage = adapter_slot[row_adapter]
    partial_value = jnp.dot(attended, out_weight, preferred_element_type=jnp.float32)
    base_out = lax.psum_scatter(partial_value, "tensor", scatter_dimension=1, tiled=True)
    owner_of = storage // held_count
    local_index = storage % held_count
    owner_hot = (owner_of[:, None] == jnp.arange(tensor_size, dtype=jnp.int32)[None, :]).astype(
        jnp.int32
    )
    position = jnp.sum(jnp.cumsum(owner_hot, axis=0) * owner_hot, axis=1) - 1
    target = owner_of * CAP + position
    slot_row = (
        jnp.full((tensor_size * CAP,), row_count, jnp.int32)
        .at[target]
        .set(jnp.arange(row_count, dtype=jnp.int32))
    )
    padded = jnp.concatenate([attended, jnp.zeros((1, attended.shape[1]), attended.dtype)], axis=0)
    outgoing = padded[slot_row]
    arrived = lax.all_to_all(outgoing, "tensor", split_axis=0, concat_axis=1, tiled=True)
    own_slots = lax.dynamic_slice_in_dim(slot_row, device * CAP, CAP)
    slot_local = jnp.concatenate([local_index, jnp.zeros((1,), jnp.int32)])[own_slots]
    selector = (slot_local[None, :] == jnp.arange(held_count, dtype=jnp.int32)[:, None]).astype(
        jnp.float32
    )
    all_shrunk = jnp.einsum(
        "cd,adk->ack", arrived, adapter_down, preferred_element_type=jnp.float32
    )
    shrunk = jnp.sum(all_shrunk * selector[:, :, None], axis=0).astype(jnp.bfloat16)
    picked = (selector[:, :, None] * shrunk[None].astype(jnp.float32)).astype(jnp.bfloat16)
    expanded = jnp.einsum(
        "ack,akd->cd", picked, adapter_up, preferred_element_type=jnp.float32
    ).astype(jnp.bfloat16)
    returned = lax.all_to_all(expanded, "tensor", split_axis=1, concat_axis=0, tiled=True)
    delta_out = returned[target]
    return (base_out + delta_out.astype(jnp.float32)).astype(jnp.bfloat16)


def shards(*arrays):
    if lax.axis_size("tensor") == 16 and arrays[2].shape[0] == 1:
        return staged(*arrays)
    return general(*arrays)


def solution(mesh):
    placed = (
        P("groups", "tensor"),
        P("tensor", None),
        P(("groups", "tensor"), None, None),
        P(("groups", "tensor"), None, None),
        P("groups"),
        P("groups"),
    )
    return jax.shard_map(
        shards, mesh=mesh, in_specs=placed, out_specs=P("groups", "tensor"), check_vma=False
    )
```

```python
import functools

import jax
import jax.numpy as jnp
from jax import lax
from jax.experimental import pallas as pl
from jax.experimental.pallas import tpu as pltpu
from jax.sharding import PartitionSpec as P

CAP = 32
IN_VMEM = pl.BlockSpec(memory_space=pltpu.VMEM)
IN_HBM = pl.BlockSpec(memory_space=pltpu.HBM)
ANYWHERE = pl.BlockSpec(memory_space=pl.ANY)
DMA = pltpu.SemaphoreType.DMA


def params(mib):
    return pltpu.CompilerParams(vmem_limit_bytes=mib * 1024 * 1024)


def cost(flops, moved):
    return pl.CostEstimate(flops=flops, bytes_accessed=moved, transcendentals=0)


def shape(dims, dtype=jnp.bfloat16):
    return jax.ShapeDtypeStruct(dims, dtype)


def dot(a, b):
    return jnp.dot(a, b, preferred_element_type=jnp.float32)


def swap(value, mask):
    count = lax.axis_size("tensor")
    return lax.ppermute(value, "tensor", [(t, t ^ mask) for t in range(count)])


def route_kernel(count, layers, slot_hbm, row_ref, own_ref, y_ref, *rest):
    target_ref, out_refs = rest[-4 - layers], rest[-3 - layers : -3]
    slot_ref, slot_sem = rest[-2:]
    rows, width = own_ref.shape
    me = lax.axis_index("tensor")
    fetch = pltpu.make_async_copy(slot_hbm, slot_ref, slot_sem)
    fetch.start()
    fetch.wait()
    ids = row_ref[...]
    owner = jnp.zeros_like(ids)
    for a in range(slot_ref.shape[0]):
        owner = jnp.where(ids == a, slot_ref[a], owner)
    hot = (lax.broadcasted_iota(jnp.int32, (count, rows), 0) == owner).astype(jnp.float32)
    earlier = (
        lax.broadcasted_iota(jnp.int32, (rows, rows), 0)
        < lax.broadcasted_iota(jnp.int32, (rows, rows), 1)
    ).astype(jnp.bfloat16)
    ahead = dot(hot.astype(jnp.bfloat16), earlier)
    place = jnp.sum(ahead * hot, axis=0, keepdims=True).astype(jnp.int32)
    target = owner * CAP + place
    target_ref[...] = target
    j = lax.broadcasted_iota(jnp.int32, (2 * CAP, rows), 0)
    for k in range(layers):
        slots = (me ^ (4 * k) ^ (j // CAP)) * CAP + j % CAP
        select = (slots == target).astype(jnp.bfloat16)
        out_refs[k][:, :width] = dot(select, own_ref[...]).astype(jnp.bfloat16)
        out_refs[k][:, width:] = dot(select, y_ref[...]).astype(jnp.bfloat16)


def route(adapter_slot, row_adapter, own, y, passed, *after):
    rows, width = own.shape
    count = lax.axis_size("tensor")
    layers = count // 4
    found = pl.pallas_call(
        functools.partial(route_kernel, count, layers),
        out_shape=[shape((1, rows), jnp.int32)]
        + [shape((2 * CAP, 2 * width))] * layers
        + [shape(passed.shape, passed.dtype)],
        in_specs=[IN_HBM] + [IN_VMEM] * 3 + [ANYWHERE] * (1 + len(after)),
        out_specs=[IN_VMEM] * (layers + 1) + [ANYWHERE],
        input_output_aliases={4: layers + 1},
        scratch_shapes=[pltpu.SMEM(adapter_slot.shape, jnp.int32), DMA(())],
        compiler_params=params(16),
        cost_estimate=cost(8 * layers * CAP * rows * width, 16 * layers * CAP * width),
        name="route",
    )(adapter_slot, row_adapter[None, :], own, y, passed, *after)
    return found[0], found[1:-1], found[-1]


def product_kernel(groups, attended_hbm, weight_hbm, *refs):
    token_ref, attended_ref, weight_ref, sems = refs[-4:]
    chips = [m for group in groups for m in group]
    width = weight_ref.shape[2] // 2
    me = lax.axis_index("tensor")
    core, chip = me % 2, me // 2
    fetches = [pltpu.make_async_copy(attended_hbm, attended_ref, sems.at[len(chips)])]
    for i, m in enumerate(chips):
        start = pl.multiple_of((chip ^ m) * 2 * width, 2 * width)
        fetches.append(
            pltpu.make_async_copy(weight_hbm.at[:, pl.ds(start, 2 * width)], weight_ref.at[i], sems.at[i])
        )
    for fetch in fetches:
        fetch.start()
    token_ref[...] = jnp.zeros(token_ref.shape, token_ref.dtype)
    fetches[0].wait()
    there = pl.ds(pl.multiple_of((1 - core) * width, width), width)
    here = pl.ds(pl.multiple_of(core * width, width), width)
    at = 0
    for g, group in enumerate(groups):
        away_ref, stay_ref = refs[2 * g : 2 * g + 2]
        for i in range(len(group)):
            fetches[at + 1].wait()
            away_ref[i] = dot(attended_ref[...], weight_ref[at, :, there]).astype(jnp.bfloat16)
            stay_ref[i] = dot(attended_ref[...], weight_ref[at, :, here])
            at += 1


def product(attended, out_weight, groups, mib):
    rows, depth = attended.shape
    width = out_weight.shape[1] // lax.axis_size("tensor")
    n = sum(len(group) for group in groups)
    out_shape = []
    for group in groups:
        out_shape.append(shape((len(group), rows, width)))
        out_shape.append(shape((len(group), rows, width), jnp.float32))
    out_shape.append(shape((8, 128), jnp.float32))
    return pl.pallas_call(
        functools.partial(product_kernel, groups),
        out_shape=out_shape,
        in_specs=[IN_HBM, IN_HBM],
        out_specs=[IN_VMEM] * len(out_shape),
        scratch_shapes=[
            pltpu.VMEM((rows, depth), jnp.bfloat16),
            pltpu.VMEM((n, depth, 2 * width), jnp.bfloat16),
            DMA((n + 1,)),
        ],
        compiler_params=params(mib),
        cost_estimate=cost(4 * n * rows * depth * width, n * (4 * depth * width + 6 * rows * width)),
        name="product",
    )(attended, out_weight)


def shrink_kernel(layers, down_ref, other_ref, *refs):
    arrived_refs, out_ref = refs[:layers], refs[-1]
    me = lax.axis_index("tensor")
    width = arrived_refs[0].shape[1] // 2
    over = (((1,), (1,)), ((), ()))
    for part, weights_ref in enumerate((down_ref, other_ref)):
        total = jnp.zeros((CAP, down_ref.shape[0]), jnp.float32)
        for k, arrived_ref in enumerate(arrived_refs):
            for side in range(2):
                block = pl.ds(pl.multiple_of((me ^ (4 * k + 2 * side)) * width, width), width)
                total += lax.dot_general(
                    arrived_ref[part * CAP : (part + 1) * CAP, side * width : (side + 1) * width],
                    weights_ref[:, block],
                    over,
                    preferred_element_type=jnp.float32,
                )
        out_ref[part * CAP : (part + 1) * CAP, :] = total


def shrink(down, other, arrived, *after):
    return pl.pallas_call(
        functools.partial(shrink_kernel, len(arrived)),
        out_shape=shape((2 * CAP, down.shape[0]), jnp.float32),
        in_specs=[IN_VMEM] * (2 + len(arrived)) + [ANYWHERE] * len(after),
        out_specs=IN_VMEM,
        compiler_params=params(16),
        cost_estimate=cost(40 * 10**9, 4 * down.size),
        name="shrink",
    )(down, other, *arrived, *after)


def grow_kernel(groups, mine_ref, other_ref, up_ref, up_other_ref, *refs):
    out_refs = refs[-len(groups) :]
    me = lax.axis_index("tensor")
    own = (mine_ref[:CAP, :] + other_ref[CAP:, :]).astype(jnp.bfloat16)
    others = (mine_ref[CAP:, :] + other_ref[:CAP, :]).astype(jnp.bfloat16)
    for masks, out_ref in zip(groups, out_refs):
        width = out_ref.shape[2]
        for i, mask in enumerate(masks):
            block = pl.ds(pl.multiple_of((me ^ mask) * width, width), width)
            out_ref[i, :CAP, :] = dot(own, up_ref[:, block]).astype(jnp.bfloat16)
            out_ref[i, CAP:, :] = dot(others, up_other_ref[:, block]).astype(jnp.bfloat16)


def grow(mine, other, up, up_other, groups, *after):
    width = up.shape[1] // lax.axis_size("tensor")
    return pl.pallas_call(
        functools.partial(grow_kernel, groups),
        out_shape=[shape((len(masks), 2 * CAP, width)) for masks in groups],
        in_specs=[IN_VMEM] * 4 + [ANYWHERE] * len(after),
        out_specs=[IN_VMEM] * len(groups),
        compiler_params=params(16),
        cost_estimate=cost(4 * CAP * up.size, 4 * up.size),
        name="grow",
    )(mine, other, up, up_other, *after)


def join_kernel(terms, target_ref, *refs):
    out_refs = refs[-len(terms) :]
    rows = target_ref.shape[1]
    me = lax.axis_index("tensor")
    j = lax.broadcasted_iota(jnp.int32, (2 * CAP, rows), 0)
    picks = {}
    for (blocks, grown), out_ref in zip(terms, out_refs):
        total = jnp.zeros(out_ref.shape, jnp.float32)
        for at, i in blocks:
            total += refs[at][i].astype(jnp.float32)
        for at, i, mask in grown:
            if mask not in picks:
                slots = (me ^ mask ^ (j // CAP)) * CAP + j % CAP
                picks[mask] = (slots == target_ref[...]).astype(jnp.bfloat16)
            total += lax.dot_general(
                picks[mask], refs[at][i], (((0,), (0,)), ((), ())), preferred_element_type=jnp.float32
            )
        out_ref[...] = total.astype(out_ref.dtype)


def join(target, operands, terms, dtype):
    rows, width = target.shape[1], operands[0].shape[2]
    n = len(terms)
    return pl.pallas_call(
        functools.partial(join_kernel, terms),
        out_shape=[shape((rows, width), dtype)] * n,
        in_specs=[IN_VMEM] * (1 + len(operands)),
        out_specs=[IN_VMEM] * n,
        compiler_params=params(24),
        cost_estimate=cost(4 * n * CAP * rows * width, 10 * n * rows * width),
        name="join",
    )(target, *operands)


def later_kernel(side_ref, came_ref, after_ref, out_ref):
    out_ref[...] = (side_ref[...] + came_ref[...].astype(jnp.float32)).astype(jnp.bfloat16)


def later(side, came, after):
    return pl.pallas_call(
        later_kernel,
        out_shape=shape(side.shape),
        in_specs=[IN_VMEM] * 3,
        out_specs=IN_VMEM,
        compiler_params=params(16),
        cost_estimate=cost(2 * side.size, 8 * side.size),
        name="later",
    )(side, came, after)


def staged(attended, out_weight, adapter_down, adapter_up, row_adapter, adapter_slot):
    f32, bf16 = jnp.float32, jnp.bfloat16
    up, down = adapter_up[0], jnp.swapaxes(adapter_down, 1, 2)[0]
    from_y = swap(attended, 2)
    down_other, up_other = swap(down, 1), swap(up, 1)
    chips = (6, 4, 3, 2, 1, 0)
    away_first, stay_first, away, stay, token = product(attended, out_weight, ((7, 5), chips), 44)
    target, outgoing, away_first = route(
        adapter_slot, row_adapter, attended, from_y, away_first, token, down_other, up_other
    )
    arrived = [outgoing[0]] + [None] * 3
    for k in (2, 3, 1):
        arrived[k] = swap(outgoing[k], 4 * k)
    came_first = swap(away_first, 1)
    go3 = (stay_first[0] + came_first[0].astype(f32)).astype(bf16)
    go2 = (stay_first[1] + came_first[1].astype(f32)).astype(bf16)
    y3, y2 = swap(go3, 2)[None], swap(go2, 2)[None]
    came = swap(away, 1)
    mine = shrink(down, down_other, arrived)
    here, over = grow(mine, swap(mine, 1), up, up_other, (tuple(2 * m for m in chips), (14, 10)), y3, y2)
    over = swap(over, 2)
    at = {m: i for i, m in enumerate(chips)}

    def blocks(m):
        return ((0, at[m]), (1, at[m])), ((2, at[m], 0),)

    def early(m, i):
        base, grown = blocks(m)
        return base + ((4 + i, 0),), grown + ((3, i, 2),)

    go1, go0 = join(target, [stay, came, here], (blocks(3), blocks(1)), bf16)
    y1, y0 = swap(go1, 2), swap(go0, 2)
    (sum3,) = join(target, [stay, came, here, over, y3], (early(6, 0),), bf16)
    z3 = swap(sum3, 4)
    (side2,) = join(target, [stay, came, here, over, y3, y2], (early(4, 1),), f32)
    side1, side0 = join(target, [stay, came, here], (blocks(2), blocks(0)), f32)
    sum2 = (side2 + z3.astype(f32)).astype(bf16)
    z2 = swap(sum2, 8)
    z1 = swap(later(side1, y1, sum2), 4)
    total = side0 + y0.astype(f32) + z1.astype(f32) + z2.astype(f32)
    return total.astype(bf16)


def general(attended, out_weight, adapter_down, adapter_up, row_adapter, adapter_slot):
    tensor_size = lax.axis_size("tensor")
    device = lax.axis_index("tensor")
    row_count = attended.shape[0]
    held_count = adapter_down.shape[0]
    storage = adapter_slot[row_adapter]
    partial_value = jnp.dot(attended, out_weight, preferred_element_type=jnp.float32)
    base_out = lax.psum_scatter(partial_value, "tensor", scatter_dimension=1, tiled=True)
    owner_of = storage // held_count
    local_index = storage % held_count
    owner_hot = (owner_of[:, None] == jnp.arange(tensor_size, dtype=jnp.int32)[None, :]).astype(
        jnp.int32
    )
    position = jnp.sum(jnp.cumsum(owner_hot, axis=0) * owner_hot, axis=1) - 1
    target = owner_of * CAP + position
    slot_row = (
        jnp.full((tensor_size * CAP,), row_count, jnp.int32)
        .at[target]
        .set(jnp.arange(row_count, dtype=jnp.int32))
    )
    padded = jnp.concatenate([attended, jnp.zeros((1, attended.shape[1]), attended.dtype)], axis=0)
    outgoing = padded[slot_row]
    arrived = lax.all_to_all(outgoing, "tensor", split_axis=0, concat_axis=1, tiled=True)
    own_slots = lax.dynamic_slice_in_dim(slot_row, device * CAP, CAP)
    slot_local = jnp.concatenate([local_index, jnp.zeros((1,), jnp.int32)])[own_slots]
    selector = (slot_local[None, :] == jnp.arange(held_count, dtype=jnp.int32)[:, None]).astype(
        jnp.float32
    )
    all_shrunk = jnp.einsum(
        "cd,adk->ack", arrived, adapter_down, preferred_element_type=jnp.float32
    )
    shrunk = jnp.sum(all_shrunk * selector[:, :, None], axis=0).astype(jnp.bfloat16)
    picked = (selector[:, :, None] * shrunk[None].astype(jnp.float32)).astype(jnp.bfloat16)
    expanded = jnp.einsum(
        "ack,akd->cd", picked, adapter_up, preferred_element_type=jnp.float32
    ).astype(jnp.bfloat16)
    returned = lax.all_to_all(expanded, "tensor", split_axis=1, concat_axis=0, tiled=True)
    delta_out = returned[target]
    return (base_out + delta_out.astype(jnp.float32)).astype(jnp.bfloat16)


def shards(*arrays):
    if lax.axis_size("tensor") == 16 and arrays[2].shape[0] == 1:
        return staged(*arrays)
    return general(*arrays)


def solution(mesh):
    placed = (
        P("groups", "tensor"),
        P("tensor", None),
        P(("groups", "tensor"), None, None),
        P(("groups", "tensor"), None, None),
        P("groups"),
        P("groups"),
    )
    return jax.shard_map(
        shards, mesh=mesh, in_specs=placed, out_specs=P("groups", "tensor"), check_vma=False
    )
```

```python
import functools

import jax
import jax.numpy as jnp
from jax import lax
from jax.experimental import pallas as pl
from jax.experimental.pallas import tpu as pltpu
from jax.sharding import PartitionSpec as P

CAP = 32
IN_VMEM = pl.BlockSpec(memory_space=pltpu.VMEM)
IN_HBM = pl.BlockSpec(memory_space=pltpu.HBM)
ANYWHERE = pl.BlockSpec(memory_space=pl.ANY)
DMA = pltpu.SemaphoreType.DMA


def params(mib):
    return pltpu.CompilerParams(vmem_limit_bytes=mib * 1024 * 1024)


def cost(flops, moved):
    return pl.CostEstimate(flops=flops, bytes_accessed=moved, transcendentals=0)


def shape(dims, dtype=jnp.bfloat16):
    return jax.ShapeDtypeStruct(dims, dtype)


def dot(a, b):
    return jnp.dot(a, b, preferred_element_type=jnp.float32)


def swap(value, mask):
    count = lax.axis_size("tensor")
    return lax.ppermute(value, "tensor", [(t, t ^ mask) for t in range(count)])


def once_kernel(*refs):
    pass


def once(values, *after):
    return pl.pallas_call(
        once_kernel,
        out_shape=[shape(value.shape, value.dtype) for value in values],
        in_specs=[ANYWHERE] * (len(values) + len(after)),
        out_specs=[ANYWHERE] * len(values),
        input_output_aliases={i: i for i in range(len(values))},
        cost_estimate=cost(0, 0),
        name="once",
    )(*values, *after)


def route_kernel(count, layers, slot_hbm, row_ref, own_ref, y_ref, *rest):
    target_ref, out_refs = rest[-3 - layers], rest[-2 - layers : -2]
    slot_ref, slot_sem = rest[-2:]
    rows, width = own_ref.shape
    me = lax.axis_index("tensor")
    fetch = pltpu.make_async_copy(slot_hbm, slot_ref, slot_sem)
    fetch.start()
    fetch.wait()
    ids = row_ref[...]
    owner = jnp.zeros_like(ids)
    for a in range(slot_ref.shape[0]):
        owner = jnp.where(ids == a, slot_ref[a], owner)
    hot = (lax.broadcasted_iota(jnp.int32, (count, rows), 0) == owner).astype(jnp.float32)
    earlier = (
        lax.broadcasted_iota(jnp.int32, (rows, rows), 0)
        < lax.broadcasted_iota(jnp.int32, (rows, rows), 1)
    ).astype(jnp.bfloat16)
    ahead = dot(hot.astype(jnp.bfloat16), earlier)
    place = jnp.sum(ahead * hot, axis=0, keepdims=True).astype(jnp.int32)
    target = owner * CAP + place
    target_ref[...] = target
    j = lax.broadcasted_iota(jnp.int32, (2 * CAP, rows), 0)
    for k in range(layers):
        slots = (me ^ (4 * k) ^ (j // CAP)) * CAP + j % CAP
        select = (slots == target).astype(jnp.bfloat16)
        out_refs[k][:, :width] = dot(select, own_ref[...]).astype(jnp.bfloat16)
        out_refs[k][:, width:] = dot(select, y_ref[...]).astype(jnp.bfloat16)


def route(adapter_slot, row_adapter, own, y, *after):
    rows, width = own.shape
    count = lax.axis_size("tensor")
    layers = count // 4
    found = pl.pallas_call(
        functools.partial(route_kernel, count, layers),
        out_shape=[shape((1, rows), jnp.int32)] + [shape((2 * CAP, 2 * width))] * layers,
        in_specs=[IN_HBM] + [IN_VMEM] * 3 + [ANYWHERE] * len(after),
        out_specs=[IN_VMEM] * (layers + 1),
        scratch_shapes=[pltpu.SMEM(adapter_slot.shape, jnp.int32), DMA(())],
        compiler_params=params(16),
        cost_estimate=cost(8 * layers * CAP * rows * width, 16 * layers * CAP * width),
        name="route",
    )(adapter_slot, row_adapter[None, :], own, y, *after)
    return found[0], found[1:]


def product_kernel(groups, attended_hbm, weight_hbm, *refs):
    token_ref, attended_ref, weight_ref, sems = refs[-4:]
    chips = [m for group in groups for m in group]
    width = weight_ref.shape[2] // 2
    me = lax.axis_index("tensor")
    core, chip = me % 2, me // 2
    fetches = [pltpu.make_async_copy(attended_hbm, attended_ref, sems.at[len(chips)])]
    for i, m in enumerate(chips):
        start = pl.multiple_of((chip ^ m) * 2 * width, 2 * width)
        fetches.append(
            pltpu.make_async_copy(weight_hbm.at[:, pl.ds(start, 2 * width)], weight_ref.at[i], sems.at[i])
        )
    for fetch in fetches:
        fetch.start()
    token_ref[...] = jnp.zeros(token_ref.shape, token_ref.dtype)
    fetches[0].wait()
    there = pl.ds(pl.multiple_of((1 - core) * width, width), width)
    here = pl.ds(pl.multiple_of(core * width, width), width)
    at = 0
    for g, group in enumerate(groups):
        away_ref, stay_ref = refs[2 * g : 2 * g + 2]
        for i in range(len(group)):
            fetches[at + 1].wait()
            away_ref[i] = dot(attended_ref[...], weight_ref[at, :, there]).astype(jnp.bfloat16)
            stay_ref[i] = dot(attended_ref[...], weight_ref[at, :, here])
            at += 1


def product(attended, out_weight, groups, mib):
    rows, depth = attended.shape
    width = out_weight.shape[1] // lax.axis_size("tensor")
    n = sum(len(group) for group in groups)
    out_shape = []
    for group in groups:
        out_shape.append(shape((len(group), rows, width)))
        out_shape.append(shape((len(group), rows, width), jnp.float32))
    out_shape.append(shape((8, 128), jnp.float32))
    return pl.pallas_call(
        functools.partial(product_kernel, groups),
        out_shape=out_shape,
        in_specs=[IN_HBM, IN_HBM],
        out_specs=[IN_VMEM] * len(out_shape),
        scratch_shapes=[
            pltpu.VMEM((rows, depth), jnp.bfloat16),
            pltpu.VMEM((n, depth, 2 * width), jnp.bfloat16),
            DMA((n + 1,)),
        ],
        compiler_params=params(mib),
        cost_estimate=cost(4 * n * rows * depth * width, n * (4 * depth * width + 6 * rows * width)),
        name="product",
    )(attended, out_weight)


def shrink_kernel(layers, down_ref, other_ref, *refs):
    arrived_refs, out_ref = refs[:layers], refs[-1]
    me = lax.axis_index("tensor")
    width = arrived_refs[0].shape[1] // 2
    over = (((1,), (1,)), ((), ()))
    for part, weights_ref in enumerate((down_ref, other_ref)):
        total = jnp.zeros((CAP, down_ref.shape[0]), jnp.float32)
        for k, arrived_ref in enumerate(arrived_refs):
            for side in range(2):
                block = pl.ds(pl.multiple_of((me ^ (4 * k + 2 * side)) * width, width), width)
                total += lax.dot_general(
                    arrived_ref[part * CAP : (part + 1) * CAP, side * width : (side + 1) * width],
                    weights_ref[:, block],
                    over,
                    preferred_element_type=jnp.float32,
                )
        out_ref[part * CAP : (part + 1) * CAP, :] = total


def shrink(down, other, arrived, *after):
    return pl.pallas_call(
        functools.partial(shrink_kernel, len(arrived)),
        out_shape=shape((2 * CAP, down.shape[0]), jnp.float32),
        in_specs=[IN_VMEM] * (2 + len(arrived)) + [ANYWHERE] * len(after),
        out_specs=IN_VMEM,
        compiler_params=params(16),
        cost_estimate=cost(40 * 10**9, 4 * down.size),
        name="shrink",
    )(down, other, *arrived, *after)


def grow_kernel(groups, mine_ref, other_ref, up_ref, up_other_ref, *refs):
    out_refs = refs[-len(groups) :]
    me = lax.axis_index("tensor")
    own = (mine_ref[:CAP, :] + other_ref[CAP:, :]).astype(jnp.bfloat16)
    others = (mine_ref[CAP:, :] + other_ref[:CAP, :]).astype(jnp.bfloat16)
    for masks, out_ref in zip(groups, out_refs):
        width = out_ref.shape[2]
        for i, mask in enumerate(masks):
            block = pl.ds(pl.multiple_of((me ^ mask) * width, width), width)
            out_ref[i, :CAP, :] = dot(own, up_ref[:, block]).astype(jnp.bfloat16)
            out_ref[i, CAP:, :] = dot(others, up_other_ref[:, block]).astype(jnp.bfloat16)


def grow(mine, other, up, up_other, groups, *after):
    width = up.shape[1] // lax.axis_size("tensor")
    return pl.pallas_call(
        functools.partial(grow_kernel, groups),
        out_shape=[shape((len(masks), 2 * CAP, width)) for masks in groups],
        in_specs=[IN_VMEM] * 4 + [ANYWHERE] * len(after),
        out_specs=[IN_VMEM] * len(groups),
        compiler_params=params(16),
        cost_estimate=cost(4 * CAP * up.size, 4 * up.size),
        name="grow",
    )(mine, other, up, up_other, *after)


def join_kernel(terms, target_ref, *refs):
    out_refs = refs[-len(terms) :]
    rows = target_ref.shape[1]
    me = lax.axis_index("tensor")
    j = lax.broadcasted_iota(jnp.int32, (2 * CAP, rows), 0)
    picks = {}
    for (blocks, grown), out_ref in zip(terms, out_refs):
        total = jnp.zeros(out_ref.shape, jnp.float32)
        for at, i in blocks:
            total += refs[at][i].astype(jnp.float32)
        for at, i, mask in grown:
            if mask not in picks:
                slots = (me ^ mask ^ (j // CAP)) * CAP + j % CAP
                picks[mask] = (slots == target_ref[...]).astype(jnp.bfloat16)
            total += lax.dot_general(
                picks[mask], refs[at][i], (((0,), (0,)), ((), ())), preferred_element_type=jnp.float32
            )
        out_ref[...] = total.astype(out_ref.dtype)


def join(target, operands, terms, dtype):
    rows, width = target.shape[1], operands[0].shape[2]
    n = len(terms)
    return pl.pallas_call(
        functools.partial(join_kernel, terms),
        out_shape=[shape((rows, width), dtype)] * n,
        in_specs=[IN_VMEM] * (1 + len(operands)),
        out_specs=[IN_VMEM] * n,
        compiler_params=params(24),
        cost_estimate=cost(4 * n * CAP * rows * width, 10 * n * rows * width),
        name="join",
    )(target, *operands)


def staged(attended, out_weight, adapter_down, adapter_up, row_adapter, adapter_slot):
    f32, bf16 = jnp.float32, jnp.bfloat16
    up, down = adapter_up[0], jnp.swapaxes(adapter_down, 1, 2)[0]
    from_y = swap(attended, 2)
    down_other, up_other = swap(down, 1), swap(up, 1)
    chips = (5, 4, 3, 2, 1, 0)
    away_first, stay_first, away, stay, token = product(attended, out_weight, ((7, 6), chips), 44)
    (away_first,) = once((away_first,), from_y, down_other, up_other)
    came_first = swap(away_first, 1)
    (away,) = once((away,), came_first)
    came = swap(away, 1)
    target, outgoing = route(adapter_slot, row_adapter, attended, from_y, token)
    arrived = [outgoing[0]] + [None] * 3
    for k in (2, 3, 1):
        arrived[k] = swap(outgoing[k], 4 * k)
    first = [stay_first[i] + came_first[i].astype(f32) for i in range(2)]
    y3 = swap(first[0].astype(bf16), 2)
    y2 = swap((stay[0] + came[0].astype(f32)).astype(bf16), 2)[None]
    y1 = swap((stay[2] + came[2].astype(f32)).astype(bf16), 2)[None]
    z3 = swap((first[1] + y3.astype(f32)).astype(bf16), 4)[None]
    mine = shrink(down, down_other, arrived)
    here_chips = (4, 2, 1, 0)
    groups = (tuple(2 * m for m in here_chips), (10, 6), (12,), (14,))
    here, over2, over4, over6 = grow(mine, swap(mine, 1), up, up_other, groups, z3, y2, y1)
    over2, over4, over6 = swap(over2, 2), swap(over4, 4), swap(over6, 6)

    def blocks(m):
        return ((0, chips.index(m)), (1, chips.index(m))), ((2, here_chips.index(m), 0),)

    base, grown = blocks(4)
    (sum2,) = join(
        target,
        [stay, came, here, over2, over4, over6, z3, y2],
        ((base + ((6, 0), (7, 0)), grown + ((3, 0, 2), (4, 0, 4), (5, 0, 6))),),
        bf16,
    )
    z2 = swap(sum2, 8)
    base, grown = blocks(2)
    (sum1,) = join(
        target, [stay, came, here, over2, y1, sum2], ((base + ((4, 0),), grown + ((3, 1, 2),)),), bf16
    )
    z1 = swap(sum1, 4)
    (go0,) = join(target, [stay, came, here], (blocks(1),), bf16)
    y0 = swap(go0, 2)
    (side0,) = join(target, [stay, came, here], (blocks(0),), f32)
    total = side0 + y0.astype(f32) + z1.astype(f32) + z2.astype(f32)
    return total.astype(bf16)


def general(attended, out_weight, adapter_down, adapter_up, row_adapter, adapter_slot):
    tensor_size = lax.axis_size("tensor")
    device = lax.axis_index("tensor")
    row_count = attended.shape[0]
    held_count = adapter_down.shape[0]
    storage = adapter_slot[row_adapter]
    partial_value = jnp.dot(attended, out_weight, preferred_element_type=jnp.float32)
    base_out = lax.psum_scatter(partial_value, "tensor", scatter_dimension=1, tiled=True)
    owner_of = storage // held_count
    local_index = storage % held_count
    owner_hot = (owner_of[:, None] == jnp.arange(tensor_size, dtype=jnp.int32)[None, :]).astype(
        jnp.int32
    )
    position = jnp.sum(jnp.cumsum(owner_hot, axis=0) * owner_hot, axis=1) - 1
    target = owner_of * CAP + position
    slot_row = (
        jnp.full((tensor_size * CAP,), row_count, jnp.int32)
        .at[target]
        .set(jnp.arange(row_count, dtype=jnp.int32))
    )
    padded = jnp.concatenate([attended, jnp.zeros((1, attended.shape[1]), attended.dtype)], axis=0)
    outgoing = padded[slot_row]
    arrived = lax.all_to_all(outgoing, "tensor", split_axis=0, concat_axis=1, tiled=True)
    own_slots = lax.dynamic_slice_in_dim(slot_row, device * CAP, CAP)
    slot_local = jnp.concatenate([local_index, jnp.zeros((1,), jnp.int32)])[own_slots]
    selector = (slot_local[None, :] == jnp.arange(held_count, dtype=jnp.int32)[:, None]).astype(
        jnp.float32
    )
    all_shrunk = jnp.einsum(
        "cd,adk->ack", arrived, adapter_down, preferred_element_type=jnp.float32
    )
    shrunk = jnp.sum(all_shrunk * selector[:, :, None], axis=0).astype(jnp.bfloat16)
    picked = (selector[:, :, None] * shrunk[None].astype(jnp.float32)).astype(jnp.bfloat16)
    expanded = jnp.einsum(
        "ack,akd->cd", picked, adapter_up, preferred_element_type=jnp.float32
    ).astype(jnp.bfloat16)
    returned = lax.all_to_all(expanded, "tensor", split_axis=1, concat_axis=0, tiled=True)
    delta_out = returned[target]
    return (base_out + delta_out.astype(jnp.float32)).astype(jnp.bfloat16)


def shards(*arrays):
    if lax.axis_size("tensor") == 16 and arrays[2].shape[0] == 1:
        return staged(*arrays)
    return general(*arrays)


def solution(mesh):
    placed = (
        P("groups", "tensor"),
        P("tensor", None),
        P(("groups", "tensor"), None, None),
        P(("groups", "tensor"), None, None),
        P("groups"),
        P("groups"),
    )
    return jax.shard_map(
        shards, mesh=mesh, in_specs=placed, out_specs=P("groups", "tensor"), check_vma=False
    )
```

```python
import functools

import jax
import jax.numpy as jnp
from jax import lax
from jax.experimental import pallas as pl
from jax.experimental.pallas import tpu as pltpu
from jax.sharding import PartitionSpec as P

CAP = 32
IN_VMEM = pl.BlockSpec(memory_space=pltpu.VMEM)
IN_HBM = pl.BlockSpec(memory_space=pltpu.HBM)
ANYWHERE = pl.BlockSpec(memory_space=pl.ANY)
DMA = pltpu.SemaphoreType.DMA


def params(mib):
    return pltpu.CompilerParams(vmem_limit_bytes=mib * 1024 * 1024)


def cost(flops, moved):
    return pl.CostEstimate(flops=flops, bytes_accessed=moved, transcendentals=0)


def shape(dims, dtype=jnp.bfloat16):
    return jax.ShapeDtypeStruct(dims, dtype)


def dot(a, b):
    return jnp.dot(a, b, preferred_element_type=jnp.float32)


def swap(value, mask):
    count = lax.axis_size("tensor")
    return lax.ppermute(value, "tensor", [(t, t ^ mask) for t in range(count)])


def once_kernel(*refs):
    pass


def once(values, *after):
    return pl.pallas_call(
        once_kernel,
        out_shape=[shape(value.shape, value.dtype) for value in values],
        in_specs=[ANYWHERE] * (len(values) + len(after)),
        out_specs=[ANYWHERE] * len(values),
        input_output_aliases={i: i for i in range(len(values))},
        compiler_params=params(1),
        cost_estimate=cost(0, 0),
        name="once",
    )(*values, *after)


def route_kernel(count, layers, slot_hbm, row_ref, own_ref, y_ref, *rest):
    target_ref, out_refs = rest[-3 - layers], rest[-2 - layers : -2]
    slot_ref, slot_sem = rest[-2:]
    rows, width = own_ref.shape
    me = lax.axis_index("tensor")
    fetch = pltpu.make_async_copy(slot_hbm, slot_ref, slot_sem)
    fetch.start()
    fetch.wait()
    ids = row_ref[...]
    owner = jnp.zeros_like(ids)
    for a in range(slot_ref.shape[0]):
        owner = jnp.where(ids == a, slot_ref[a], owner)
    hot = (lax.broadcasted_iota(jnp.int32, (count, rows), 0) == owner).astype(jnp.float32)
    earlier = (
        lax.broadcasted_iota(jnp.int32, (rows, rows), 0)
        < lax.broadcasted_iota(jnp.int32, (rows, rows), 1)
    ).astype(jnp.bfloat16)
    ahead = dot(hot.astype(jnp.bfloat16), earlier)
    place = jnp.sum(ahead * hot, axis=0, keepdims=True).astype(jnp.int32)
    target = owner * CAP + place
    target_ref[...] = target
    j = lax.broadcasted_iota(jnp.int32, (2 * CAP, rows), 0)
    for k in range(layers):
        slots = (me ^ (4 * k) ^ (j // CAP)) * CAP + j % CAP
        select = (slots == target).astype(jnp.bfloat16)
        out_refs[k][:, :width] = dot(select, own_ref[...]).astype(jnp.bfloat16)
        out_refs[k][:, width:] = dot(select, y_ref[...]).astype(jnp.bfloat16)


def route(adapter_slot, row_adapter, own, y, *after):
    rows, width = own.shape
    count = lax.axis_size("tensor")
    layers = count // 4
    found = pl.pallas_call(
        functools.partial(route_kernel, count, layers),
        out_shape=[shape((1, rows), jnp.int32)] + [shape((2 * CAP, 2 * width))] * layers,
        in_specs=[IN_HBM] + [IN_VMEM] * 3 + [ANYWHERE] * len(after),
        out_specs=[IN_VMEM] * (layers + 1),
        scratch_shapes=[pltpu.SMEM(adapter_slot.shape, jnp.int32), DMA(())],
        compiler_params=params(16),
        cost_estimate=cost(8 * layers * CAP * rows * width, 16 * layers * CAP * width),
        name="route",
    )(adapter_slot, row_adapter[None, :], own, y, *after)
    return found[0], found[1:]


def product_kernel(groups, attended_hbm, weight_hbm, *refs):
    token_ref, attended_ref, weight_ref, sems = refs[-4:]
    chips = [m for group in groups for m in group]
    width = weight_ref.shape[2] // 2
    me = lax.axis_index("tensor")
    core, chip = me % 2, me // 2
    fetches = [pltpu.make_async_copy(attended_hbm, attended_ref, sems.at[len(chips)])]
    for i, m in enumerate(chips):
        start = pl.multiple_of((chip ^ m) * 2 * width, 2 * width)
        fetches.append(
            pltpu.make_async_copy(weight_hbm.at[:, pl.ds(start, 2 * width)], weight_ref.at[i], sems.at[i])
        )
    for fetch in fetches:
        fetch.start()
    token_ref[...] = jnp.zeros(token_ref.shape, token_ref.dtype)
    fetches[0].wait()
    there = pl.ds(pl.multiple_of((1 - core) * width, width), width)
    here = pl.ds(pl.multiple_of(core * width, width), width)
    at = 0
    for g, group in enumerate(groups):
        away_ref, stay_ref = refs[2 * g : 2 * g + 2]
        for i in range(len(group)):
            fetches[at + 1].wait()
            away_ref[i] = dot(attended_ref[...], weight_ref[at, :, there]).astype(jnp.bfloat16)
            stay_ref[i] = dot(attended_ref[...], weight_ref[at, :, here])
            at += 1


def product(attended, out_weight, groups, mib):
    rows, depth = attended.shape
    width = out_weight.shape[1] // lax.axis_size("tensor")
    n = sum(len(group) for group in groups)
    out_shape = []
    for group in groups:
        out_shape.append(shape((len(group), rows, width)))
        out_shape.append(shape((len(group), rows, width), jnp.float32))
    out_shape.append(shape((8, 128), jnp.float32))
    return pl.pallas_call(
        functools.partial(product_kernel, groups),
        out_shape=out_shape,
        in_specs=[IN_HBM, IN_HBM],
        out_specs=[IN_VMEM] * len(out_shape),
        scratch_shapes=[
            pltpu.VMEM((rows, depth), jnp.bfloat16),
            pltpu.VMEM((n, depth, 2 * width), jnp.bfloat16),
            DMA((n + 1,)),
        ],
        compiler_params=params(mib),
        cost_estimate=cost(4 * n * rows * depth * width, n * (4 * depth * width + 6 * rows * width)),
        name="product",
    )(attended, out_weight)


def shrink_kernel(layers, down_ref, other_ref, *refs):
    arrived_refs, out_ref = refs[:layers], refs[-1]
    me = lax.axis_index("tensor")
    width = arrived_refs[0].shape[1] // 2
    over = (((1,), (1,)), ((), ()))
    for part, weights_ref in enumerate((down_ref, other_ref)):
        total = jnp.zeros((CAP, down_ref.shape[0]), jnp.float32)
        for k, arrived_ref in enumerate(arrived_refs):
            for side in range(2):
                block = pl.ds(pl.multiple_of((me ^ (4 * k + 2 * side)) * width, width), width)
                total += lax.dot_general(
                    arrived_ref[part * CAP : (part + 1) * CAP, side * width : (side + 1) * width],
                    weights_ref[:, block],
                    over,
                    preferred_element_type=jnp.float32,
                )
        out_ref[part * CAP : (part + 1) * CAP, :] = total


def shrink(down, other, arrived, *after):
    return pl.pallas_call(
        functools.partial(shrink_kernel, len(arrived)),
        out_shape=shape((2 * CAP, down.shape[0]), jnp.float32),
        in_specs=[IN_VMEM] * (2 + len(arrived)) + [ANYWHERE] * len(after),
        out_specs=IN_VMEM,
        compiler_params=params(16),
        cost_estimate=cost(40 * 10**9, 4 * down.size),
        name="shrink",
    )(down, other, *arrived, *after)


def grow_kernel(groups, mine_ref, other_ref, up_ref, up_other_ref, *refs):
    out_refs = refs[-len(groups) :]
    me = lax.axis_index("tensor")
    own = (mine_ref[:CAP, :] + other_ref[CAP:, :]).astype(jnp.bfloat16)
    others = (mine_ref[CAP:, :] + other_ref[:CAP, :]).astype(jnp.bfloat16)
    for masks, out_ref in zip(groups, out_refs):
        width = out_ref.shape[2]
        for i, mask in enumerate(masks):
            block = pl.ds(pl.multiple_of((me ^ mask) * width, width), width)
            out_ref[i, :CAP, :] = dot(own, up_ref[:, block]).astype(jnp.bfloat16)
            out_ref[i, CAP:, :] = dot(others, up_other_ref[:, block]).astype(jnp.bfloat16)


def grow(mine, other, up, up_other, groups, *after):
    width = up.shape[1] // lax.axis_size("tensor")
    return pl.pallas_call(
        functools.partial(grow_kernel, groups),
        out_shape=[shape((len(masks), 2 * CAP, width)) for masks in groups],
        in_specs=[IN_VMEM] * 4 + [ANYWHERE] * len(after),
        out_specs=[IN_VMEM] * len(groups),
        compiler_params=params(16),
        cost_estimate=cost(4 * CAP * up.size, 4 * up.size),
        name="grow",
    )(mine, other, up, up_other, *after)


def join_kernel(terms, target_ref, *refs):
    out_refs = refs[-len(terms) :]
    rows = target_ref.shape[1]
    me = lax.axis_index("tensor")
    j = lax.broadcasted_iota(jnp.int32, (2 * CAP, rows), 0)
    picks = {}
    for (blocks, grown), out_ref in zip(terms, out_refs):
        total = jnp.zeros(out_ref.shape, jnp.float32)
        for at, i in blocks:
            total += refs[at][i].astype(jnp.float32)
        for at, i, mask in grown:
            if mask not in picks:
                slots = (me ^ mask ^ (j // CAP)) * CAP + j % CAP
                picks[mask] = (slots == target_ref[...]).astype(jnp.bfloat16)
            total += lax.dot_general(
                picks[mask], refs[at][i], (((0,), (0,)), ((), ())), preferred_element_type=jnp.float32
            )
        out_ref[...] = total.astype(out_ref.dtype)


def join(target, operands, terms, dtype):
    rows, width = target.shape[1], operands[0].shape[2]
    n = len(terms)
    return pl.pallas_call(
        functools.partial(join_kernel, terms),
        out_shape=[shape((rows, width), dtype)] * n,
        in_specs=[IN_VMEM] * (1 + len(operands)),
        out_specs=[IN_VMEM] * n,
        compiler_params=params(24),
        cost_estimate=cost(4 * n * CAP * rows * width, 10 * n * rows * width),
        name="join",
    )(target, *operands)


def staged(attended, out_weight, adapter_down, adapter_up, row_adapter, adapter_slot):
    f32, bf16 = jnp.float32, jnp.bfloat16
    up, down = adapter_up[0], jnp.swapaxes(adapter_down, 1, 2)[0]
    from_y = swap(attended, 2)
    down_other, up_other = swap(down, 1), swap(up, 1)
    chips = (5, 4, 3, 2, 1, 0)
    away_first, stay_first, away, stay, token = product(attended, out_weight, ((7, 6), chips), 44)
    (away_first,) = once((away_first,), from_y, down_other, up_other)
    came_first = swap(away_first, 1)
    (away,) = once((away,), came_first)
    came = swap(away, 1)
    target, outgoing = route(adapter_slot, row_adapter, attended, from_y, token)
    arrived = [outgoing[0]] + [None] * 3
    for k in (2, 3, 1):
        arrived[k] = swap(outgoing[k], 4 * k)
    first = [stay_first[i] + came_first[i].astype(f32) for i in range(2)]
    y3 = swap(first[0].astype(bf16), 2)
    y2 = swap((stay[0] + came[0].astype(f32)).astype(bf16), 2)[None]
    y1 = swap((stay[2] + came[2].astype(f32)).astype(bf16), 2)[None]
    z3 = swap((first[1] + y3.astype(f32)).astype(bf16), 4)[None]
    mine = shrink(down, down_other, arrived)
    here_chips = (4, 2, 1, 0)
    groups = (tuple(2 * m for m in here_chips), (10, 6), (12,), (14,))
    here, over2, over4, over6 = grow(mine, swap(mine, 1), up, up_other, groups, z3, y2, y1)
    over2, over4, over6 = swap(over2, 2), swap(over4, 4), swap(over6, 6)

    def blocks(m):
        return ((0, chips.index(m)), (1, chips.index(m))), ((2, here_chips.index(m), 0),)

    base, grown = blocks(4)
    (sum2,) = join(
        target,
        [stay, came, here, over2, over4, over6, z3, y2],
        ((base + ((6, 0), (7, 0)), grown + ((3, 0, 2), (4, 0, 4), (5, 0, 6))),),
        bf16,
    )
    z2 = swap(sum2, 8)
    base, grown = blocks(2)
    (sum1,) = join(
        target, [stay, came, here, over2, y1, sum2], ((base + ((4, 0),), grown + ((3, 1, 2),)),), bf16
    )
    z1 = swap(sum1, 4)
    (go0,) = join(target, [stay, came, here], (blocks(1),), bf16)
    y0 = swap(go0, 2)
    (side0,) = join(target, [stay, came, here], (blocks(0),), f32)
    total = side0 + y0.astype(f32) + z1.astype(f32) + z2.astype(f32)
    return total.astype(bf16)


def general(attended, out_weight, adapter_down, adapter_up, row_adapter, adapter_slot):
    tensor_size = lax.axis_size("tensor")
    device = lax.axis_index("tensor")
    row_count = attended.shape[0]
    held_count = adapter_down.shape[0]
    storage = adapter_slot[row_adapter]
    partial_value = jnp.dot(attended, out_weight, preferred_element_type=jnp.float32)
    base_out = lax.psum_scatter(partial_value, "tensor", scatter_dimension=1, tiled=True)
    owner_of = storage // held_count
    local_index = storage % held_count
    owner_hot = (owner_of[:, None] == jnp.arange(tensor_size, dtype=jnp.int32)[None, :]).astype(
        jnp.int32
    )
    position = jnp.sum(jnp.cumsum(owner_hot, axis=0) * owner_hot, axis=1) - 1
    target = owner_of * CAP + position
    slot_row = (
        jnp.full((tensor_size * CAP,), row_count, jnp.int32)
        .at[target]
        .set(jnp.arange(row_count, dtype=jnp.int32))
    )
    padded = jnp.concatenate([attended, jnp.zeros((1, attended.shape[1]), attended.dtype)], axis=0)
    outgoing = padded[slot_row]
    arrived = lax.all_to_all(outgoing, "tensor", split_axis=0, concat_axis=1, tiled=True)
    own_slots = lax.dynamic_slice_in_dim(slot_row, device * CAP, CAP)
    slot_local = jnp.concatenate([local_index, jnp.zeros((1,), jnp.int32)])[own_slots]
    selector = (slot_local[None, :] == jnp.arange(held_count, dtype=jnp.int32)[:, None]).astype(
        jnp.float32
    )
    all_shrunk = jnp.einsum(
        "cd,adk->ack", arrived, adapter_down, preferred_element_type=jnp.float32
    )
    shrunk = jnp.sum(all_shrunk * selector[:, :, None], axis=0).astype(jnp.bfloat16)
    picked = (selector[:, :, None] * shrunk[None].astype(jnp.float32)).astype(jnp.bfloat16)
    expanded = jnp.einsum(
        "ack,akd->cd", picked, adapter_up, preferred_element_type=jnp.float32
    ).astype(jnp.bfloat16)
    returned = lax.all_to_all(expanded, "tensor", split_axis=1, concat_axis=0, tiled=True)
    delta_out = returned[target]
    return (base_out + delta_out.astype(jnp.float32)).astype(jnp.bfloat16)


def shards(*arrays):
    if lax.axis_size("tensor") == 16 and arrays[2].shape[0] == 1:
        return staged(*arrays)
    return general(*arrays)


def solution(mesh):
    placed = (
        P("groups", "tensor"),
        P("tensor", None),
        P(("groups", "tensor"), None, None),
        P(("groups", "tensor"), None, None),
        P("groups"),
        P("groups"),
    )
    return jax.shard_map(
        shards, mesh=mesh, in_specs=placed, out_specs=P("groups", "tensor"), check_vma=False
    )
```

```python
import functools

import jax
import jax.numpy as jnp
from jax import lax
from jax.experimental import pallas as pl
from jax.experimental.pallas import tpu as pltpu
from jax.sharding import PartitionSpec as P

CAP = 32
IN_VMEM = pl.BlockSpec(memory_space=pltpu.VMEM)
IN_HBM = pl.BlockSpec(memory_space=pltpu.HBM)
ANYWHERE = pl.BlockSpec(memory_space=pl.ANY)
DMA = pltpu.SemaphoreType.DMA


def params(mib):
    return pltpu.CompilerParams(vmem_limit_bytes=mib * 1024 * 1024)


def cost(flops, moved):
    return pl.CostEstimate(flops=flops, bytes_accessed=moved, transcendentals=0)


def shape(dims, dtype=jnp.bfloat16):
    return jax.ShapeDtypeStruct(dims, dtype)


def dot(a, b):
    return jnp.dot(a, b, preferred_element_type=jnp.float32)


def swap(value, mask):
    count = lax.axis_size("tensor")
    return lax.ppermute(value, "tensor", [(t, t ^ mask) for t in range(count)])


def once_kernel(*refs):
    pass


def once(values, *after):
    return pl.pallas_call(
        once_kernel,
        out_shape=[shape(value.shape, value.dtype) for value in values],
        in_specs=[ANYWHERE] * (len(values) + len(after)),
        out_specs=[ANYWHERE] * len(values),
        input_output_aliases={i: i for i in range(len(values))},
        compiler_params=params(1),
        cost_estimate=cost(0, 0),
        name="once",
    )(*values, *after)


def route_kernel(count, layers, slot_hbm, row_ref, own_ref, y_ref, *rest):
    target_ref, out_refs = rest[-3 - layers], rest[-2 - layers : -2]
    slot_ref, slot_sem = rest[-2:]
    rows, width = own_ref.shape
    me = lax.axis_index("tensor")
    fetch = pltpu.make_async_copy(slot_hbm, slot_ref, slot_sem)
    fetch.start()
    fetch.wait()
    ids = row_ref[...]
    owner = jnp.zeros_like(ids)
    for a in range(slot_ref.shape[0]):
        owner = jnp.where(ids == a, slot_ref[a], owner)
    hot = (lax.broadcasted_iota(jnp.int32, (count, rows), 0) == owner).astype(jnp.float32)
    earlier = (
        lax.broadcasted_iota(jnp.int32, (rows, rows), 0)
        < lax.broadcasted_iota(jnp.int32, (rows, rows), 1)
    ).astype(jnp.bfloat16)
    ahead = dot(hot.astype(jnp.bfloat16), earlier)
    place = jnp.sum(ahead * hot, axis=0, keepdims=True).astype(jnp.int32)
    target = owner * CAP + place
    target_ref[...] = target
    j = lax.broadcasted_iota(jnp.int32, (2 * CAP, rows), 0)
    for k in range(layers):
        slots = (me ^ (4 * k) ^ (j // CAP)) * CAP + j % CAP
        select = (slots == target).astype(jnp.bfloat16)
        out_refs[k][:, :width] = dot(select, own_ref[...]).astype(jnp.bfloat16)
        out_refs[k][:, width:] = dot(select, y_ref[...]).astype(jnp.bfloat16)


def route(adapter_slot, row_adapter, own, y, *after):
    rows, width = own.shape
    count = lax.axis_size("tensor")
    layers = count // 4
    found = pl.pallas_call(
        functools.partial(route_kernel, count, layers),
        out_shape=[shape((1, rows), jnp.int32)] + [shape((2 * CAP, 2 * width))] * layers,
        in_specs=[IN_HBM] + [IN_VMEM] * 3 + [ANYWHERE] * len(after),
        out_specs=[IN_VMEM] * (layers + 1),
        scratch_shapes=[pltpu.SMEM(adapter_slot.shape, jnp.int32), DMA(())],
        compiler_params=params(16),
        cost_estimate=cost(8 * layers * CAP * rows * width, 16 * layers * CAP * width),
        name="route",
    )(adapter_slot, row_adapter[None, :], own, y, *after)
    return found[0], found[1:]


def product_kernel(groups, attended_hbm, weight_hbm, *refs):
    token_ref, attended_ref, weight_ref, sems = refs[-4:]
    chips = [m for group in groups for m in group]
    width = weight_ref.shape[2] // 2
    me = lax.axis_index("tensor")
    core, chip = me % 2, me // 2
    fetches = [pltpu.make_async_copy(attended_hbm, attended_ref, sems.at[len(chips)])]
    for i, m in enumerate(chips):
        start = pl.multiple_of((chip ^ m) * 2 * width, 2 * width)
        fetches.append(
            pltpu.make_async_copy(weight_hbm.at[:, pl.ds(start, 2 * width)], weight_ref.at[i], sems.at[i])
        )
    for fetch in fetches:
        fetch.start()
    token_ref[...] = jnp.zeros(token_ref.shape, token_ref.dtype)
    fetches[0].wait()
    there = pl.ds(pl.multiple_of((1 - core) * width, width), width)
    here = pl.ds(pl.multiple_of(core * width, width), width)
    at = 0
    for g, group in enumerate(groups):
        away_ref, stay_ref = refs[2 * g : 2 * g + 2]
        for i in range(len(group)):
            fetches[at + 1].wait()
            away_ref[i] = dot(attended_ref[...], weight_ref[at, :, there]).astype(jnp.bfloat16)
            stay_ref[i] = dot(attended_ref[...], weight_ref[at, :, here])
            at += 1


def product(attended, out_weight, groups, mib):
    rows, depth = attended.shape
    width = out_weight.shape[1] // lax.axis_size("tensor")
    n = sum(len(group) for group in groups)
    out_shape = []
    for group in groups:
        out_shape.append(shape((len(group), rows, width)))
        out_shape.append(shape((len(group), rows, width), jnp.float32))
    out_shape.append(shape((8, 128), jnp.float32))
    return pl.pallas_call(
        functools.partial(product_kernel, groups),
        out_shape=out_shape,
        in_specs=[IN_HBM, IN_HBM],
        out_specs=[IN_VMEM] * len(out_shape),
        scratch_shapes=[
            pltpu.VMEM((rows, depth), jnp.bfloat16),
            pltpu.VMEM((n, depth, 2 * width), jnp.bfloat16),
            DMA((n + 1,)),
        ],
        compiler_params=params(mib),
        cost_estimate=cost(4 * n * rows * depth * width, n * (4 * depth * width + 6 * rows * width)),
        name="product",
    )(attended, out_weight)


def shrink_kernel(distances, down_ref, other_ref, *refs):
    arrived_refs, out_ref = refs[: len(distances)], refs[-1]
    me = lax.axis_index("tensor")
    width = arrived_refs[0].shape[1] // 2
    over = (((1,), (1,)), ((), ()))
    for part, weights_ref in enumerate((down_ref, other_ref)):
        total = jnp.zeros((CAP, down_ref.shape[0]), jnp.float32)
        for k, arrived_ref in zip(distances, arrived_refs):
            for side in range(2):
                block = pl.ds(pl.multiple_of((me ^ (4 * k + 2 * side)) * width, width), width)
                total += lax.dot_general(
                    arrived_ref[part * CAP : (part + 1) * CAP, side * width : (side + 1) * width],
                    weights_ref[:, block],
                    over,
                    preferred_element_type=jnp.float32,
                )
        out_ref[part * CAP : (part + 1) * CAP, :] = total


def shrink(down, other, arrived, *after):
    return pl.pallas_call(
        functools.partial(shrink_kernel, tuple(arrived)),
        out_shape=shape((2 * CAP, down.shape[0]), jnp.float32),
        in_specs=[IN_VMEM] * (2 + len(arrived)) + [ANYWHERE] * len(after),
        out_specs=IN_VMEM,
        compiler_params=params(16),
        cost_estimate=cost(40*10**9, 4 * down.size),
        name="shrink",
    )(down, other, *arrived.values(), *after)


def grow_kernel(groups, mine_ref, other_ref, up_ref, up_other_ref, *refs):
    out_refs = refs[-len(groups) :]
    me = lax.axis_index("tensor")
    own = (mine_ref[:CAP, :] + other_ref[CAP:, :]).astype(jnp.bfloat16)
    others = (mine_ref[CAP:, :] + other_ref[:CAP, :]).astype(jnp.bfloat16)
    for masks, out_ref in zip(groups, out_refs):
        width = out_ref.shape[2]
        for i, mask in enumerate(masks):
            block = pl.ds(pl.multiple_of((me ^ mask) * width, width), width)
            out_ref[i, :CAP, :] = dot(own, up_ref[:, block]).astype(jnp.bfloat16)
            out_ref[i, CAP:, :] = dot(others, up_other_ref[:, block]).astype(jnp.bfloat16)


def grow(mine, other, up, up_other, groups, *after):
    width = up.shape[1] // lax.axis_size("tensor")
    return pl.pallas_call(
        functools.partial(grow_kernel, groups),
        out_shape=[shape((len(masks), 2 * CAP, width)) for masks in groups],
        in_specs=[IN_VMEM] * 4 + [ANYWHERE] * len(after),
        out_specs=[IN_VMEM] * len(groups),
        compiler_params=params(16),
        cost_estimate=cost(4*CAP*up.size, 4 * up.size),
        name="grow",
    )(mine, other, up, up_other, *after)


def join_kernel(terms, target_ref, *refs):
    out_refs = refs[-len(terms) :]
    rows = target_ref.shape[1]
    me = lax.axis_index("tensor")
    j = lax.broadcasted_iota(jnp.int32, (2 * CAP, rows), 0)
    picks = {}
    for (blocks, grown), out_ref in zip(terms, out_refs):
        total = jnp.zeros(out_ref.shape, jnp.float32)
        for at, i in blocks:
            total += refs[at][i].astype(jnp.float32)
        for at, i, mask in grown:
            if mask not in picks:
                slots = (me ^ mask ^ (j // CAP)) * CAP + j % CAP
                picks[mask] = (slots == target_ref[...]).astype(jnp.bfloat16)
            total += lax.dot_general(
                picks[mask], refs[at][i], (((0,), (0,)), ((), ())), preferred_element_type=jnp.float32
            )
        out_ref[...] = total.astype(out_ref.dtype)


def join(target, operands, terms, dtype):
    rows, width = target.shape[1], operands[0].shape[2]
    n = len(terms)
    return pl.pallas_call(
        functools.partial(join_kernel, terms),
        out_shape=[shape((rows, width), dtype)] * n,
        in_specs=[IN_VMEM] * (1 + len(operands)),
        out_specs=[IN_VMEM] * n,
        compiler_params=params(24),
        cost_estimate=cost(4 * n * CAP * rows * width, 10 * n * rows * width),
        name="join",
    )(target, *operands)


def staged(attended, out_weight, adapter_down, adapter_up, row_adapter, adapter_slot):
    f32, bf16 = jnp.float32, jnp.bfloat16
    up, down = adapter_up[0], jnp.swapaxes(adapter_down, 1, 2)[0]
    from_y = swap(attended, 2)
    down_other, up_other = swap(down, 1), swap(up, 1)
    chips = (6, 4, 3, 2, 1, 0)
    away_first, stay_first, away, stay, token = product(attended, out_weight, ((7, 5), chips), 44)
    target, outgoing = route(adapter_slot, row_adapter, attended, from_y, token, down_other, up_other)
    arrived = {k: swap(outgoing[k], 4 * k) for k in (2,3,1)}
    arrived[0] = outgoing[0]
    away_first, away = once((away_first, away), target)
    came_first, came = swap(away_first, 1), swap(away, 1)

    def base(m):
        return stay[chips.index(m)] + came[chips.index(m)].astype(f32)

    y3 = swap((stay_first[0] + came_first[0].astype(f32)).astype(bf16), 2)
    y2 = swap((stay_first[1] + came_first[1].astype(f32)).astype(bf16), 2)[None]
    mine = shrink(down, down_other, arrived)
    ready3, go1 = once((y3, base(3).astype(bf16)), mine)
    z3 = swap((base(6) + ready3.astype(f32)).astype(bf16), 4)[None]
    y1 = swap(go1, 2)[None]
    here_chips = (4, 2, 1, 0)
    groups = (tuple(2 * m for m in here_chips), (10, 6), (12,), (14,))
    here, over2, over4, over6 = grow(mine, swap(mine, 1), up, up_other, groups, y3, y2)
    over2, over4, over6 = swap(over2, 2), swap(over4, 4), swap(over6, 6)

    def blocks(m):
        return ((0, chips.index(m)), (1, chips.index(m))), ((2, here_chips.index(m), 0),)

    sums, grown = blocks(4)
    (sum2,) = join(
        target,
        [stay, came, here, over2, over4, over6, z3, y2],
        ((sums + ((6, 0), (7, 0)), grown + ((3, 0, 2), (4, 0, 4), (5, 0, 6))),),
        bf16,
    )
    z2 = swap(sum2, 8)
    sums, grown = blocks(2)
    (sum1,) = join(
        target, [stay, came, here, over2, y1, sum2], ((sums + ((4, 0),), grown + ((3, 1, 2),)),), bf16
    )
    z1 = swap(sum1, 4)
    (go0,) = join(target, [stay, came, here, sum2], (blocks(1),), bf16)
    y0 = swap(go0, 2)
    (side0,) = join(target, [stay, came, here], (blocks(0),), f32)
    total = side0 + y0.astype(f32) + z2.astype(f32) + z1.astype(f32)
    return total.astype(bf16)


def general(attended, out_weight, adapter_down, adapter_up, row_adapter, adapter_slot):
    tensor_size = lax.axis_size("tensor")
    device = lax.axis_index("tensor")
    row_count = attended.shape[0]
    held_count = adapter_down.shape[0]
    storage = adapter_slot[row_adapter]
    partial_value = jnp.dot(attended, out_weight, preferred_element_type=jnp.float32)
    base_out = lax.psum_scatter(partial_value, "tensor", scatter_dimension=1, tiled=True)
    owner_of = storage // held_count
    local_index = storage % held_count
    owner_hot = (owner_of[:, None] == jnp.arange(tensor_size, dtype=jnp.int32)[None, :]).astype(
        jnp.int32
    )
    position = jnp.sum(jnp.cumsum(owner_hot, axis=0) * owner_hot, axis=1) - 1
    target = owner_of * CAP + position
    slot_row = (
        jnp.full((tensor_size * CAP,), row_count, jnp.int32)
        .at[target]
        .set(jnp.arange(row_count, dtype=jnp.int32))
    )
    padded = jnp.concatenate([attended, jnp.zeros((1, attended.shape[1]), attended.dtype)], axis=0)
    outgoing = padded[slot_row]
    arrived = lax.all_to_all(outgoing, "tensor", split_axis=0, concat_axis=1, tiled=True)
    own_slots = lax.dynamic_slice_in_dim(slot_row, device * CAP, CAP)
    slot_local = jnp.concatenate([local_index, jnp.zeros((1,), jnp.int32)])[own_slots]
    selector = (slot_local[None, :] == jnp.arange(held_count, dtype=jnp.int32)[:, None]).astype(
        jnp.float32
    )
    all_shrunk = jnp.einsum(
        "cd,adk->ack", arrived, adapter_down, preferred_element_type=jnp.float32
    )
    shrunk = jnp.sum(all_shrunk * selector[:, :, None], axis=0).astype(jnp.bfloat16)
    picked = (selector[:, :, None] * shrunk[None].astype(jnp.float32)).astype(jnp.bfloat16)
    expanded = jnp.einsum(
        "ack,akd->cd", picked, adapter_up, preferred_element_type=jnp.float32
    ).astype(jnp.bfloat16)
    returned = lax.all_to_all(expanded, "tensor", split_axis=1, concat_axis=0, tiled=True)
    delta_out = returned[target]
    return (base_out + delta_out.astype(jnp.float32)).astype(jnp.bfloat16)


def shards(*arrays):
    if lax.axis_size("tensor") == 16 and arrays[2].shape[0] == 1:
        return staged(*arrays)
    return general(*arrays)


def solution(mesh):
    placed = (
        P("groups", "tensor"),
        P("tensor", None),
        P(("groups", "tensor"), None, None),
        P(("groups", "tensor"), None, None),
        P("groups"),
        P("groups"),
    )
    return jax.shard_map(
        shards, mesh=mesh, in_specs=placed, out_specs=P("groups", "tensor"), check_vma=False
    )
```

```python
import functools

import jax
import jax.numpy as jnp
from jax import lax
from jax.experimental import pallas as pl
from jax.experimental.pallas import tpu as pltpu
from jax.sharding import PartitionSpec as P

CAP = 32
IN_VMEM = pl.BlockSpec(memory_space=pltpu.VMEM)
IN_HBM = pl.BlockSpec(memory_space=pltpu.HBM)
ANYWHERE = pl.BlockSpec(memory_space=pl.ANY)
DMA = pltpu.SemaphoreType.DMA


def params(mib):
    return pltpu.CompilerParams(vmem_limit_bytes=mib * 1024 * 1024)


def cost(flops, moved):
    return pl.CostEstimate(flops=flops, bytes_accessed=moved, transcendentals=0)


def shape(dims, dtype=jnp.bfloat16):
    return jax.ShapeDtypeStruct(dims, dtype)


def dot(a, b):
    return jnp.dot(a, b, preferred_element_type=jnp.float32)


def swap(value, mask):
    count = lax.axis_size("tensor")
    return lax.ppermute(value, "tensor", [(t, t ^ mask) for t in range(count)])


def once_kernel(*refs):
    pass


def once(values, *after):
    return pl.pallas_call(
        once_kernel,
        out_shape=[shape(value.shape, value.dtype) for value in values],
        in_specs=[ANYWHERE] * (len(values) + len(after)),
        out_specs=[ANYWHERE] * len(values),
        input_output_aliases={i: i for i in range(len(values))},
        compiler_params=params(1),
        cost_estimate=cost(0, 0),
        name="once",
    )(*values, *after)


def columns_kernel(down_hbm, other_hbm, out_ref, sems):
    me = lax.axis_index("tensor")
    rank = out_ref.shape[0] // 2
    layers = lax.axis_size("tensor") // 4
    width = out_ref.shape[1] // layers
    fetches = []
    for i, source in enumerate((down_hbm, other_hbm)):
        for k in range(layers):
            start = pl.multiple_of((me ^ 2 ^ (4 * k)) * width, width)
            fetches.append(
                pltpu.make_async_copy(
                    source.at[:, pl.ds(start, width)],
                    out_ref.at[pl.ds(i * rank, rank), pl.ds(k * width, width)],
                    sems.at[i * layers + k],
                )
            )
    for fetch in fetches:
        fetch.start()
    for fetch in fetches:
        fetch.wait()


def columns(down, other):
    rank, depth = down.shape
    return pl.pallas_call(
        columns_kernel,
        out_shape=shape((2 * rank, depth // 4)),
        in_specs=[ANYWHERE, ANYWHERE],
        out_specs=IN_VMEM,
        scratch_shapes=[DMA((2 * (lax.axis_size("tensor") // 4),))],
        compiler_params=params(8),
        cost_estimate=cost(0, 2 * down.size),
        name="columns",
    )(down, other)


def route_kernel(count, slot_hbm, row_ref, own_ref, *rest):
    layers = count // 4
    target_ref, out_refs = rest[-3 - layers], rest[-2 - layers : -2]
    slot_ref, slot_sem = rest[-2:]
    rows = own_ref.shape[0]
    me = lax.axis_index("tensor")
    fetch = pltpu.make_async_copy(slot_hbm, slot_ref, slot_sem)
    fetch.start()
    fetch.wait()
    ids = row_ref[...]
    owner = jnp.zeros_like(ids)
    for a in range(slot_ref.shape[0]):
        owner = jnp.where(ids == a, slot_ref[a], owner)
    hot = (lax.broadcasted_iota(jnp.int32, (count, rows), 0) == owner).astype(jnp.float32)
    earlier = (
        lax.broadcasted_iota(jnp.int32, (rows, rows), 0)
        < lax.broadcasted_iota(jnp.int32, (rows, rows), 1)
    ).astype(jnp.bfloat16)
    ahead = dot(hot.astype(jnp.bfloat16), earlier)
    place = jnp.sum(ahead * hot, axis=0, keepdims=True).astype(jnp.int32)
    target = owner * CAP + place
    target_ref[...] = target
    j = lax.broadcasted_iota(jnp.int32, (4 * CAP, rows), 0)
    for k in range(layers):
        slots = (me ^ (4 * k) ^ (j // CAP)) * CAP + j % CAP
        select = (slots == target).astype(jnp.bfloat16)
        out_refs[k][...] = dot(select, own_ref[...]).astype(jnp.bfloat16)


def route(adapter_slot, row_adapter, own, *after):
    rows, width = own.shape
    count = lax.axis_size("tensor")
    layers = count // 4
    found = pl.pallas_call(
        functools.partial(route_kernel, count),
        out_shape=[shape((1, rows), jnp.int32)] + [shape((4 * CAP, width))] * layers,
        in_specs=[IN_HBM] + [IN_VMEM] * 2 + [ANYWHERE] * len(after),
        out_specs=[IN_VMEM] * (layers + 1),
        scratch_shapes=[pltpu.SMEM(adapter_slot.shape, jnp.int32), DMA(())],
        compiler_params=params(16),
        cost_estimate=cost(8 * layers * CAP * rows * width, 16 * layers * CAP * width),
        name="route",
    )(adapter_slot, row_adapter[None, :], own, *after)
    return found[0], found[1:]


def product_kernel(chips, attended_hbm, weight_hbm, *refs):
    away_ref, stay_ref, token_ref, attended_ref, weight_ref, sems = refs[-6:]
    width = weight_ref.shape[2] // 2
    me = lax.axis_index("tensor")
    core, chip = me % 2, me // 2
    fetches = [pltpu.make_async_copy(attended_hbm, attended_ref, sems.at[len(chips)])]
    for i, m in enumerate(chips):
        start = pl.multiple_of((chip ^ m) * 2 * width, 2 * width)
        fetches.append(
            pltpu.make_async_copy(weight_hbm.at[:, pl.ds(start, 2 * width)], weight_ref.at[i], sems.at[i])
        )
    for fetch in fetches:
        fetch.start()
    token_ref[...] = jnp.zeros(token_ref.shape, token_ref.dtype)
    fetches[0].wait()
    there = pl.ds(pl.multiple_of((1 - core) * width, width), width)
    here = pl.ds(pl.multiple_of(core * width, width), width)
    for i in range(len(chips)):
        fetches[i + 1].wait()
        away_ref[i] = dot(attended_ref[...], weight_ref[i, :, there]).astype(jnp.bfloat16)
        stay_ref[i] = dot(attended_ref[...], weight_ref[i, :, here])


def product(attended, out_weight, chips, mib, *after):
    rows, depth = attended.shape
    width = out_weight.shape[1] // lax.axis_size("tensor")
    n = len(chips)
    return pl.pallas_call(
        functools.partial(product_kernel, chips),
        out_shape=(
            shape((n, rows, width)),
            shape((n, rows, width), jnp.float32),
            shape((8, 128), jnp.float32),
        ),
        in_specs=[IN_HBM, IN_HBM] + [ANYWHERE] * len(after),
        out_specs=[IN_VMEM] * 3,
        scratch_shapes=[
            pltpu.VMEM((rows, depth), jnp.bfloat16),
            pltpu.VMEM((n, depth, 2 * width), jnp.bfloat16),
            DMA((n + 1,)),
        ],
        compiler_params=params(mib),
        cost_estimate=cost(4 * n * rows * depth * width, n * (4 * depth * width + 6 * rows * width)),
        name="product",
    )(attended, out_weight, *after)


def shrink_kernel(distances, down_ref, other_ref, across_ref, *refs):
    arrived_refs, out_refs = refs[: len(distances)], refs[-2:]
    me = lax.axis_index("tensor")
    rank = down_ref.shape[0]
    width = arrived_refs[0].shape[1]
    over = (((1,), (1,)), ((), ()))
    for owner in range(4):
        total = jnp.zeros((CAP, rank), jnp.float32)
        for k, arrived_ref in zip(distances, arrived_refs):
            if owner < 2:
                block = pl.ds(pl.multiple_of((me ^ (4 * k)) * width, width), width)
                weights = (down_ref, other_ref)[owner][:, block]
            else:
                weights = across_ref[(owner - 2) * rank : (owner - 1) * rank, k * width : (k + 1) * width]
            total += lax.dot_general(
                arrived_ref[owner * CAP : (owner + 1) * CAP, :],
                weights,
                over,
                preferred_element_type=jnp.float32,
            )
        out_refs[owner // 2][owner % 2 * CAP : (owner % 2 + 1) * CAP, :] = total


def shrink(down, other, across, arrived, *after):
    rank = down.shape[0]
    return pl.pallas_call(
        functools.partial(shrink_kernel, tuple(arrived)),
        out_shape=[shape((2 * CAP, rank), jnp.float32)] * 2,
        in_specs=[IN_VMEM] * (3 + len(arrived)) + [ANYWHERE] * len(after),
        out_specs=[IN_VMEM] * 2,
        compiler_params=params(16),
        cost_estimate=cost(40 * 10**9, 4 * down.size),
        name="shrink",
    )(down, other, across, *arrived.values(), *after)


def grow_kernel(groups, mine_ref, other_ref, up_ref, up_other_ref, *refs):
    out_refs = refs[-len(groups) :]
    me = lax.axis_index("tensor")
    own = (mine_ref[:CAP, :] + other_ref[CAP:, :]).astype(jnp.bfloat16)
    others = (mine_ref[CAP:, :] + other_ref[:CAP, :]).astype(jnp.bfloat16)
    for masks, out_ref in zip(groups, out_refs):
        width = out_ref.shape[2]
        for i, mask in enumerate(masks):
            block = pl.ds(pl.multiple_of((me ^ mask) * width, width), width)
            out_ref[i, :CAP, :] = dot(own, up_ref[:, block]).astype(jnp.bfloat16)
            out_ref[i, CAP:, :] = dot(others, up_other_ref[:, block]).astype(jnp.bfloat16)


def grow(mine, other, up, up_other, groups, *after):
    width = up.shape[1] // lax.axis_size("tensor")
    return pl.pallas_call(
        functools.partial(grow_kernel, groups),
        out_shape=[shape((len(masks), 2 * CAP, width)) for masks in groups],
        in_specs=[IN_VMEM] * 4 + [ANYWHERE] * len(after),
        out_specs=[IN_VMEM] * len(groups),
        compiler_params=params(16),
        cost_estimate=cost(4 * 10**9, 4 * up.size),
        name="grow",
    )(mine, other, up, up_other, *after)


def join_kernel(terms, target_ref, *refs):
    out_refs = refs[-len(terms) :]
    rows = target_ref.shape[1]
    me = lax.axis_index("tensor")
    j = lax.broadcasted_iota(jnp.int32, (2 * CAP, rows), 0)
    picks = {}
    for (blocks, grown), out_ref in zip(terms, out_refs):
        total = jnp.zeros(out_ref.shape, jnp.float32)
        for at, i in blocks:
            total += refs[at][i].astype(jnp.float32)
        for at, i, mask in grown:
            if mask not in picks:
                slots = (me ^ mask ^ (j // CAP)) * CAP + j % CAP
                picks[mask] = (slots == target_ref[...]).astype(jnp.bfloat16)
            total += lax.dot_general(
                picks[mask], refs[at][i], (((0,), (0,)), ((), ())), preferred_element_type=jnp.float32
            )
        out_ref[...] = total.astype(out_ref.dtype)


def join(target, operands, terms, dtype):
    rows, width = target.shape[1], operands[0].shape[2]
    n = len(terms)
    return pl.pallas_call(
        functools.partial(join_kernel, terms),
        out_shape=[shape((rows, width), dtype)] * n,
        in_specs=[IN_VMEM] * (1 + len(operands)),
        out_specs=[IN_VMEM] * n,
        compiler_params=params(24),
        cost_estimate=cost(4 * n * CAP * rows * width, 10 * n * rows * width),
        name="join",
    )(target, *operands)


def gather_kernel(side_ref, y_ref, z_ref, out_ref):
    out_ref[...] = side_ref[...] + y_ref[...].astype(jnp.float32) + z_ref[...].astype(jnp.float32)


def gather(side, y, z):
    return pl.pallas_call(
        gather_kernel,
        out_shape=shape(side.shape, jnp.float32),
        in_specs=[IN_VMEM] * 3,
        out_specs=IN_VMEM,
        compiler_params=params(16),
        cost_estimate=cost(2 * side.size, 12 * side.size),
        name="gather",
    )(side, y, z)


def staged(attended, out_weight, adapter_down, adapter_up, row_adapter, adapter_slot):
    f32, bf16 = jnp.float32, jnp.bfloat16
    up, down = adapter_up[0], jnp.swapaxes(adapter_down, 1, 2)[0]
    down_other, up_other = swap(down, 1), swap(up, 1)
    firsts, chips = (7, 6, 5), (4, 3, 2, 1, 0)
    away_first, stay_first, token = product(attended, out_weight, firsts, 44)
    to_y = columns(down, down_other)
    across = swap(to_y, 2)
    target, outgoing = route(adapter_slot, row_adapter, attended, token, to_y, up_other)
    came_first = swap(away_first, 1)
    arrived = {k: swap(outgoing[k], 4 * k) for k in (2, 3, 1)}
    arrived[0] = outgoing[0]
    away, stay, _ = product(attended, out_weight, chips, 44, target)
    came = swap(away, 1)
    first = [stay_first[i] + came_first[i].astype(f32) for i in range(3)]
    y3, y2 = swap(first[0].astype(bf16), 2), swap(first[2].astype(bf16), 2)[None]
    z3 = swap((first[1] + y3.astype(f32)).astype(bf16), 4)[None]
    mine, theirs = shrink(down, down_other, across, arrived)
    mine = mine + swap(theirs, 2)
    here_chips = (4, 3, 2, 1, 0)
    groups = (tuple(2 * m for m in here_chips), (10,), (12,), (14,))
    here, over2, over4, over6 = grow(mine, swap(mine, 1), up, up_other, groups, y3, came)
    over2, over4, over6 = swap(over2, 2), swap(over4, 4), swap(over6, 6)

    def blocks(m):
        return ((0, chips.index(m)), (1, chips.index(m))), ((2, here_chips.index(m), 0),)

    (ready2,) = join(target, [stay, came, z3, y2], ((((0, 0), (1, 0), (2, 0), (3, 0)), ()),), f32)
    (go1,) = join(target, [stay, came, here, over2, over4, over6, ready2], (blocks(3),), bf16)
    y1 = swap(go1, 2)
    (sum2,) = join(
        target,
        [ready2[None], here, over2, over4, over6],
        ((((0, 0),), ((1, here_chips.index(4), 0), (2, 0, 2), (3, 0, 4), (4, 0, 6))),),
        bf16,
    )
    z2 = swap(sum2, 8)
    (go0,) = join(target, [stay, came, here, sum2], (blocks(1),), bf16)
    y0 = swap(go0, 2)
    sums, grown = blocks(2)
    (sum1,) = join(target, [stay, came, here, y1[None], sum2], ((sums + ((3, 0),), grown),), bf16)
    z1 = swap(sum1, 4)
    (side0,) = join(target, [stay, came, here], (blocks(0),), f32)
    total = gather(side0, y0, z2) + z1.astype(f32)
    return total.astype(bf16)


def general(attended, out_weight, adapter_down, adapter_up, row_adapter, adapter_slot):
    tensor_size = lax.axis_size("tensor")
    device = lax.axis_index("tensor")
    row_count = attended.shape[0]
    held_count = adapter_down.shape[0]
    storage = adapter_slot[row_adapter]
    partial_value = jnp.dot(attended, out_weight, preferred_element_type=jnp.float32)
    base_out = lax.psum_scatter(partial_value, "tensor", scatter_dimension=1, tiled=True)
    owner_of = storage // held_count
    local_index = storage % held_count
    owner_hot = (owner_of[:, None] == jnp.arange(tensor_size, dtype=jnp.int32)[None, :]).astype(
        jnp.int32
    )
    position = jnp.sum(jnp.cumsum(owner_hot, axis=0) * owner_hot, axis=1) - 1
    target = owner_of * CAP + position
    slot_row = (
        jnp.full((tensor_size * CAP,), row_count, jnp.int32)
        .at[target]
        .set(jnp.arange(row_count, dtype=jnp.int32))
    )
    padded = jnp.concatenate([attended, jnp.zeros((1, attended.shape[1]), attended.dtype)], axis=0)
    outgoing = padded[slot_row]
    arrived = lax.all_to_all(outgoing, "tensor", split_axis=0, concat_axis=1, tiled=True)
    own_slots = lax.dynamic_slice_in_dim(slot_row, device * CAP, CAP)
    slot_local = jnp.concatenate([local_index, jnp.zeros((1,), jnp.int32)])[own_slots]
    selector = (slot_local[None, :] == jnp.arange(held_count, dtype=jnp.int32)[:, None]).astype(
        jnp.float32
    )
    all_shrunk = jnp.einsum(
        "cd,adk->ack", arrived, adapter_down, preferred_element_type=jnp.float32
    )
    shrunk = jnp.sum(all_shrunk * selector[:, :, None], axis=0).astype(jnp.bfloat16)
    picked = (selector[:, :, None] * shrunk[None].astype(jnp.float32)).astype(jnp.bfloat16)
    expanded = jnp.einsum(
        "ack,akd->cd", picked, adapter_up, preferred_element_type=jnp.float32
    ).astype(jnp.bfloat16)
    returned = lax.all_to_all(expanded, "tensor", split_axis=1, concat_axis=0, tiled=True)
    delta_out = returned[target]
    return (base_out + delta_out.astype(jnp.float32)).astype(jnp.bfloat16)


def shards(*arrays):
    if lax.axis_size("tensor") == 16 and arrays[2].shape[0] == 1:
        return staged(*arrays)
    return general(*arrays)


def solution(mesh):
    placed = (
        P("groups", "tensor"),
        P("tensor", None),
        P(("groups", "tensor"), None, None),
        P(("groups", "tensor"), None, None),
        P("groups"),
        P("groups"),
    )
    return jax.shard_map(
        shards, mesh=mesh, in_specs=placed, out_specs=P("groups", "tensor"), check_vma=False
    )
```

```python
import functools

import jax
import jax.numpy as jnp
from jax import lax
from jax.experimental import pallas as pl
from jax.experimental.pallas import tpu as pltpu
from jax.sharding import PartitionSpec as P

CAP = 32
IN_VMEM = pl.BlockSpec(memory_space=pltpu.VMEM)
IN_HBM = pl.BlockSpec(memory_space=pltpu.HBM)
ANYWHERE = pl.BlockSpec(memory_space=pl.ANY)
DMA = pltpu.SemaphoreType.DMA


def params(mib):
    return pltpu.CompilerParams(vmem_limit_bytes=mib * 1024 * 1024)


def cost(flops, moved):
    return pl.CostEstimate(flops=flops, bytes_accessed=moved, transcendentals=0)


def shape(dims, dtype=jnp.bfloat16):
    return jax.ShapeDtypeStruct(dims, dtype)


def dot(a, b):
    return jnp.dot(a, b, preferred_element_type=jnp.float32)


def swap(value, mask):
    count = lax.axis_size("tensor")
    return lax.ppermute(value, "tensor", [(t, t ^ mask) for t in range(count)])


def once_kernel(*refs):
    pass


def once(values, *after):
    return pl.pallas_call(
        once_kernel,
        out_shape=[shape(value.shape, value.dtype) for value in values],
        in_specs=[ANYWHERE] * (len(values) + len(after)),
        out_specs=[ANYWHERE] * len(values),
        input_output_aliases={i: i for i in range(len(values))},
        compiler_params=params(1),
        cost_estimate=cost(0, 0),
        name="once",
    )(*values, *after)


def route_kernel(count, layers, slot_hbm, row_ref, own_ref, y_ref, *rest):
    target_ref, out_refs = rest[-3 - layers], rest[-2 - layers : -2]
    slot_ref, slot_sem = rest[-2:]
    rows, width = own_ref.shape
    me = lax.axis_index("tensor")
    fetch = pltpu.make_async_copy(slot_hbm, slot_ref, slot_sem)
    fetch.start()
    fetch.wait()
    ids = row_ref[...]
    owner = jnp.zeros_like(ids)
    for a in range(slot_ref.shape[0]):
        owner = jnp.where(ids == a, slot_ref[a], owner)
    hot = (lax.broadcasted_iota(jnp.int32, (count, rows), 0) == owner).astype(jnp.float32)
    earlier = (
        lax.broadcasted_iota(jnp.int32, (rows, rows), 0)
        < lax.broadcasted_iota(jnp.int32, (rows, rows), 1)
    ).astype(jnp.bfloat16)
    ahead = dot(hot.astype(jnp.bfloat16), earlier)
    place = jnp.sum(ahead * hot, axis=0, keepdims=True).astype(jnp.int32)
    target = owner * CAP + place
    target_ref[...] = target
    j = lax.broadcasted_iota(jnp.int32, (2 * CAP, rows), 0)
    for k in range(layers):
        slots = (me ^ (4 * k) ^ (j // CAP)) * CAP + j % CAP
        select = (slots == target).astype(jnp.bfloat16)
        out_refs[k][:, :width] = dot(select, own_ref[...]).astype(jnp.bfloat16)
        out_refs[k][:, width:] = dot(select, y_ref[...]).astype(jnp.bfloat16)


def route(adapter_slot, row_adapter, own, y, *after):
    rows, width = own.shape
    count = lax.axis_size("tensor")
    layers = count // 4
    found = pl.pallas_call(
        functools.partial(route_kernel, count, layers),
        out_shape=[shape((1, rows), jnp.int32)] + [shape((2 * CAP, 2 * width))] * layers,
        in_specs=[IN_HBM] + [IN_VMEM] * 3 + [ANYWHERE] * len(after),
        out_specs=[IN_VMEM] * (layers + 1),
        scratch_shapes=[pltpu.SMEM(adapter_slot.shape, jnp.int32), DMA(())],
        compiler_params=params(16),
        cost_estimate=cost(8 * layers * CAP * rows * width, 16 * layers * CAP * width),
        name="route",
    )(adapter_slot, row_adapter[None, :], own, y, *after)
    return found[0], found[1:]


def product_kernel(chips, attended_hbm, weight_hbm, *refs):
    away_ref, stay_ref, token_ref, attended_ref, weight_ref, sems = refs[-6:]
    width = weight_ref.shape[2] // 2
    me = lax.axis_index("tensor")
    core, chip = me % 2, me // 2
    fetches = [pltpu.make_async_copy(attended_hbm, attended_ref, sems.at[len(chips)])]
    for i, m in enumerate(chips):
        start = pl.multiple_of((chip ^ m) * 2 * width, 2 * width)
        fetches.append(
            pltpu.make_async_copy(weight_hbm.at[:, pl.ds(start, 2 * width)], weight_ref.at[i], sems.at[i])
        )
    for fetch in fetches:
        fetch.start()
    token_ref[...] = jnp.zeros(token_ref.shape, token_ref.dtype)
    fetches[0].wait()
    there = pl.ds(pl.multiple_of((1 - core) * width, width), width)
    here = pl.ds(pl.multiple_of(core * width, width), width)
    for i in range(len(chips)):
        fetches[i + 1].wait()
        away_ref[i] = dot(attended_ref[...], weight_ref[i, :, there]).astype(jnp.bfloat16)
        stay_ref[i] = dot(attended_ref[...], weight_ref[i, :, here])


def product(attended, out_weight, chips, mib, *after):
    rows, depth = attended.shape
    width = out_weight.shape[1] // lax.axis_size("tensor")
    n = len(chips)
    return pl.pallas_call(
        functools.partial(product_kernel, chips),
        out_shape=(
            shape((n, rows, width)),
            shape((n, rows, width), jnp.float32),
            shape((8, 128), jnp.float32),
        ),
        in_specs=[IN_HBM, IN_HBM] + [ANYWHERE] * len(after),
        out_specs=[IN_VMEM] * 3,
        scratch_shapes=[
            pltpu.VMEM((rows, depth), jnp.bfloat16),
            pltpu.VMEM((n, depth, 2 * width), jnp.bfloat16),
            DMA((n + 1,)),
        ],
        compiler_params=params(mib),
        cost_estimate=cost(4 * n * rows * depth * width, n * (4 * depth * width + 6 * rows * width)),
        name="product",
    )(attended, out_weight, *after)


def shrink_kernel(distances, down_ref, other_ref, *refs):
    arrived_refs, out_ref = refs[: len(distances)], refs[-1]
    me = lax.axis_index("tensor")
    width = arrived_refs[0].shape[1] // 2
    over = (((1,), (1,)), ((), ()))
    for part, weights_ref in enumerate((down_ref, other_ref)):
        total = jnp.zeros((CAP, down_ref.shape[0]), jnp.float32)
        for k, arrived_ref in zip(distances, arrived_refs):
            for side in range(2):
                block = pl.ds(pl.multiple_of((me ^ (4 * k + 2 * side)) * width, width), width)
                total += lax.dot_general(
                    arrived_ref[part * CAP : (part + 1) * CAP, side * width : (side + 1) * width],
                    weights_ref[:, block],
                    over,
                    preferred_element_type=jnp.float32,
                )
        out_ref[part * CAP : (part + 1) * CAP, :] = total


def shrink(down, other, arrived, *after):
    return pl.pallas_call(
        functools.partial(shrink_kernel, tuple(arrived)),
        out_shape=shape((2 * CAP, down.shape[0]), jnp.float32),
        in_specs=[IN_VMEM] * (2 + len(arrived)) + [ANYWHERE] * len(after),
        out_specs=IN_VMEM,
        compiler_params=params(16),
        cost_estimate=cost(40*10**9, 4 * down.size),
        name="shrink",
    )(down, other, *arrived.values(), *after)


def grow_kernel(groups, mine_ref, other_ref, up_ref, up_other_ref, *refs):
    out_refs = refs[-len(groups) :]
    me = lax.axis_index("tensor")
    own = (mine_ref[:CAP, :] + other_ref[CAP:, :]).astype(jnp.bfloat16)
    others = (mine_ref[CAP:, :] + other_ref[:CAP, :]).astype(jnp.bfloat16)
    for masks, out_ref in zip(groups, out_refs):
        width = out_ref.shape[2]
        for i, mask in enumerate(masks):
            block = pl.ds(pl.multiple_of((me ^ mask) * width, width), width)
            out_ref[i, :CAP, :] = dot(own, up_ref[:, block]).astype(jnp.bfloat16)
            out_ref[i, CAP:, :] = dot(others, up_other_ref[:, block]).astype(jnp.bfloat16)


def grow(mine, other, up, up_other, groups, *after):
    width = up.shape[1] // lax.axis_size("tensor")
    return pl.pallas_call(
        functools.partial(grow_kernel, groups),
        out_shape=[shape((len(masks), 2 * CAP, width)) for masks in groups],
        in_specs=[IN_VMEM] * 4 + [ANYWHERE] * len(after),
        out_specs=[IN_VMEM] * len(groups),
        compiler_params=params(16),
        cost_estimate=cost(4 * 10**9, 4 * up.size),
        name="grow",
    )(mine, other, up, up_other, *after)


def join_kernel(terms, target_ref, *refs):
    out_refs = refs[-len(terms) :]
    rows = target_ref.shape[1]
    me = lax.axis_index("tensor")
    j = lax.broadcasted_iota(jnp.int32, (2 * CAP, rows), 0)
    picks = {}
    for (blocks, grown), out_ref in zip(terms, out_refs):
        total = jnp.zeros(out_ref.shape, jnp.float32)
        for at, i in blocks:
            total += refs[at][i].astype(jnp.float32)
        for at, i, mask in grown:
            if mask not in picks:
                slots = (me ^ mask ^ (j // CAP)) * CAP + j % CAP
                picks[mask] = (slots == target_ref[...]).astype(jnp.bfloat16)
            total += lax.dot_general(
                picks[mask], refs[at][i], (((0,), (0,)), ((), ())), preferred_element_type=jnp.float32
            )
        out_ref[...] = total.astype(out_ref.dtype)


def join(target, operands, terms, dtype):
    rows, width = target.shape[1], operands[0].shape[2]
    n = len(terms)
    return pl.pallas_call(
        functools.partial(join_kernel, terms),
        out_shape=[shape((rows, width), dtype)] * n,
        in_specs=[IN_VMEM] * (1 + len(operands)),
        out_specs=[IN_VMEM] * n,
        compiler_params=params(24),
        cost_estimate=cost(4 * n * CAP * rows * width, 10 * n * rows * width),
        name="join",
    )(target, *operands)


def gather_kernel(sum_ref, came_ref, out_ref):
    out_ref[...] = sum_ref[...] + came_ref[...].astype(jnp.float32)


def gather(total, came):
    return pl.pallas_call(
        gather_kernel,
        out_shape=shape(total.shape, jnp.float32),
        in_specs=[IN_VMEM] * 2,
        out_specs=IN_VMEM,
        compiler_params=params(16),
        cost_estimate=cost(total.size, 10 * total.size),
        name="gather",
    )(total, came)


def staged(attended, out_weight, adapter_down, adapter_up, row_adapter, adapter_slot):
    f32, bf16 = jnp.float32, jnp.bfloat16
    up, down = adapter_up[0], jnp.swapaxes(adapter_down, 1, 2)[0]
    from_y = swap(attended, 2)
    down_other, up_other = swap(down, 1), swap(up, 1)
    firsts, chips = (7, 6, 5), (4, 3, 2, 1, 0)
    away_first, stay_first, token = product(attended, out_weight, firsts, 44)
    came_first = swap(away_first, 1)
    first = [stay_first[i] + came_first[i].astype(f32) for i in range(3)]
    go3, go2 = first[0].astype(bf16), first[2].astype(bf16)
    target, outgoing = route(adapter_slot, row_adapter, attended, from_y, token, down_other, up_other)
    arrived = {k: swap(outgoing[k], 4 * k) for k in (2, 3, 1)}
    arrived[0] = outgoing[0]
    y3, y2 = swap(go3, 2), swap(go2, 2)[None]
    z3 = swap((first[1] + y3.astype(f32)).astype(bf16), 4)[None]
    away, stay, _ = product(attended, out_weight, chips, 44, target)
    came = swap(away, 1)

    def base(m):
        return stay[chips.index(m)] + came[chips.index(m)].astype(f32)

    y1, y0 = swap(base(3).astype(bf16), 2), swap(base(1).astype(bf16), 2)
    mine = shrink(down, down_other, arrived)
    groups = ((8, 0), (10, 2), (12, 4), (14, 6))
    here, over2, over4, over6 = grow(mine, swap(mine, 1), up, up_other, groups, y2, came)
    over2, over4, over6 = swap(over2, 2), swap(over4, 4), swap(over6, 6)
    (ready2,) = join(target, [stay, came, z3, y2], ((((0, 0), (1, 0), (2, 0), (3, 0)), ()),), f32)
    grown = [here, over2, over4, over6]
    (sum2,) = join(
        target, [ready2[None]] + grown, ((((0, 0),), tuple((1 + i, 0, 2 * i) for i in range(4))),), bf16
    )
    z2 = swap(sum2, 8)
    (side0,) = join(
        target,
        [stay, came, sum2] + grown,
        ((((0, 4), (1, 4)), tuple((3 + i, 1, 2 * i) for i in range(4))),),
        f32,
    )
    z1 = swap((base(2) + y1.astype(f32)).astype(bf16), 4)
    total = gather(side0, z2) + y0.astype(f32) + z1.astype(f32)
    return total.astype(bf16)


def general(attended, out_weight, adapter_down, adapter_up, row_adapter, adapter_slot):
    tensor_size = lax.axis_size("tensor")
    device = lax.axis_index("tensor")
    row_count = attended.shape[0]
    held_count = adapter_down.shape[0]
    storage = adapter_slot[row_adapter]
    partial_value = jnp.dot(attended, out_weight, preferred_element_type=jnp.float32)
    base_out = lax.psum_scatter(partial_value, "tensor", scatter_dimension=1, tiled=True)
    owner_of = storage // held_count
    local_index = storage % held_count
    owner_hot = (owner_of[:, None] == jnp.arange(tensor_size, dtype=jnp.int32)[None, :]).astype(
        jnp.int32
    )
    position = jnp.sum(jnp.cumsum(owner_hot, axis=0) * owner_hot, axis=1) - 1
    target = owner_of * CAP + position
    slot_row = (
        jnp.full((tensor_size * CAP,), row_count, jnp.int32)
        .at[target]
        .set(jnp.arange(row_count, dtype=jnp.int32))
    )
    padded = jnp.concatenate([attended, jnp.zeros((1, attended.shape[1]), attended.dtype)], axis=0)
    outgoing = padded[slot_row]
    arrived = lax.all_to_all(outgoing, "tensor", split_axis=0, concat_axis=1, tiled=True)
    own_slots = lax.dynamic_slice_in_dim(slot_row, device * CAP, CAP)
    slot_local = jnp.concatenate([local_index, jnp.zeros((1,), jnp.int32)])[own_slots]
    selector = (slot_local[None, :] == jnp.arange(held_count, dtype=jnp.int32)[:, None]).astype(
        jnp.float32
    )
    all_shrunk = jnp.einsum(
        "cd,adk->ack", arrived, adapter_down, preferred_element_type=jnp.float32
    )
    shrunk = jnp.sum(all_shrunk * selector[:, :, None], axis=0).astype(jnp.bfloat16)
    picked = (selector[:, :, None] * shrunk[None].astype(jnp.float32)).astype(jnp.bfloat16)
    expanded = jnp.einsum(
        "ack,akd->cd", picked, adapter_up, preferred_element_type=jnp.float32
    ).astype(jnp.bfloat16)
    returned = lax.all_to_all(expanded, "tensor", split_axis=1, concat_axis=0, tiled=True)
    delta_out = returned[target]
    return (base_out + delta_out.astype(jnp.float32)).astype(jnp.bfloat16)


def shards(*arrays):
    if lax.axis_size("tensor") == 16 and arrays[2].shape[0] == 1:
        return staged(*arrays)
    return general(*arrays)


def solution(mesh):
    placed = (
        P("groups", "tensor"),
        P("tensor", None),
        P(("groups", "tensor"), None, None),
        P(("groups", "tensor"), None, None),
        P("groups"),
        P("groups"),
    )
    return jax.shard_map(
        shards, mesh=mesh, in_specs=placed, out_specs=P("groups", "tensor"), check_vma=False
    )
```

```python
import functools

import jax
import jax.numpy as jnp
from jax import lax
from jax.experimental import pallas as pl
from jax.experimental.pallas import tpu as pltpu
from jax.sharding import PartitionSpec as P

CAP = 32
IN_VMEM = pl.BlockSpec(memory_space=pltpu.VMEM)
IN_HBM = pl.BlockSpec(memory_space=pltpu.HBM)
ANYWHERE = pl.BlockSpec(memory_space=pl.ANY)
DMA = pltpu.SemaphoreType.DMA


def params(mib):
    return pltpu.CompilerParams(vmem_limit_bytes=mib * 1024 * 1024)


def cost(flops, moved):
    return pl.CostEstimate(flops=flops, bytes_accessed=moved, transcendentals=0)


def shape(dims, dtype=jnp.bfloat16):
    return jax.ShapeDtypeStruct(dims, dtype)


def dot(a, b):
    return jnp.dot(a, b, preferred_element_type=jnp.float32)


def swap(value, mask):
    count = lax.axis_size("tensor")
    return lax.ppermute(value, "tensor", [(t, t ^ mask) for t in range(count)])


def once_kernel(*refs):
    pass


def once(values, *after):
    return pl.pallas_call(
        once_kernel,
        out_shape=[shape(value.shape, value.dtype) for value in values],
        in_specs=[ANYWHERE] * (len(values) + len(after)),
        out_specs=[ANYWHERE] * len(values),
        input_output_aliases={i: i for i in range(len(values))},
        compiler_params=params(1),
        cost_estimate=cost(0, 0),
        name="once",
    )(*values, *after)


def route_kernel(count, layers, slot_hbm, row_ref, own_ref, y_ref, *rest):
    target_ref, out_refs = rest[-3 - layers], rest[-2 - layers : -2]
    slot_ref, slot_sem = rest[-2:]
    rows, width = own_ref.shape
    me = lax.axis_index("tensor")
    fetch = pltpu.make_async_copy(slot_hbm, slot_ref, slot_sem)
    fetch.start()
    fetch.wait()
    ids = row_ref[...]
    owner = jnp.zeros_like(ids)
    for a in range(slot_ref.shape[0]):
        owner = jnp.where(ids == a, slot_ref[a], owner)
    hot = (lax.broadcasted_iota(jnp.int32, (count, rows), 0) == owner).astype(jnp.float32)
    earlier = (
        lax.broadcasted_iota(jnp.int32, (rows, rows), 0)
        < lax.broadcasted_iota(jnp.int32, (rows, rows), 1)
    ).astype(jnp.bfloat16)
    ahead = dot(hot.astype(jnp.bfloat16), earlier)
    place = jnp.sum(ahead * hot, axis=0, keepdims=True).astype(jnp.int32)
    target = owner * CAP + place
    target_ref[...] = target
    j = lax.broadcasted_iota(jnp.int32, (2 * CAP, rows), 0)
    for k in range(layers):
        slots = (me ^ (4 * k) ^ (j // CAP)) * CAP + j % CAP
        select = (slots == target).astype(jnp.bfloat16)
        out_refs[k][:, :width] = dot(select, own_ref[...]).astype(jnp.bfloat16)
        out_refs[k][:, width:] = dot(select, y_ref[...]).astype(jnp.bfloat16)


def route(adapter_slot, row_adapter, own, y, *after):
    rows, width = own.shape
    count = lax.axis_size("tensor")
    layers = count // 4
    found = pl.pallas_call(
        functools.partial(route_kernel, count, layers),
        out_shape=[shape((1, rows), jnp.int32)] + [shape((2 * CAP, 2 * width))] * layers,
        in_specs=[IN_HBM] + [IN_VMEM] * 3 + [ANYWHERE] * len(after),
        out_specs=[IN_VMEM] * (layers + 1),
        scratch_shapes=[pltpu.SMEM(adapter_slot.shape, jnp.int32), DMA(())],
        compiler_params=params(16),
        cost_estimate=cost(8 * layers * CAP * rows * width, 16 * layers * CAP * width),
        name="route",
    )(adapter_slot, row_adapter[None, :], own, y, *after)
    return found[0], found[1:]


def product_kernel(groups, attended_hbm, weight_hbm, *refs):
    token_ref, attended_ref, weight_ref, sems = refs[-4:]
    chips = [m for group in groups for m in group]
    width = weight_ref.shape[2] // 2
    me = lax.axis_index("tensor")
    core, chip = me % 2, me // 2
    fetches = [pltpu.make_async_copy(attended_hbm, attended_ref, sems.at[len(chips)])]
    for i, m in enumerate(chips):
        start = pl.multiple_of((chip ^ m) * 2 * width, 2 * width)
        fetches.append(
            pltpu.make_async_copy(weight_hbm.at[:, pl.ds(start, 2 * width)], weight_ref.at[i], sems.at[i])
        )
    for fetch in fetches:
        fetch.start()
    token_ref[...] = jnp.zeros(token_ref.shape, token_ref.dtype)
    fetches[0].wait()
    there = pl.ds(pl.multiple_of((1 - core) * width, width), width)
    here = pl.ds(pl.multiple_of(core * width, width), width)
    at = 0
    for g, group in enumerate(groups):
        away_ref, stay_ref = refs[2 * g : 2 * g + 2]
        for i in range(len(group)):
            fetches[at + 1].wait()
            away_ref[i] = dot(attended_ref[...], weight_ref[at, :, there]).astype(jnp.bfloat16)
            stay_ref[i] = dot(attended_ref[...], weight_ref[at, :, here])
            at += 1


def product(attended, out_weight, groups, mib):
    rows, depth = attended.shape
    width = out_weight.shape[1] // lax.axis_size("tensor")
    n = sum(len(group) for group in groups)
    out_shape = []
    for group in groups:
        out_shape.append(shape((len(group), rows, width)))
        out_shape.append(shape((len(group), rows, width), jnp.float32))
    out_shape.append(shape((8, 128), jnp.float32))
    return pl.pallas_call(
        functools.partial(product_kernel, groups),
        out_shape=out_shape,
        in_specs=[IN_HBM, IN_HBM],
        out_specs=[IN_VMEM] * len(out_shape),
        scratch_shapes=[
            pltpu.VMEM((rows, depth), jnp.bfloat16),
            pltpu.VMEM((n, depth, 2 * width), jnp.bfloat16),
            DMA((n + 1,)),
        ],
        compiler_params=params(mib),
        cost_estimate=cost(4 * n * rows * depth * width, n * (4 * depth * width + 6 * rows * width)),
        name="product",
    )(attended, out_weight)


def shrink_kernel(distances, down_ref, other_ref, *refs):
    arrived_refs, out_ref = refs[: len(distances)], refs[-1]
    me = lax.axis_index("tensor")
    width = arrived_refs[0].shape[1] // 2
    over = (((1,), (1,)), ((), ()))
    for part, weights_ref in enumerate((down_ref, other_ref)):
        total = jnp.zeros((CAP, down_ref.shape[0]), jnp.float32)
        for k, arrived_ref in zip(distances, arrived_refs):
            for side in range(2):
                block = pl.ds(pl.multiple_of((me ^ (4 * k + 2 * side)) * width, width), width)
                total += lax.dot_general(
                    arrived_ref[part * CAP : (part + 1) * CAP, side * width : (side + 1) * width],
                    weights_ref[:, block],
                    over,
                    preferred_element_type=jnp.float32,
                )
        out_ref[part * CAP : (part + 1) * CAP, :] = total


def shrink(down, other, arrived, *after):
    return pl.pallas_call(
        functools.partial(shrink_kernel, tuple(arrived)),
        out_shape=shape((2 * CAP, down.shape[0]), jnp.float32),
        in_specs=[IN_VMEM] * (2 + len(arrived)) + [ANYWHERE] * len(after),
        out_specs=IN_VMEM,
        compiler_params=params(16),
        cost_estimate=cost(40 * 10**9, 4 * down.size),
        name="shrink",
    )(down, other, *arrived.values(), *after)


def grow_kernel(groups, mine_ref, other_ref, up_ref, up_other_ref, *refs):
    out_refs = refs[-len(groups) :]
    me = lax.axis_index("tensor")
    own = (mine_ref[:CAP, :] + other_ref[CAP:, :]).astype(jnp.bfloat16)
    others = (mine_ref[CAP:, :] + other_ref[:CAP, :]).astype(jnp.bfloat16)
    for masks, out_ref in zip(groups, out_refs):
        width = out_ref.shape[2]
        for i, mask in enumerate(masks):
            block = pl.ds(pl.multiple_of((me ^ mask) * width, width), width)
            out_ref[i, :CAP, :] = dot(own, up_ref[:, block]).astype(jnp.bfloat16)
            out_ref[i, CAP:, :] = dot(others, up_other_ref[:, block]).astype(jnp.bfloat16)


def grow(mine, other, up, up_other, groups, *after):
    width = up.shape[1] // lax.axis_size("tensor")
    return pl.pallas_call(
        functools.partial(grow_kernel, groups),
        out_shape=[shape((len(masks), 2 * CAP, width)) for masks in groups],
        in_specs=[IN_VMEM] * 4 + [ANYWHERE] * len(after),
        out_specs=[IN_VMEM] * len(groups),
        compiler_params=params(16),
        cost_estimate=cost(4 * CAP * up.size, 4 * up.size),
        name="grow",
    )(mine, other, up, up_other, *after)


def join_kernel(terms, target_ref, *refs):
    out_refs = refs[-len(terms) :]
    rows = target_ref.shape[1]
    me = lax.axis_index("tensor")
    j = lax.broadcasted_iota(jnp.int32, (2 * CAP, rows), 0)
    picks = {}
    for (blocks, grown), out_ref in zip(terms, out_refs):
        total = jnp.zeros(out_ref.shape, jnp.float32)
        for at, i in blocks:
            total += refs[at][i].astype(jnp.float32)
        for at, i, mask in grown:
            if mask not in picks:
                slots = (me ^ mask ^ (j // CAP)) * CAP + j % CAP
                picks[mask] = (slots == target_ref[...]).astype(jnp.bfloat16)
            total += lax.dot_general(
                picks[mask], refs[at][i], (((0,), (0,)), ((), ())), preferred_element_type=jnp.float32
            )
        out_ref[...] = total.astype(out_ref.dtype)


def join(target, operands, terms, dtype):
    rows, width = target.shape[1], operands[0].shape[2]
    n = len(terms)
    return pl.pallas_call(
        functools.partial(join_kernel, terms),
        out_shape=[shape((rows, width), dtype)] * n,
        in_specs=[IN_VMEM] * (1 + len(operands)),
        out_specs=[IN_VMEM] * n,
        compiler_params=params(24),
        cost_estimate=cost(4 * n * CAP * rows * width, 10 * n * rows * width),
        name="join",
    )(target, *operands)


def gather_kernel(sum_ref, came_ref, out_ref):
    out_ref[...] = sum_ref[...] + came_ref[...].astype(jnp.float32)


def gather(total, came):
    return pl.pallas_call(
        gather_kernel,
        out_shape=shape(total.shape, jnp.float32),
        in_specs=[IN_VMEM] * 2,
        out_specs=IN_VMEM,
        compiler_params=params(16),
        cost_estimate=cost(total.size, 10 * total.size),
        name="gather",
    )(total, came)


def staged(attended, out_weight, adapter_down, adapter_up, row_adapter, adapter_slot):
    f32, bf16 = jnp.float32, jnp.bfloat16
    up, down = adapter_up[0], jnp.swapaxes(adapter_down, 1, 2)[0]
    from_y = swap(attended, 2)
    down_other, up_other = swap(down, 1), swap(up, 1)
    firsts, chips = (7, 6, 5), (4, 3, 2, 1, 0)
    away_first, stay_first, away, stay, token = product(attended, out_weight, (firsts, chips), 44)
    (away_first,) = once((away_first,), from_y, down_other, up_other)
    came_first = swap(away_first, 1)
    first = [stay_first[i] + came_first[i].astype(f32) for i in range(3)]
    target, outgoing = route(adapter_slot, row_adapter, attended, from_y, token)
    arrived = {k: swap(outgoing[k], 4 * k) for k in (1, 2, 3)}
    arrived[0] = outgoing[0]
    (go3,) = once((first[0].astype(bf16),), target)
    y3 = swap(go3, 2)
    (go2,) = once((first[2].astype(bf16),), arrived[1])
    y2 = swap(go2, 2)[None]
    z3 = swap((first[1] + y3.astype(f32)).astype(bf16), 4)[None]
    (away,) = once((away,), target)
    came = swap(away, 1)
    mine = shrink(down, down_other, arrived)
    groups = ((8, 6, 4, 2, 0), (10,), (12,), (14,))
    here, over2, over4, over6 = grow(mine, swap(mine, 1), up, up_other, groups, y3, came)
    over2, over4, over6 = swap(over2, 2), swap(over4, 4), swap(over6, 6)
    (ready2,) = join(target, [stay, came, z3, y2], ((((0, 0), (1, 0), (2, 0), (3, 0)), ()),), f32)
    grown = [here, over2, over4, over6]
    (sum2,) = join(
        target, [ready2[None]] + grown, ((((0, 0),), tuple((1 + i, 0, 2 * i) for i in range(4))),), bf16
    )
    z2 = swap(sum2, 8)

    def blocks(m):
        return ((0, chips.index(m)), (1, chips.index(m))), ((2, chips.index(m), 0),)

    (go1,) = join(target, [stay, came, here, sum2], (blocks(3),), bf16)
    y1 = swap(go1, 2)
    (go0,) = join(target, [stay, came, here, sum2], (blocks(1),), bf16)
    y0 = swap(go0, 2)
    sums, grown = blocks(2)
    (sum1,) = join(target, [stay, came, here, y1[None], sum2], ((sums + ((3, 0),), grown),), bf16)
    z1 = swap(sum1, 4)
    (side0,) = join(target, [stay, came, here], (blocks(0),), f32)
    total = gather(side0, z2) + y0.astype(f32) + z1.astype(f32)
    return total.astype(bf16)


def general(attended, out_weight, adapter_down, adapter_up, row_adapter, adapter_slot):
    tensor_size = lax.axis_size("tensor")
    device = lax.axis_index("tensor")
    row_count = attended.shape[0]
    held_count = adapter_down.shape[0]
    storage = adapter_slot[row_adapter]
    partial_value = jnp.dot(attended, out_weight, preferred_element_type=jnp.float32)
    base_out = lax.psum_scatter(partial_value, "tensor", scatter_dimension=1, tiled=True)
    owner_of = storage // held_count
    local_index = storage % held_count
    owner_hot = (owner_of[:, None] == jnp.arange(tensor_size, dtype=jnp.int32)[None, :]).astype(
        jnp.int32
    )
    position = jnp.sum(jnp.cumsum(owner_hot, axis=0) * owner_hot, axis=1) - 1
    target = owner_of * CAP + position
    slot_row = (
        jnp.full((tensor_size * CAP,), row_count, jnp.int32)
        .at[target]
        .set(jnp.arange(row_count, dtype=jnp.int32))
    )
    padded = jnp.concatenate([attended, jnp.zeros((1, attended.shape[1]), attended.dtype)], axis=0)
    outgoing = padded[slot_row]
    arrived = lax.all_to_all(outgoing, "tensor", split_axis=0, concat_axis=1, tiled=True)
    own_slots = lax.dynamic_slice_in_dim(slot_row, device * CAP, CAP)
    slot_local = jnp.concatenate([local_index, jnp.zeros((1,), jnp.int32)])[own_slots]
    selector = (slot_local[None, :] == jnp.arange(held_count, dtype=jnp.int32)[:, None]).astype(
        jnp.float32
    )
    all_shrunk = jnp.einsum(
        "cd,adk->ack", arrived, adapter_down, preferred_element_type=jnp.float32
    )
    shrunk = jnp.sum(all_shrunk * selector[:, :, None], axis=0).astype(jnp.bfloat16)
    picked = (selector[:, :, None] * shrunk[None].astype(jnp.float32)).astype(jnp.bfloat16)
    expanded = jnp.einsum(
        "ack,akd->cd", picked, adapter_up, preferred_element_type=jnp.float32
    ).astype(jnp.bfloat16)
    returned = lax.all_to_all(expanded, "tensor", split_axis=1, concat_axis=0, tiled=True)
    delta_out = returned[target]
    return (base_out + delta_out.astype(jnp.float32)).astype(jnp.bfloat16)


def shards(*arrays):
    if lax.axis_size("tensor") == 16 and arrays[2].shape[0] == 1:
        return staged(*arrays)
    return general(*arrays)


def solution(mesh):
    placed = (
        P("groups", "tensor"),
        P("tensor", None),
        P(("groups", "tensor"), None, None),
        P(("groups", "tensor"), None, None),
        P("groups"),
        P("groups"),
    )
    return jax.shard_map(
        shards, mesh=mesh, in_specs=placed, out_specs=P("groups", "tensor"), check_vma=False
    )
```

```python
import functools

import jax
import jax.numpy as jnp
from jax import lax
from jax.experimental import pallas as pl
from jax.experimental.pallas import tpu as pltpu
from jax.sharding import PartitionSpec as P

CAP = 32
IN_VMEM = pl.BlockSpec(memory_space=pltpu.VMEM)
IN_HBM = pl.BlockSpec(memory_space=pltpu.HBM)
ANYWHERE = pl.BlockSpec(memory_space=pl.ANY)
DMA = pltpu.SemaphoreType.DMA


def params(mib):
    return pltpu.CompilerParams(vmem_limit_bytes=mib * 1024 * 1024)


def cost(flops, moved):
    return pl.CostEstimate(flops=flops, bytes_accessed=moved, transcendentals=0)


def shape(dims, dtype=jnp.bfloat16):
    return jax.ShapeDtypeStruct(dims, dtype)


def dot(a, b):
    return jnp.dot(a, b, preferred_element_type=jnp.float32)


def swap(value, mask):
    count = lax.axis_size("tensor")
    return lax.ppermute(value, "tensor", [(t, t ^ mask) for t in range(count)])


def once_kernel(*refs):
    pass


def once(values, *after):
    return pl.pallas_call(
        once_kernel,
        out_shape=[shape(value.shape, value.dtype) for value in values],
        in_specs=[ANYWHERE] * (len(values) + len(after)),
        out_specs=[ANYWHERE] * len(values),
        input_output_aliases={i: i for i in range(len(values))},
        compiler_params=params(1),
        cost_estimate=cost(0, 0),
        name="once",
    )(*values, *after)


def route_kernel(count, layers, slot_hbm, row_ref, own_ref, y_ref, *rest):
    target_ref, out_refs = rest[-3 - layers], rest[-2 - layers : -2]
    slot_ref, slot_sem = rest[-2:]
    rows, width = own_ref.shape
    me = lax.axis_index("tensor")
    fetch = pltpu.make_async_copy(slot_hbm, slot_ref, slot_sem)
    fetch.start()
    fetch.wait()
    ids = row_ref[...]
    owner = jnp.zeros_like(ids)
    for a in range(slot_ref.shape[0]):
        owner = jnp.where(ids == a, slot_ref[a], owner)
    hot = (lax.broadcasted_iota(jnp.int32, (count, rows), 0) == owner).astype(jnp.float32)
    earlier = (
        lax.broadcasted_iota(jnp.int32, (rows, rows), 0)
        < lax.broadcasted_iota(jnp.int32, (rows, rows), 1)
    ).astype(jnp.bfloat16)
    ahead = dot(hot.astype(jnp.bfloat16), earlier)
    place = jnp.sum(ahead * hot, axis=0, keepdims=True).astype(jnp.int32)
    target = owner * CAP + place
    target_ref[...] = target
    j = lax.broadcasted_iota(jnp.int32, (2 * CAP, rows), 0)
    for k in range(layers):
        slots = (me ^ (4 * k) ^ (j // CAP)) * CAP + j % CAP
        select = (slots == target).astype(jnp.bfloat16)
        out_refs[k][:, :width] = dot(select, own_ref[...]).astype(jnp.bfloat16)
        out_refs[k][:, width:] = dot(select, y_ref[...]).astype(jnp.bfloat16)


def route(adapter_slot, row_adapter, own, y, *after):
    rows, width = own.shape
    count = lax.axis_size("tensor")
    layers = count // 4
    found = pl.pallas_call(
        functools.partial(route_kernel, count, layers),
        out_shape=[shape((1, rows), jnp.int32)] + [shape((2 * CAP, 2 * width))] * layers,
        in_specs=[IN_HBM] + [IN_VMEM] * 3 + [ANYWHERE] * len(after),
        out_specs=[IN_VMEM] * (layers + 1),
        scratch_shapes=[pltpu.SMEM(adapter_slot.shape, jnp.int32), DMA(())],
        compiler_params=params(16),
        cost_estimate=cost(8 * layers * CAP * rows * width, 16 * layers * CAP * width),
        name="route",
    )(adapter_slot, row_adapter[None, :], own, y, *after)
    return found[0], found[1:]


def product_kernel(groups, attended_hbm, weight_hbm, *refs):
    token_ref, attended_ref, weight_ref, sems = refs[-4:]
    chips = [m for group in groups for m in group]
    width = weight_ref.shape[2] // 2
    me = lax.axis_index("tensor")
    core, chip = me % 2, me // 2
    fetches = [pltpu.make_async_copy(attended_hbm, attended_ref, sems.at[len(chips)])]
    for i, m in enumerate(chips):
        start = pl.multiple_of((chip ^ m) * 2 * width, 2 * width)
        fetches.append(
            pltpu.make_async_copy(weight_hbm.at[:, pl.ds(start, 2 * width)], weight_ref.at[i], sems.at[i])
        )
    for fetch in fetches:
        fetch.start()
    token_ref[...] = jnp.zeros(token_ref.shape, token_ref.dtype)
    fetches[0].wait()
    there = pl.ds(pl.multiple_of((1 - core) * width, width), width)
    here = pl.ds(pl.multiple_of(core * width, width), width)
    at = 0
    for g, group in enumerate(groups):
        away_ref, stay_ref = refs[2 * g : 2 * g + 2]
        for i in range(len(group)):
            fetches[at + 1].wait()
            away_ref[i] = dot(attended_ref[...], weight_ref[at, :, there]).astype(jnp.bfloat16)
            stay_ref[i] = dot(attended_ref[...], weight_ref[at, :, here])
            at += 1


def product(attended, out_weight, groups, mib):
    rows, depth = attended.shape
    width = out_weight.shape[1] // lax.axis_size("tensor")
    n = sum(len(group) for group in groups)
    out_shape = []
    for group in groups:
        out_shape.append(shape((len(group), rows, width)))
        out_shape.append(shape((len(group), rows, width), jnp.float32))
    out_shape.append(shape((8, 128), jnp.float32))
    return pl.pallas_call(
        functools.partial(product_kernel, groups),
        out_shape=out_shape,
        in_specs=[IN_HBM, IN_HBM],
        out_specs=[IN_VMEM] * len(out_shape),
        scratch_shapes=[
            pltpu.VMEM((rows, depth), jnp.bfloat16),
            pltpu.VMEM((n, depth, 2 * width), jnp.bfloat16),
            DMA((n + 1,)),
        ],
        compiler_params=params(mib),
        cost_estimate=cost(4 * n * rows * depth * width, n * (4 * depth * width + 6 * rows * width)),
        name="product",
    )(attended, out_weight)


def shrink_kernel(distances, down_ref, other_ref, *refs):
    arrived_refs, out_ref = refs[: len(distances)], refs[-1]
    me = lax.axis_index("tensor")
    width = arrived_refs[0].shape[1] // 2
    over = (((1,), (1,)), ((), ()))
    for part, weights_ref in enumerate((down_ref, other_ref)):
        total = jnp.zeros((CAP, down_ref.shape[0]), jnp.float32)
        for k, arrived_ref in zip(distances, arrived_refs):
            for side in range(2):
                block = pl.ds(pl.multiple_of((me ^ (4 * k + 2 * side)) * width, width), width)
                total += lax.dot_general(
                    arrived_ref[part * CAP : (part + 1) * CAP, side * width : (side + 1) * width],
                    weights_ref[:, block],
                    over,
                    preferred_element_type=jnp.float32,
                )
        out_ref[part * CAP : (part + 1) * CAP, :] = total


def shrink(down, other, arrived, *after):
    return pl.pallas_call(
        functools.partial(shrink_kernel, tuple(arrived)),
        out_shape=shape((2 * CAP, down.shape[0]), jnp.float32),
        in_specs=[IN_VMEM] * (2 + len(arrived)) + [ANYWHERE] * len(after),
        out_specs=IN_VMEM,
        compiler_params=params(16),
        cost_estimate=cost(40 * 10**9, 4 * down.size),
        name="shrink",
    )(down, other, *arrived.values(), *after)


def grow_kernel(groups, mine_ref, other_ref, up_ref, up_other_ref, *refs):
    out_refs = refs[-len(groups) :]
    me = lax.axis_index("tensor")
    own = (mine_ref[:CAP, :] + other_ref[CAP:, :]).astype(jnp.bfloat16)
    others = (mine_ref[CAP:, :] + other_ref[:CAP, :]).astype(jnp.bfloat16)
    for masks, out_ref in zip(groups, out_refs):
        width = out_ref.shape[2]
        for i, mask in enumerate(masks):
            block = pl.ds(pl.multiple_of((me ^ mask) * width, width), width)
            out_ref[i, :CAP, :] = dot(own, up_ref[:, block]).astype(jnp.bfloat16)
            out_ref[i, CAP:, :] = dot(others, up_other_ref[:, block]).astype(jnp.bfloat16)


def grow(mine, other, up, up_other, groups, *after):
    width = up.shape[1] // lax.axis_size("tensor")
    return pl.pallas_call(
        functools.partial(grow_kernel, groups),
        out_shape=[shape((len(masks), 2 * CAP, width)) for masks in groups],
        in_specs=[IN_VMEM] * 4 + [ANYWHERE] * len(after),
        out_specs=[IN_VMEM] * len(groups),
        compiler_params=params(16),
        cost_estimate=cost(4 * 10**9, 4 * up.size),
        name="grow",
    )(mine, other, up, up_other, *after)


def join_kernel(terms, target_ref, *refs):
    out_refs = refs[-len(terms) :]
    rows = target_ref.shape[1]
    me = lax.axis_index("tensor")
    j = lax.broadcasted_iota(jnp.int32, (2 * CAP, rows), 0)
    picks = {}
    for (blocks, grown), out_ref in zip(terms, out_refs):
        total = jnp.zeros(out_ref.shape, jnp.float32)
        for at, i in blocks:
            total += refs[at][i].astype(jnp.float32)
        for at, i, mask in grown:
            if mask not in picks:
                slots = (me ^ mask ^ (j // CAP)) * CAP + j % CAP
                picks[mask] = (slots == target_ref[...]).astype(jnp.bfloat16)
            total += lax.dot_general(
                picks[mask], refs[at][i], (((0,), (0,)), ((), ())), preferred_element_type=jnp.float32
            )
        out_ref[...] = total.astype(out_ref.dtype)


def join(target, operands, terms, dtype):
    rows, width = target.shape[1], operands[0].shape[2]
    n = len(terms)
    return pl.pallas_call(
        functools.partial(join_kernel, terms),
        out_shape=[shape((rows, width), dtype)] * n,
        in_specs=[IN_VMEM] * (1 + len(operands)),
        out_specs=[IN_VMEM] * n,
        compiler_params=params(24),
        cost_estimate=cost(4 * n * CAP * rows * width, 10 * n * rows * width),
        name="join",
    )(target, *operands)


def gather_kernel(sum_ref, came_ref, out_ref):
    out_ref[...] = sum_ref[...] + came_ref[...].astype(jnp.float32)


def gather(total, came):
    return pl.pallas_call(
        gather_kernel,
        out_shape=shape(total.shape, jnp.float32),
        in_specs=[IN_VMEM] * 2,
        out_specs=IN_VMEM,
        compiler_params=params(16),
        cost_estimate=cost(total.size, 10 * total.size),
        name="gather",
    )(total, came)


def staged(attended, out_weight, adapter_down, adapter_up, row_adapter, adapter_slot):
    f32, bf16 = jnp.float32, jnp.bfloat16
    up, down = adapter_up[0], jnp.swapaxes(adapter_down, 1, 2)[0]
    from_y = swap(attended, 2)
    down_other, up_other = swap(down, 1), swap(up, 1)
    firsts, chips = (7, 6, 5), (4, 3, 2, 1, 0)
    away_first, stay_first, away, stay, token = product(attended, out_weight, (firsts, chips), 44)
    (away_first,) = once((away_first,), from_y)
    came_first = swap(away_first, 1)
    first = [stay_first[i] + came_first[i].astype(f32) for i in range(3)]
    target, outgoing = route(adapter_slot, row_adapter, attended, from_y, token, down_other, up_other)
    arrived = {k: swap(outgoing[k], 4 * k) for k in (1, 2, 3)}
    arrived[0] = outgoing[0]
    go3 = first[0].astype(bf16)
    y3 = swap(go3, 2)
    (go2,) = once((first[2].astype(bf16),), go3)
    y2 = swap(go2, 2)[None]
    z3 = swap((first[1] + y3.astype(f32)).astype(bf16), 4)[None]
    (away,) = once((away,), target)
    came = swap(away, 1)
    mine = shrink(down, down_other, arrived)
    groups = ((8, 6, 4, 2, 0), (10,), (12,), (14,))
    here, over2, over4, over6 = grow(mine, swap(mine, 1), up, up_other, groups, came)
    over2, over4, over6 = swap(over2, 2), swap(over4, 4), swap(over6, 6)
    (ready2,) = join(target, [stay, came, z3, y2], ((((0, 0), (1, 0), (2, 0), (3, 0)), ()),), f32)
    grown = [here, over2, over4, over6]
    (sum2,) = join(
        target, [ready2[None]] + grown, ((((0, 0),), tuple((1 + i, 0, 2 * i) for i in range(4))),), bf16
    )
    z2 = swap(sum2, 8)

    def blocks(m):
        return ((0, chips.index(m)), (1, chips.index(m))), ((2, chips.index(m), 0),)

    (go1,) = join(target, [stay, came, here, sum2], (blocks(3),), bf16)
    y1 = swap(go1, 2)
    (go0,) = join(target, [stay, came, here, sum2], (blocks(1),), bf16)
    y0 = swap(go0, 2)
    sums, grown = blocks(2)
    (sum1,) = join(target, [stay, came, here, y1[None], sum2], ((sums + ((3, 0),), grown),), bf16)
    z1 = swap(sum1, 4)
    (side0,) = join(target, [stay, came, here], (blocks(0),), f32)
    total = gather(side0, z2) + y0.astype(f32) + z1.astype(f32)
    return total.astype(bf16)


def general(attended, out_weight, adapter_down, adapter_up, row_adapter, adapter_slot):
    tensor_size = lax.axis_size("tensor")
    device = lax.axis_index("tensor")
    row_count = attended.shape[0]
    held_count = adapter_down.shape[0]
    storage = adapter_slot[row_adapter]
    partial_value = jnp.dot(attended, out_weight, preferred_element_type=jnp.float32)
    base_out = lax.psum_scatter(partial_value, "tensor", scatter_dimension=1, tiled=True)
    owner_of = storage // held_count
    local_index = storage % held_count
    owner_hot = (owner_of[:, None] == jnp.arange(tensor_size, dtype=jnp.int32)[None, :]).astype(
        jnp.int32
    )
    position = jnp.sum(jnp.cumsum(owner_hot, axis=0) * owner_hot, axis=1) - 1
    target = owner_of * CAP + position
    slot_row = (
        jnp.full((tensor_size * CAP,), row_count, jnp.int32)
        .at[target]
        .set(jnp.arange(row_count, dtype=jnp.int32))
    )
    padded = jnp.concatenate([attended, jnp.zeros((1, attended.shape[1]), attended.dtype)], axis=0)
    outgoing = padded[slot_row]
    arrived = lax.all_to_all(outgoing, "tensor", split_axis=0, concat_axis=1, tiled=True)
    own_slots = lax.dynamic_slice_in_dim(slot_row, device * CAP, CAP)
    slot_local = jnp.concatenate([local_index, jnp.zeros((1,), jnp.int32)])[own_slots]
    selector = (slot_local[None, :] == jnp.arange(held_count, dtype=jnp.int32)[:, None]).astype(
        jnp.float32
    )
    all_shrunk = jnp.einsum(
        "cd,adk->ack", arrived, adapter_down, preferred_element_type=jnp.float32
    )
    shrunk = jnp.sum(all_shrunk * selector[:, :, None], axis=0).astype(jnp.bfloat16)
    picked = (selector[:, :, None] * shrunk[None].astype(jnp.float32)).astype(jnp.bfloat16)
    expanded = jnp.einsum(
        "ack,akd->cd", picked, adapter_up, preferred_element_type=jnp.float32
    ).astype(jnp.bfloat16)
    returned = lax.all_to_all(expanded, "tensor", split_axis=1, concat_axis=0, tiled=True)
    delta_out = returned[target]
    return (base_out + delta_out.astype(jnp.float32)).astype(jnp.bfloat16)


def shards(*arrays):
    if lax.axis_size("tensor") == 16 and arrays[2].shape[0] == 1:
        return staged(*arrays)
    return general(*arrays)


def solution(mesh):
    placed = (
        P("groups", "tensor"),
        P("tensor", None),
        P(("groups", "tensor"), None, None),
        P(("groups", "tensor"), None, None),
        P("groups"),
        P("groups"),
    )
    return jax.shard_map(
        shards, mesh=mesh, in_specs=placed, out_specs=P("groups", "tensor"), check_vma=False
    )
```

```python
import functools

import jax
import jax.numpy as jnp
from jax import lax
from jax.experimental import pallas as pl
from jax.experimental.pallas import tpu as pltpu
from jax.sharding import PartitionSpec as P

CAP = 32
IN_VMEM = pl.BlockSpec(memory_space=pltpu.VMEM)
IN_HBM = pl.BlockSpec(memory_space=pltpu.HBM)
ANYWHERE = pl.BlockSpec(memory_space=pl.ANY)
DMA = pltpu.SemaphoreType.DMA


def params(mib):
    return pltpu.CompilerParams(vmem_limit_bytes=mib * 1024 * 1024)


def cost(flops, moved):
    return pl.CostEstimate(flops=flops, bytes_accessed=moved, transcendentals=0)


def shape(dims, dtype=jnp.bfloat16):
    return jax.ShapeDtypeStruct(dims, dtype)


def dot(a, b):
    return jnp.dot(a, b, preferred_element_type=jnp.float32)


def swap(value, mask):
    count = lax.axis_size("tensor")
    return lax.ppermute(value, "tensor", [(t, t ^ mask) for t in range(count)])


def once_kernel(*refs):
    pass


def once(values, *after):
    return pl.pallas_call(
        once_kernel,
        out_shape=[shape(value.shape, value.dtype) for value in values],
        in_specs=[ANYWHERE] * (len(values) + len(after)),
        out_specs=[ANYWHERE] * len(values),
        input_output_aliases={i: i for i in range(len(values))},
        compiler_params=params(1),
        cost_estimate=cost(0, 0),
        name="once",
    )(*values, *after)


def route_kernel(count, layers, slot_hbm, row_ref, own_ref, y_ref, *rest):
    target_ref, out_refs = rest[-3 - layers], rest[-2 - layers : -2]
    slot_ref, slot_sem = rest[-2:]
    rows, width = own_ref.shape
    me = lax.axis_index("tensor")
    fetch = pltpu.make_async_copy(slot_hbm, slot_ref, slot_sem)
    fetch.start()
    fetch.wait()
    ids = row_ref[...]
    owner = jnp.zeros_like(ids)
    for a in range(slot_ref.shape[0]):
        owner = jnp.where(ids == a, slot_ref[a], owner)
    hot = (lax.broadcasted_iota(jnp.int32, (count, rows), 0) == owner).astype(jnp.float32)
    earlier = (
        lax.broadcasted_iota(jnp.int32, (rows, rows), 0)
        < lax.broadcasted_iota(jnp.int32, (rows, rows), 1)
    ).astype(jnp.bfloat16)
    ahead = dot(hot.astype(jnp.bfloat16), earlier)
    place = jnp.sum(ahead * hot, axis=0, keepdims=True).astype(jnp.int32)
    target = owner * CAP + place
    target_ref[...] = target
    j = lax.broadcasted_iota(jnp.int32, (2 * CAP, rows), 0)
    for k in range(layers):
        slots = (me ^ (4 * k) ^ (j // CAP)) * CAP + j % CAP
        select = (slots == target).astype(jnp.bfloat16)
        out_refs[k][:, :width] = dot(select, own_ref[...]).astype(jnp.bfloat16)
        out_refs[k][:, width:] = dot(select, y_ref[...]).astype(jnp.bfloat16)


def route(adapter_slot, row_adapter, own, y, *after):
    rows, width = own.shape
    count = lax.axis_size("tensor")
    layers = count // 4
    found = pl.pallas_call(
        functools.partial(route_kernel, count, layers),
        out_shape=[shape((1, rows), jnp.int32)] + [shape((2 * CAP, 2 * width))] * layers,
        in_specs=[IN_HBM] + [IN_VMEM] * 3 + [ANYWHERE] * len(after),
        out_specs=[IN_VMEM] * (layers + 1),
        scratch_shapes=[pltpu.SMEM(adapter_slot.shape, jnp.int32), DMA(())],
        compiler_params=params(16),
        cost_estimate=cost(8 * layers * CAP * rows * width, 16 * layers * CAP * width),
        name="route",
    )(adapter_slot, row_adapter[None, :], own, y, *after)
    return found[0], found[1:]


def product_kernel(groups, attended_hbm, weight_hbm, *refs):
    token_ref, attended_ref, weight_ref, sems = refs[-4:]
    chips = [m for group in groups for m in group]
    width = weight_ref.shape[2] // 2
    me = lax.axis_index("tensor")
    core, chip = me % 2, me // 2
    fetches = [pltpu.make_async_copy(attended_hbm, attended_ref, sems.at[len(chips)])]
    for i, m in enumerate(chips):
        start = pl.multiple_of((chip ^ m) * 2 * width, 2 * width)
        fetches.append(
            pltpu.make_async_copy(weight_hbm.at[:, pl.ds(start, 2 * width)], weight_ref.at[i], sems.at[i])
        )
    for fetch in fetches:
        fetch.start()
    token_ref[...] = jnp.zeros(token_ref.shape, token_ref.dtype)
    fetches[0].wait()
    there = pl.ds(pl.multiple_of((1 - core) * width, width), width)
    here = pl.ds(pl.multiple_of(core * width, width), width)
    at = 0
    for g, group in enumerate(groups):
        away_ref, stay_ref = refs[2 * g : 2 * g + 2]
        for i in range(len(group)):
            fetches[at + 1].wait()
            away_ref[i] = dot(attended_ref[...], weight_ref[at, :, there]).astype(jnp.bfloat16)
            stay_ref[i] = dot(attended_ref[...], weight_ref[at, :, here])
            at += 1


def product(attended, out_weight, groups, mib):
    rows, depth = attended.shape
    width = out_weight.shape[1] // lax.axis_size("tensor")
    n = sum(len(group) for group in groups)
    out_shape = []
    for group in groups:
        out_shape.append(shape((len(group), rows, width)))
        out_shape.append(shape((len(group), rows, width), jnp.float32))
    out_shape.append(shape((8, 128), jnp.float32))
    return pl.pallas_call(
        functools.partial(product_kernel, groups),
        out_shape=out_shape,
        in_specs=[IN_HBM, IN_HBM],
        out_specs=[IN_VMEM] * len(out_shape),
        scratch_shapes=[
            pltpu.VMEM((rows, depth), jnp.bfloat16),
            pltpu.VMEM((n, depth, 2 * width), jnp.bfloat16),
            DMA((n + 1,)),
        ],
        compiler_params=params(mib),
        cost_estimate=cost(4 * n * rows * depth * width, n * (4 * depth * width + 6 * rows * width)),
        name="product",
    )(attended, out_weight)


def shrink_kernel(distances, down_ref, other_ref, *refs):
    arrived_refs, out_ref = refs[: len(distances)], refs[-1]
    me = lax.axis_index("tensor")
    width = arrived_refs[0].shape[1] // 2
    over = (((1,), (1,)), ((), ()))
    for part, weights_ref in enumerate((down_ref, other_ref)):
        total = jnp.zeros((CAP, down_ref.shape[0]), jnp.float32)
        for k, arrived_ref in zip(distances, arrived_refs):
            for side in range(2):
                block = pl.ds(pl.multiple_of((me ^ (4 * k + 2 * side)) * width, width), width)
                total += lax.dot_general(
                    arrived_ref[part * CAP : (part + 1) * CAP, side * width : (side + 1) * width],
                    weights_ref[:, block],
                    over,
                    preferred_element_type=jnp.float32,
                )
        out_ref[part * CAP : (part + 1) * CAP, :] = total


def shrink(down, other, arrived, *after):
    return pl.pallas_call(
        functools.partial(shrink_kernel, tuple(arrived)),
        out_shape=shape((2 * CAP, down.shape[0]), jnp.float32),
        in_specs=[IN_VMEM] * (2 + len(arrived)) + [ANYWHERE] * len(after),
        out_specs=IN_VMEM,
        compiler_params=params(16),
        cost_estimate=cost(40 * 10**9, 4 * down.size),
        name="shrink",
    )(down, other, *arrived.values(), *after)


def grow_kernel(groups, mine_ref, other_ref, up_ref, up_other_ref, *refs):
    out_refs = refs[-len(groups) :]
    me = lax.axis_index("tensor")
    own = (mine_ref[:CAP, :] + other_ref[CAP:, :]).astype(jnp.bfloat16)
    others = (mine_ref[CAP:, :] + other_ref[:CAP, :]).astype(jnp.bfloat16)
    for masks, out_ref in zip(groups, out_refs):
        width = out_ref.shape[2]
        for i, mask in enumerate(masks):
            block = pl.ds(pl.multiple_of((me ^ mask) * width, width), width)
            out_ref[i, :CAP, :] = dot(own, up_ref[:, block]).astype(jnp.bfloat16)
            out_ref[i, CAP:, :] = dot(others, up_other_ref[:, block]).astype(jnp.bfloat16)


def grow(mine, other, up, up_other, groups, *after):
    width = up.shape[1] // lax.axis_size("tensor")
    return pl.pallas_call(
        functools.partial(grow_kernel, groups),
        out_shape=[shape((len(masks), 2 * CAP, width)) for masks in groups],
        in_specs=[IN_VMEM] * 4 + [ANYWHERE] * len(after),
        out_specs=[IN_VMEM] * len(groups),
        compiler_params=params(16),
        cost_estimate=cost(4 * CAP * up.size, 4 * up.size),
        name="grow",
    )(mine, other, up, up_other, *after)


def join_kernel(terms, target_ref, *refs):
    out_refs = refs[-len(terms) :]
    rows = target_ref.shape[1]
    me = lax.axis_index("tensor")
    j = lax.broadcasted_iota(jnp.int32, (2 * CAP, rows), 0)
    picks = {}
    for (blocks, grown), out_ref in zip(terms, out_refs):
        total = jnp.zeros(out_ref.shape, jnp.float32)
        for at, i in blocks:
            total += refs[at][i].astype(jnp.float32)
        for at, i, mask in grown:
            if mask not in picks:
                slots = (me ^ mask ^ (j // CAP)) * CAP + j % CAP
                picks[mask] = (slots == target_ref[...]).astype(jnp.bfloat16)
            total += lax.dot_general(
                picks[mask], refs[at][i], (((0,), (0,)), ((), ())), preferred_element_type=jnp.float32
            )
        out_ref[...] = total.astype(out_ref.dtype)


def join(target, operands, terms, dtype):
    rows, width = target.shape[1], operands[0].shape[2]
    n = len(terms)
    return pl.pallas_call(
        functools.partial(join_kernel, terms),
        out_shape=[shape((rows, width), dtype)] * n,
        in_specs=[IN_VMEM] * (1 + len(operands)),
        out_specs=[IN_VMEM] * n,
        compiler_params=params(24),
        cost_estimate=cost(4 * n * CAP * rows * width, 10 * n * rows * width),
        name="join",
    )(target, *operands)


def gather_kernel(sum_ref, came_ref, out_ref):
    out_ref[...] = sum_ref[...] + came_ref[...].astype(jnp.float32)


def gather(total, came):
    return pl.pallas_call(
        gather_kernel,
        out_shape=shape(total.shape, jnp.float32),
        in_specs=[IN_VMEM] * 2,
        out_specs=IN_VMEM,
        compiler_params=params(16),
        cost_estimate=cost(total.size, 10 * total.size),
        name="gather",
    )(total, came)


def staged(attended, out_weight, adapter_down, adapter_up, row_adapter, adapter_slot):
    f32, bf16 = jnp.float32, jnp.bfloat16
    up, down = adapter_up[0], jnp.swapaxes(adapter_down, 1, 2)[0]
    from_y = swap(attended, 2)
    down_other, up_other = swap(down, 1), swap(up, 1)
    firsts, chips = (7, 6, 5), (4, 3, 2, 1, 0)
    away_first, stay_first, away, stay, token = product(attended, out_weight, (firsts, chips), 44)
    (away_first,) = once((away_first,), from_y)
    came_first = swap(away_first, 1)
    first = [stay_first[i] + came_first[i].astype(f32) for i in range(3)]
    target, outgoing = route(adapter_slot, row_adapter, attended, from_y, token, down_other, up_other)
    arrived = {k: swap(outgoing[k], 4 * k) for k in (1, 2, 3)}
    arrived[0] = outgoing[0]
    go3 = first[0].astype(bf16)
    y3 = swap(go3, 2)
    (go2,) = once((first[2].astype(bf16),), go3)
    y2 = swap(go2, 2)[None]
    z3 = swap((first[1] + y3.astype(f32)).astype(bf16), 4)[None]
    (away,) = once((away,), target)
    came = swap(away, 1)
    go1 = (stay[1] + came[1].astype(f32)).astype(bf16)
    y1 = swap(go1, 2)[None]
    mine = shrink(down, down_other, arrived)
    groups = ((8, 4, 2, 0), (10, 6), (12,), (14,))
    here, over2, over4, over6 = grow(mine, swap(mine, 1), up, up_other, groups, came)
    over2, over4, over6 = swap(over2, 2), swap(over4, 4), swap(over6, 6)
    (ready2,) = join(target, [stay, came, z3, y2], ((((0, 0), (1, 0), (2, 0), (3, 0)), ()),), f32)
    grown = [here, over2, over4, over6]
    (sum2,) = join(
        target, [ready2[None]] + grown, ((((0, 0),), tuple((1 + i, 0, 2 * i) for i in range(4))),), bf16
    )
    z2 = swap(sum2, 8)

    def blocks(m):
        return ((0, chips.index(m)), (1, chips.index(m))), ((2, (4, 2, 1, 0).index(m), 0),)

    (go0,) = join(target, [stay, came, here, sum2], (blocks(1),), bf16)
    y0 = swap(go0, 2)
    sums, own = blocks(2)
    (sum1,) = join(
        target, [stay, came, here, over2, y1, sum2], ((sums + ((4, 0),), own + ((3, 1, 2),)),), bf16
    )
    z1 = swap(sum1, 4)
    (side0,) = join(target, [stay, came, here], (blocks(0),), f32)
    total = gather(side0, z2) + y0.astype(f32) + z1.astype(f32)
    return total.astype(bf16)


def general(attended, out_weight, adapter_down, adapter_up, row_adapter, adapter_slot):
    tensor_size = lax.axis_size("tensor")
    device = lax.axis_index("tensor")
    row_count = attended.shape[0]
    held_count = adapter_down.shape[0]
    storage = adapter_slot[row_adapter]
    partial_value = jnp.dot(attended, out_weight, preferred_element_type=jnp.float32)
    base_out = lax.psum_scatter(partial_value, "tensor", scatter_dimension=1, tiled=True)
    owner_of = storage // held_count
    local_index = storage % held_count
    owner_hot = (owner_of[:, None] == jnp.arange(tensor_size, dtype=jnp.int32)[None, :]).astype(
        jnp.int32
    )
    position = jnp.sum(jnp.cumsum(owner_hot, axis=0) * owner_hot, axis=1) - 1
    target = owner_of * CAP + position
    slot_row = (
        jnp.full((tensor_size * CAP,), row_count, jnp.int32)
        .at[target]
        .set(jnp.arange(row_count, dtype=jnp.int32))
    )
    padded = jnp.concatenate([attended, jnp.zeros((1, attended.shape[1]), attended.dtype)], axis=0)
    outgoing = padded[slot_row]
    arrived = lax.all_to_all(outgoing, "tensor", split_axis=0, concat_axis=1, tiled=True)
    own_slots = lax.dynamic_slice_in_dim(slot_row, device * CAP, CAP)
    slot_local = jnp.concatenate([local_index, jnp.zeros((1,), jnp.int32)])[own_slots]
    selector = (slot_local[None, :] == jnp.arange(held_count, dtype=jnp.int32)[:, None]).astype(
        jnp.float32
    )
    all_shrunk = jnp.einsum(
        "cd,adk->ack", arrived, adapter_down, preferred_element_type=jnp.float32
    )
    shrunk = jnp.sum(all_shrunk * selector[:, :, None], axis=0).astype(jnp.bfloat16)
    picked = (selector[:, :, None] * shrunk[None].astype(jnp.float32)).astype(jnp.bfloat16)
    expanded = jnp.einsum(
        "ack,akd->cd", picked, adapter_up, preferred_element_type=jnp.float32
    ).astype(jnp.bfloat16)
    returned = lax.all_to_all(expanded, "tensor", split_axis=1, concat_axis=0, tiled=True)
    delta_out = returned[target]
    return (base_out + delta_out.astype(jnp.float32)).astype(jnp.bfloat16)


def shards(*arrays):
    if lax.axis_size("tensor") == 16 and arrays[2].shape[0] == 1:
        return staged(*arrays)
    return general(*arrays)


def solution(mesh):
    placed = (
        P("groups", "tensor"),
        P("tensor", None),
        P(("groups", "tensor"), None, None),
        P(("groups", "tensor"), None, None),
        P("groups"),
        P("groups"),
    )
    return jax.shard_map(
        shards, mesh=mesh, in_specs=placed, out_specs=P("groups", "tensor"), check_vma=False
    )
```

```python
import functools

import jax
import jax.numpy as jnp
from jax import lax
from jax.experimental import pallas as pl
from jax.experimental.pallas import tpu as pltpu
from jax.sharding import PartitionSpec as P

CAP = 32
IN_VMEM = pl.BlockSpec(memory_space=pltpu.VMEM)
IN_HBM = pl.BlockSpec(memory_space=pltpu.HBM)
ANYWHERE = pl.BlockSpec(memory_space=pl.ANY)
DMA = pltpu.SemaphoreType.DMA


def params(mib):
    return pltpu.CompilerParams(vmem_limit_bytes=mib * 1024 * 1024)


def cost(flops, moved):
    return pl.CostEstimate(flops=flops, bytes_accessed=moved, transcendentals=0)


def shape(dims, dtype=jnp.bfloat16):
    return jax.ShapeDtypeStruct(dims, dtype)


def dot(a, b):
    return jnp.dot(a, b, preferred_element_type=jnp.float32)


def swap(value, mask):
    count = lax.axis_size("tensor")
    return lax.ppermute(value, "tensor", [(t, t ^ mask) for t in range(count)])


def once_kernel(*refs):
    pass


def once(values, *after):
    return pl.pallas_call(
        once_kernel,
        out_shape=[shape(value.shape, value.dtype) for value in values],
        in_specs=[ANYWHERE] * (len(values) + len(after)),
        out_specs=[ANYWHERE] * len(values),
        input_output_aliases={i: i for i in range(len(values))},
        compiler_params=params(1),
        cost_estimate=cost(0, 0),
        name="once",
    )(*values, *after)


def route_kernel(count, layers, slot_hbm, row_ref, own_ref, y_ref, *rest):
    target_ref, out_refs = rest[-3 - layers], rest[-2 - layers : -2]
    slot_ref, slot_sem = rest[-2:]
    rows, width = own_ref.shape
    me = lax.axis_index("tensor")
    fetch = pltpu.make_async_copy(slot_hbm, slot_ref, slot_sem)
    fetch.start()
    fetch.wait()
    ids = row_ref[...]
    owner = jnp.zeros_like(ids)
    for a in range(slot_ref.shape[0]):
        owner = jnp.where(ids == a, slot_ref[a], owner)
    hot = (lax.broadcasted_iota(jnp.int32, (count, rows), 0) == owner).astype(jnp.float32)
    earlier = (
        lax.broadcasted_iota(jnp.int32, (rows, rows), 0)
        < lax.broadcasted_iota(jnp.int32, (rows, rows), 1)
    ).astype(jnp.bfloat16)
    ahead = dot(hot.astype(jnp.bfloat16), earlier)
    place = jnp.sum(ahead * hot, axis=0, keepdims=True).astype(jnp.int32)
    target = owner * CAP + place
    target_ref[...] = target
    j = lax.broadcasted_iota(jnp.int32, (2 * CAP, rows), 0)
    for k in range(layers):
        slots = (me ^ (4 * k) ^ (j // CAP)) * CAP + j % CAP
        select = (slots == target).astype(jnp.bfloat16)
        out_refs[k][:, :width] = dot(select, own_ref[...]).astype(jnp.bfloat16)
        out_refs[k][:, width:] = dot(select, y_ref[...]).astype(jnp.bfloat16)


def route(adapter_slot, row_adapter, own, y, *after):
    rows, width = own.shape
    count = lax.axis_size("tensor")
    layers = count // 4
    found = pl.pallas_call(
        functools.partial(route_kernel, count, layers),
        out_shape=[shape((1, rows), jnp.int32)] + [shape((2 * CAP, 2 * width))] * layers,
        in_specs=[IN_HBM] + [IN_VMEM] * 3 + [ANYWHERE] * len(after),
        out_specs=[IN_VMEM] * (layers + 1),
        scratch_shapes=[pltpu.SMEM(adapter_slot.shape, jnp.int32), DMA(())],
        compiler_params=params(16),
        cost_estimate=cost(8 * layers * CAP * rows * width, 16 * layers * CAP * width),
        name="route",
    )(adapter_slot, row_adapter[None, :], own, y, *after)
    return found[0], found[1:]


def product_kernel(groups, attended_hbm, weight_hbm, *refs):
    token_ref, attended_ref, weight_ref, sems = refs[-4:]
    chips = [m for group in groups for m in group]
    width = weight_ref.shape[2] // 2
    me = lax.axis_index("tensor")
    core, chip = me % 2, me // 2
    fetches = [pltpu.make_async_copy(attended_hbm, attended_ref, sems.at[len(chips)])]
    for i, m in enumerate(chips):
        start = pl.multiple_of((chip ^ m) * 2 * width, 2 * width)
        fetches.append(
            pltpu.make_async_copy(weight_hbm.at[:, pl.ds(start, 2 * width)], weight_ref.at[i], sems.at[i])
        )
    for fetch in fetches:
        fetch.start()
    token_ref[...] = jnp.zeros(token_ref.shape, token_ref.dtype)
    fetches[0].wait()
    there = pl.ds(pl.multiple_of((1 - core) * width, width), width)
    here = pl.ds(pl.multiple_of(core * width, width), width)
    at = 0
    for g, group in enumerate(groups):
        away_ref, stay_ref = refs[2 * g : 2 * g + 2]
        for i in range(len(group)):
            fetches[at + 1].wait()
            away_ref[i] = dot(attended_ref[...], weight_ref[at, :, there]).astype(jnp.bfloat16)
            stay_ref[i] = dot(attended_ref[...], weight_ref[at, :, here])
            at += 1


def product(attended, out_weight, groups, mib):
    rows, depth = attended.shape
    width = out_weight.shape[1] // lax.axis_size("tensor")
    n = sum(len(group) for group in groups)
    out_shape = []
    for group in groups:
        out_shape.append(shape((len(group), rows, width)))
        out_shape.append(shape((len(group), rows, width), jnp.float32))
    out_shape.append(shape((8, 128), jnp.float32))
    return pl.pallas_call(
        functools.partial(product_kernel, groups),
        out_shape=out_shape,
        in_specs=[IN_HBM, IN_HBM],
        out_specs=[IN_VMEM] * len(out_shape),
        scratch_shapes=[
            pltpu.VMEM((rows, depth), jnp.bfloat16),
            pltpu.VMEM((n, depth, 2 * width), jnp.bfloat16),
            DMA((n + 1,)),
        ],
        compiler_params=params(mib),
        cost_estimate=cost(4 * n * rows * depth * width, n * (4 * depth * width + 6 * rows * width)),
        name="product",
    )(attended, out_weight)


def shrink_kernel(distances, down_ref, other_ref, *refs):
    arrived_refs, out_ref = refs[: len(distances)], refs[-1]
    me = lax.axis_index("tensor")
    width = arrived_refs[0].shape[1] // 2
    over = (((1,), (1,)), ((), ()))
    for part, weights_ref in enumerate((down_ref, other_ref)):
        total = jnp.zeros((CAP, down_ref.shape[0]), jnp.float32)
        for k, arrived_ref in zip(distances, arrived_refs):
            for side in range(2):
                block = pl.ds(pl.multiple_of((me ^ (4 * k + 2 * side)) * width, width), width)
                total += lax.dot_general(
                    arrived_ref[part * CAP : (part + 1) * CAP, side * width : (side + 1) * width],
                    weights_ref[:, block],
                    over,
                    preferred_element_type=jnp.float32,
                )
        out_ref[part * CAP : (part + 1) * CAP, :] = total


def shrink(down, other, arrived, *after):
    return pl.pallas_call(
        functools.partial(shrink_kernel, tuple(arrived)),
        out_shape=shape((2 * CAP, down.shape[0]), jnp.float32),
        in_specs=[IN_VMEM] * (2 + len(arrived)) + [ANYWHERE] * len(after),
        out_specs=IN_VMEM,
        compiler_params=params(16),
        cost_estimate=cost(40 * 10**9, 4 * down.size),
        name="shrink",
    )(down, other, *arrived.values(), *after)


def grow_kernel(groups, mine_ref, other_ref, up_ref, up_other_ref, *refs):
    out_refs = refs[-len(groups) :]
    me = lax.axis_index("tensor")
    own = (mine_ref[:CAP, :] + other_ref[CAP:, :]).astype(jnp.bfloat16)
    others = (mine_ref[CAP:, :] + other_ref[:CAP, :]).astype(jnp.bfloat16)
    for masks, out_ref in zip(groups, out_refs):
        width = out_ref.shape[2]
        for i, mask in enumerate(masks):
            block = pl.ds(pl.multiple_of((me ^ mask) * width, width), width)
            out_ref[i, :CAP, :] = dot(own, up_ref[:, block]).astype(jnp.bfloat16)
            out_ref[i, CAP:, :] = dot(others, up_other_ref[:, block]).astype(jnp.bfloat16)


def grow(mine, other, up, up_other, groups, *after):
    width = up.shape[1] // lax.axis_size("tensor")
    return pl.pallas_call(
        functools.partial(grow_kernel, groups),
        out_shape=[shape((len(masks), 2 * CAP, width)) for masks in groups],
        in_specs=[IN_VMEM] * 4 + [ANYWHERE] * len(after),
        out_specs=[IN_VMEM] * len(groups),
        compiler_params=params(16),
        cost_estimate=cost(4 * CAP * up.size, 4 * up.size),
        name="grow",
    )(mine, other, up, up_other, *after)


def join_kernel(terms, target_ref, *refs):
    out_refs = refs[-len(terms) :]
    rows = target_ref.shape[1]
    me = lax.axis_index("tensor")
    j = lax.broadcasted_iota(jnp.int32, (2 * CAP, rows), 0)
    picks = {}
    for (blocks, grown), out_ref in zip(terms, out_refs):
        total = jnp.zeros(out_ref.shape, jnp.float32)
        for at, i in blocks:
            total += refs[at][i].astype(jnp.float32)
        for at, i, mask in grown:
            if mask not in picks:
                slots = (me ^ mask ^ (j // CAP)) * CAP + j % CAP
                picks[mask] = (slots == target_ref[...]).astype(jnp.bfloat16)
            total += lax.dot_general(
                picks[mask], refs[at][i], (((0,), (0,)), ((), ())), preferred_element_type=jnp.float32
            )
        out_ref[...] = total.astype(out_ref.dtype)


def join(target, operands, terms, dtype):
    rows, width = target.shape[1], operands[0].shape[2]
    n = len(terms)
    return pl.pallas_call(
        functools.partial(join_kernel, terms),
        out_shape=[shape((rows, width), dtype)] * n,
        in_specs=[IN_VMEM] * (1 + len(operands)),
        out_specs=[IN_VMEM] * n,
        compiler_params=params(24),
        cost_estimate=cost(4 * n * CAP * rows * width, 10 * n * rows * width),
        name="join",
    )(target, *operands)


def gather_kernel(sum_ref, came_ref, out_ref):
    out_ref[...] = sum_ref[...] + came_ref[...].astype(jnp.float32)


def gather(total, came):
    return pl.pallas_call(
        gather_kernel,
        out_shape=shape(total.shape, jnp.float32),
        in_specs=[IN_VMEM] * 2,
        out_specs=IN_VMEM,
        compiler_params=params(16),
        cost_estimate=cost(total.size, 10 * total.size),
        name="gather",
    )(total, came)


def staged(attended, out_weight, adapter_down, adapter_up, row_adapter, adapter_slot):
    f32, bf16 = jnp.float32, jnp.bfloat16
    up, down = adapter_up[0], jnp.swapaxes(adapter_down, 1, 2)[0]
    from_y = swap(attended, 2)
    down_other, up_other = swap(down, 1), swap(up, 1)
    firsts, chips = (7, 6, 5), (4, 3, 2, 1, 0)
    away_first, stay_first, away, stay, token = product(attended, out_weight, (firsts, chips), 44)
    (away_first,) = once((away_first,), from_y)
    came_first = swap(away_first, 1)
    first = [stay_first[i] + came_first[i].astype(f32) for i in range(3)]
    target, outgoing = route(adapter_slot, row_adapter, attended, from_y, token, down_other, up_other)
    arrived = {k: swap(outgoing[k], 4 * k) for k in (1, 2, 3)}
    arrived[0] = outgoing[0]
    go3 = first[0].astype(bf16)
    y3 = swap(go3, 2)
    (go2,) = once((first[2].astype(bf16),), go3)
    y2 = swap(go2, 2)[None]
    z3 = swap((first[1] + y3.astype(f32)).astype(bf16), 4)[None]
    (away,) = once((away,), target)
    came = swap(away, 1)
    go1 = (stay[1] + came[1].astype(f32)).astype(bf16)
    y1 = swap(go1, 2)[None]
    mine = shrink(down, down_other, arrived)
    groups = ((8, 4, 2, 0), (10, 6), (12,), (14,))
    here, over2, over4, over6 = grow(mine, swap(mine, 1), up, up_other, groups, came, y2)
    over6, over4, over2 = swap(over6, 6), swap(over4, 4), swap(over2, 2)
    (ready2,) = join(target, [stay, came, z3, y2], ((((0, 0), (1, 0), (2, 0), (3, 0)), ()),), f32)
    (sum2,) = join(
        target,
        [ready2[None], over6, over4, over2, here],
        ((((0, 0),), ((1, 0, 6), (2, 0, 4), (3, 0, 2), (4, 0, 0))),),
        bf16,
    )
    z2 = swap(sum2, 8)

    def blocks(m):
        return ((0, chips.index(m)), (1, chips.index(m))), ((2, (4, 2, 1, 0).index(m), 0),)

    sums, own = blocks(2)
    (sum1,) = join(
        target, [stay, came, here, over2, y1, sum2], ((sums + ((4, 0),), own + ((3, 1, 2),)),), bf16
    )
    z1 = swap(sum1, 4)
    (go0,) = join(target, [stay, came, here, sum1], (blocks(1),), bf16)
    y0 = swap(go0, 2)
    (side0,) = join(target, [stay, came, here], (blocks(0),), f32)
    total = gather(gather(side0, z2), z1) + y0.astype(f32)
    return total.astype(bf16)


def general(attended, out_weight, adapter_down, adapter_up, row_adapter, adapter_slot):
    tensor_size = lax.axis_size("tensor")
    device = lax.axis_index("tensor")
    row_count = attended.shape[0]
    held_count = adapter_down.shape[0]
    storage = adapter_slot[row_adapter]
    partial_value = jnp.dot(attended, out_weight, preferred_element_type=jnp.float32)
    base_out = lax.psum_scatter(partial_value, "tensor", scatter_dimension=1, tiled=True)
    owner_of = storage // held_count
    local_index = storage % held_count
    owner_hot = (owner_of[:, None] == jnp.arange(tensor_size, dtype=jnp.int32)[None, :]).astype(
        jnp.int32
    )
    position = jnp.sum(jnp.cumsum(owner_hot, axis=0) * owner_hot, axis=1) - 1
    target = owner_of * CAP + position
    slot_row = (
        jnp.full((tensor_size * CAP,), row_count, jnp.int32)
        .at[target]
        .set(jnp.arange(row_count, dtype=jnp.int32))
    )
    padded = jnp.concatenate([attended, jnp.zeros((1, attended.shape[1]), attended.dtype)], axis=0)
    outgoing = padded[slot_row]
    arrived = lax.all_to_all(outgoing, "tensor", split_axis=0, concat_axis=1, tiled=True)
    own_slots = lax.dynamic_slice_in_dim(slot_row, device * CAP, CAP)
    slot_local = jnp.concatenate([local_index, jnp.zeros((1,), jnp.int32)])[own_slots]
    selector = (slot_local[None, :] == jnp.arange(held_count, dtype=jnp.int32)[:, None]).astype(
        jnp.float32
    )
    all_shrunk = jnp.einsum(
        "cd,adk->ack", arrived, adapter_down, preferred_element_type=jnp.float32
    )
    shrunk = jnp.sum(all_shrunk * selector[:, :, None], axis=0).astype(jnp.bfloat16)
    picked = (selector[:, :, None] * shrunk[None].astype(jnp.float32)).astype(jnp.bfloat16)
    expanded = jnp.einsum(
        "ack,akd->cd", picked, adapter_up, preferred_element_type=jnp.float32
    ).astype(jnp.bfloat16)
    returned = lax.all_to_all(expanded, "tensor", split_axis=1, concat_axis=0, tiled=True)
    delta_out = returned[target]
    return (base_out + delta_out.astype(jnp.float32)).astype(jnp.bfloat16)


def shards(*arrays):
    if lax.axis_size("tensor") == 16 and arrays[2].shape[0] == 1:
        return staged(*arrays)
    return general(*arrays)


def solution(mesh):
    placed = (
        P("groups", "tensor"),
        P("tensor", None),
        P(("groups", "tensor"), None, None),
        P(("groups", "tensor"), None, None),
        P("groups"),
        P("groups"),
    )
    return jax.shard_map(
        shards, mesh=mesh, in_specs=placed, out_specs=P("groups", "tensor"), check_vma=False
    )
```

```python
import functools

import jax
import jax.numpy as jnp
from jax import lax
from jax.experimental import pallas as pl
from jax.experimental.pallas import tpu as pltpu
from jax.sharding import PartitionSpec as P

CAP = 32
IN_VMEM = pl.BlockSpec(memory_space=pltpu.VMEM)
IN_HBM = pl.BlockSpec(memory_space=pltpu.HBM)
ANYWHERE = pl.BlockSpec(memory_space=pl.ANY)
DMA = pltpu.SemaphoreType.DMA


def params(mib):
    return pltpu.CompilerParams(vmem_limit_bytes=mib * 1024 * 1024)


def cost(flops, moved):
    return pl.CostEstimate(flops=flops, bytes_accessed=moved, transcendentals=0)


def shape(dims, dtype=jnp.bfloat16):
    return jax.ShapeDtypeStruct(dims, dtype)


def dot(a, b):
    return jnp.dot(a, b, preferred_element_type=jnp.float32)


def swap(value, mask):
    count = lax.axis_size("tensor")
    return lax.ppermute(value, "tensor", [(t, t ^ mask) for t in range(count)])


def once_kernel(*refs):
    pass


def once(values, *after):
    return pl.pallas_call(
        once_kernel,
        out_shape=[shape(value.shape, value.dtype) for value in values],
        in_specs=[ANYWHERE] * (len(values) + len(after)),
        out_specs=[ANYWHERE] * len(values),
        input_output_aliases={i: i for i in range(len(values))},
        compiler_params=params(1),
        cost_estimate=cost(0, 0),
        name="once",
    )(*values, *after)


def route_kernel(count, layers, slot_hbm, row_ref, own_ref, y_ref, *rest):
    target_ref, out_refs = rest[-3 - layers], rest[-2 - layers : -2]
    slot_ref, slot_sem = rest[-2:]
    rows, width = own_ref.shape
    me = lax.axis_index("tensor")
    fetch = pltpu.make_async_copy(slot_hbm, slot_ref, slot_sem)
    fetch.start()
    fetch.wait()
    ids = row_ref[...]
    owner = jnp.zeros_like(ids)
    for a in range(slot_ref.shape[0]):
        owner = jnp.where(ids == a, slot_ref[a], owner)
    hot = (lax.broadcasted_iota(jnp.int32, (count, rows), 0) == owner).astype(jnp.float32)
    earlier = (
        lax.broadcasted_iota(jnp.int32, (rows, rows), 0)
        < lax.broadcasted_iota(jnp.int32, (rows, rows), 1)
    ).astype(jnp.bfloat16)
    ahead = dot(hot.astype(jnp.bfloat16), earlier)
    place = jnp.sum(ahead * hot, axis=0, keepdims=True).astype(jnp.int32)
    target = owner * CAP + place
    target_ref[...] = target
    j = lax.broadcasted_iota(jnp.int32, (2 * CAP, rows), 0)
    for k in range(layers):
        slots = (me ^ (4 * k) ^ (j // CAP)) * CAP + j % CAP
        select = (slots == target).astype(jnp.bfloat16)
        out_refs[k][:, :width] = dot(select, own_ref[...]).astype(jnp.bfloat16)
        out_refs[k][:, width:] = dot(select, y_ref[...]).astype(jnp.bfloat16)


def route(adapter_slot, row_adapter, own, y, *after):
    rows, width = own.shape
    count = lax.axis_size("tensor")
    layers = count // 4
    found = pl.pallas_call(
        functools.partial(route_kernel, count, layers),
        out_shape=[shape((1, rows), jnp.int32)] + [shape((2 * CAP, 2 * width))] * layers,
        in_specs=[IN_HBM] + [IN_VMEM] * 3 + [ANYWHERE] * len(after),
        out_specs=[IN_VMEM] * (layers + 1),
        scratch_shapes=[pltpu.SMEM(adapter_slot.shape, jnp.int32), DMA(())],
        compiler_params=params(16),
        cost_estimate=cost(8 * layers * CAP * rows * width, 16 * layers * CAP * width),
        name="route",
    )(adapter_slot, row_adapter[None, :], own, y, *after)
    return found[0], found[1:]


def product_kernel(groups, attended_hbm, weight_hbm, *refs):
    token_ref, attended_ref, weight_ref, sems = refs[-4:]
    chips = [m for group in groups for m in group]
    width = weight_ref.shape[2] // 2
    me = lax.axis_index("tensor")
    core, chip = me % 2, me // 2
    fetches = [pltpu.make_async_copy(attended_hbm, attended_ref, sems.at[len(chips)])]
    for i, m in enumerate(chips):
        start = pl.multiple_of((chip ^ m) * 2 * width, 2 * width)
        fetches.append(
            pltpu.make_async_copy(weight_hbm.at[:, pl.ds(start, 2 * width)], weight_ref.at[i], sems.at[i])
        )
    for fetch in fetches:
        fetch.start()
    token_ref[...] = jnp.zeros(token_ref.shape, token_ref.dtype)
    fetches[0].wait()
    there = pl.ds(pl.multiple_of((1 - core) * width, width), width)
    here = pl.ds(pl.multiple_of(core * width, width), width)
    at = 0
    for g, group in enumerate(groups):
        away_ref, stay_ref = refs[2 * g : 2 * g + 2]
        for i in range(len(group)):
            fetches[at + 1].wait()
            away_ref[i] = dot(attended_ref[...], weight_ref[at, :, there]).astype(jnp.bfloat16)
            stay_ref[i] = dot(attended_ref[...], weight_ref[at, :, here])
            at += 1


def product(attended, out_weight, groups, mib):
    rows, depth = attended.shape
    width = out_weight.shape[1] // lax.axis_size("tensor")
    n = sum(len(group) for group in groups)
    out_shape = []
    for group in groups:
        out_shape.append(shape((len(group), rows, width)))
        out_shape.append(shape((len(group), rows, width), jnp.float32))
    out_shape.append(shape((8, 128), jnp.float32))
    return pl.pallas_call(
        functools.partial(product_kernel, groups),
        out_shape=out_shape,
        in_specs=[IN_HBM, IN_HBM],
        out_specs=[IN_VMEM] * len(out_shape),
        scratch_shapes=[
            pltpu.VMEM((rows, depth), jnp.bfloat16),
            pltpu.VMEM((n, depth, 2 * width), jnp.bfloat16),
            DMA((n + 1,)),
        ],
        compiler_params=params(mib),
        cost_estimate=cost(4 * n * rows * depth * width, n * (4 * depth * width + 6 * rows * width)),
        name="product",
    )(attended, out_weight)


def shrink_kernel(distances, down_ref, other_ref, *refs):
    arrived_refs, out_ref = refs[: len(distances)], refs[-1]
    me = lax.axis_index("tensor")
    width = arrived_refs[0].shape[1] // 2
    over = (((1,), (1,)), ((), ()))
    for part, weights_ref in enumerate((down_ref, other_ref)):
        total = jnp.zeros((CAP, down_ref.shape[0]), jnp.float32)
        for k, arrived_ref in zip(distances, arrived_refs):
            for side in range(2):
                block = pl.ds(pl.multiple_of((me ^ (4 * k + 2 * side)) * width, width), width)
                total += lax.dot_general(
                    arrived_ref[part * CAP : (part + 1) * CAP, side * width : (side + 1) * width],
                    weights_ref[:, block],
                    over,
                    preferred_element_type=jnp.float32,
                )
        out_ref[part * CAP : (part + 1) * CAP, :] = total


def shrink(down, other, arrived, *after):
    return pl.pallas_call(
        functools.partial(shrink_kernel, tuple(arrived)),
        out_shape=shape((2 * CAP, down.shape[0]), jnp.float32),
        in_specs=[IN_VMEM] * (2 + len(arrived)) + [ANYWHERE] * len(after),
        out_specs=IN_VMEM,
        compiler_params=params(16),
        cost_estimate=cost(40 * 10**9, 4 * down.size),
        name="shrink",
    )(down, other, *arrived.values(), *after)


def grow_kernel(groups, mine_ref, other_ref, up_ref, up_other_ref, *refs):
    out_refs = refs[-len(groups) :]
    me = lax.axis_index("tensor")
    own = (mine_ref[:CAP, :] + other_ref[CAP:, :]).astype(jnp.bfloat16)
    others = (mine_ref[CAP:, :] + other_ref[:CAP, :]).astype(jnp.bfloat16)
    for masks, out_ref in zip(groups, out_refs):
        width = out_ref.shape[2]
        for i, mask in enumerate(masks):
            block = pl.ds(pl.multiple_of((me ^ mask) * width, width), width)
            out_ref[i, :CAP, :] = dot(own, up_ref[:, block]).astype(jnp.bfloat16)
            out_ref[i, CAP:, :] = dot(others, up_other_ref[:, block]).astype(jnp.bfloat16)


def grow(mine, other, up, up_other, groups, *after):
    width = up.shape[1] // lax.axis_size("tensor")
    return pl.pallas_call(
        functools.partial(grow_kernel, groups),
        out_shape=[shape((len(masks), 2 * CAP, width)) for masks in groups],
        in_specs=[IN_VMEM] * 4 + [ANYWHERE] * len(after),
        out_specs=[IN_VMEM] * len(groups),
        compiler_params=params(16),
        cost_estimate=cost(4 * CAP * up.size, 4 * up.size),
        name="grow",
    )(mine, other, up, up_other, *after)


def join_kernel(terms, target_ref, *refs):
    out_refs = refs[-len(terms) :]
    rows = target_ref.shape[1]
    me = lax.axis_index("tensor")
    j = lax.broadcasted_iota(jnp.int32, (2 * CAP, rows), 0)
    picks = {}
    for (blocks, grown), out_ref in zip(terms, out_refs):
        total = jnp.zeros(out_ref.shape, jnp.float32)
        for at, i in blocks:
            total += refs[at][i].astype(jnp.float32)
        for at, i, mask in grown:
            if mask not in picks:
                slots = (me ^ mask ^ (j // CAP)) * CAP + j % CAP
                picks[mask] = (slots == target_ref[...]).astype(jnp.bfloat16)
            total += lax.dot_general(
                picks[mask], refs[at][i], (((0,), (0,)), ((), ())), preferred_element_type=jnp.float32
            )
        out_ref[...] = total.astype(out_ref.dtype)


def join(target, operands, terms, dtype):
    rows, width = target.shape[1], operands[0].shape[2]
    n = len(terms)
    return pl.pallas_call(
        functools.partial(join_kernel, terms),
        out_shape=[shape((rows, width), dtype)] * n,
        in_specs=[IN_VMEM] * (1 + len(operands)),
        out_specs=[IN_VMEM] * n,
        compiler_params=params(24),
        cost_estimate=cost(4 * n * CAP * rows * width, 10 * n * rows * width),
        name="join",
    )(target, *operands)


def gather_kernel(sum_ref, came_ref, out_ref):
    out_ref[...] = sum_ref[...] + came_ref[...].astype(jnp.float32)


def gather(total, came):
    return pl.pallas_call(
        gather_kernel,
        out_shape=shape(total.shape, jnp.float32),
        in_specs=[IN_VMEM] * 2,
        out_specs=IN_VMEM,
        compiler_params=params(16),
        cost_estimate=cost(total.size, 10 * total.size),
        name="gather",
    )(total, came)


def staged(attended, out_weight, adapter_down, adapter_up, row_adapter, adapter_slot):
    f32, bf16 = jnp.float32, jnp.bfloat16
    up, down = adapter_up[0], jnp.swapaxes(adapter_down, 1, 2)[0]
    from_y = swap(attended, 2)
    down_other, up_other = swap(down, 1), swap(up, 1)
    firsts, chips = (7, 5, 6), (4, 3, 2, 1, 0)
    away_first, stay_first, away, stay, token = product(attended, out_weight, (firsts, chips), 44)
    (away_first,) = once((away_first,), from_y)
    came_first = swap(away_first, 1)
    target, outgoing = route(adapter_slot, row_adapter, attended, from_y, token, down_other, up_other)
    arrived = {k: swap(outgoing[k], 4 * k) for k in (2, 3, 1)}
    arrived[0] = outgoing[0]
    ys = swap((stay_first[:2] + came_first[:2].astype(f32)).astype(bf16), 2)
    last = stay_first[2] + came_first[2].astype(f32) + ys[0].astype(f32)
    z3 = swap(last.astype(bf16), 4)[None]
    (away,) = once((away,), target)
    came = swap(away, 1)
    go1 = (stay[1] + came[1].astype(f32)).astype(bf16)
    y1 = swap(go1, 2)[None]
    mine = shrink(down, down_other, arrived)
    groups = ((8, 4, 2, 0), (10, 6), (12,), (14,))
    here, over2, over4, over6 = grow(mine, swap(mine, 1), up, up_other, groups, came, ys)
    over6, over4, over2 = swap(over6, 6), swap(over4, 4), swap(over2, 2)
    (ready2,) = join(target, [stay, came, z3, ys], ((((0, 0), (1, 0), (2, 0), (3, 1)), ()),), f32)
    (sum2,) = join(
        target,
        [ready2[None], over6, over4, over2, here],
        ((((0, 0),), ((1, 0, 6), (2, 0, 4), (3, 0, 2), (4, 0, 0))),),
        bf16,
    )
    z2 = swap(sum2, 8)

    def blocks(m):
        return ((0, chips.index(m)), (1, chips.index(m))), ((2, (4, 2, 1, 0).index(m), 0),)

    sums, own = blocks(2)
    (sum1,) = join(
        target, [stay, came, here, over2, y1, sum2], ((sums + ((4, 0),), own + ((3, 1, 2),)),), bf16
    )
    z1 = swap(sum1, 4)
    (go0,) = join(target, [stay, came, here, sum1], (blocks(1),), bf16)
    y0 = swap(go0, 2)
    (side0,) = join(target, [stay, came, here], (blocks(0),), f32)
    total = gather(gather(side0, z2), z1) + y0.astype(f32)
    return total.astype(bf16)


def general(attended, out_weight, adapter_down, adapter_up, row_adapter, adapter_slot):
    tensor_size = lax.axis_size("tensor")
    device = lax.axis_index("tensor")
    row_count = attended.shape[0]
    held_count = adapter_down.shape[0]
    storage = adapter_slot[row_adapter]
    partial_value = jnp.dot(attended, out_weight, preferred_element_type=jnp.float32)
    base_out = lax.psum_scatter(partial_value, "tensor", scatter_dimension=1, tiled=True)
    owner_of = storage // held_count
    local_index = storage % held_count
    owner_hot = (owner_of[:, None] == jnp.arange(tensor_size, dtype=jnp.int32)[None, :]).astype(
        jnp.int32
    )
    position = jnp.sum(jnp.cumsum(owner_hot, axis=0) * owner_hot, axis=1) - 1
    target = owner_of * CAP + position
    slot_row = (
        jnp.full((tensor_size * CAP,), row_count, jnp.int32)
        .at[target]
        .set(jnp.arange(row_count, dtype=jnp.int32))
    )
    padded = jnp.concatenate([attended, jnp.zeros((1, attended.shape[1]), attended.dtype)], axis=0)
    outgoing = padded[slot_row]
    arrived = lax.all_to_all(outgoing, "tensor", split_axis=0, concat_axis=1, tiled=True)
    own_slots = lax.dynamic_slice_in_dim(slot_row, device * CAP, CAP)
    slot_local = jnp.concatenate([local_index, jnp.zeros((1,), jnp.int32)])[own_slots]
    selector = (slot_local[None, :] == jnp.arange(held_count, dtype=jnp.int32)[:, None]).astype(
        jnp.float32
    )
    all_shrunk = jnp.einsum(
        "cd,adk->ack", arrived, adapter_down, preferred_element_type=jnp.float32
    )
    shrunk = jnp.sum(all_shrunk * selector[:, :, None], axis=0).astype(jnp.bfloat16)
    picked = (selector[:, :, None] * shrunk[None].astype(jnp.float32)).astype(jnp.bfloat16)
    expanded = jnp.einsum(
        "ack,akd->cd", picked, adapter_up, preferred_element_type=jnp.float32
    ).astype(jnp.bfloat16)
    returned = lax.all_to_all(expanded, "tensor", split_axis=1, concat_axis=0, tiled=True)
    delta_out = returned[target]
    return (base_out + delta_out.astype(jnp.float32)).astype(jnp.bfloat16)


def shards(*arrays):
    if lax.axis_size("tensor") == 16 and arrays[2].shape[0] == 1:
        return staged(*arrays)
    return general(*arrays)


def solution(mesh):
    placed = (
        P("groups", "tensor"),
        P("tensor", None),
        P(("groups", "tensor"), None, None),
        P(("groups", "tensor"), None, None),
        P("groups"),
        P("groups"),
    )
    return jax.shard_map(
        shards, mesh=mesh, in_specs=placed, out_specs=P("groups", "tensor"), check_vma=False
    )
```

```python
import functools

import jax
import jax.numpy as jnp
from jax import lax
from jax.experimental import pallas as pl
from jax.experimental.pallas import tpu as pltpu
from jax.sharding import PartitionSpec as P

CAP = 32
IN_VMEM = pl.BlockSpec(memory_space=pltpu.VMEM)
IN_HBM = pl.BlockSpec(memory_space=pltpu.HBM)
ANYWHERE = pl.BlockSpec(memory_space=pl.ANY)
DMA = pltpu.SemaphoreType.DMA


def params(mib):
    return pltpu.CompilerParams(vmem_limit_bytes=mib * 1024 * 1024)


def cost(flops, moved):
    return pl.CostEstimate(flops=flops, bytes_accessed=moved, transcendentals=0)


def shape(dims, dtype=jnp.bfloat16):
    return jax.ShapeDtypeStruct(dims, dtype)


def dot(a, b):
    return jnp.dot(a, b, preferred_element_type=jnp.float32)


def swap(value, mask):
    count = lax.axis_size("tensor")
    return lax.ppermute(value, "tensor", [(t, t ^ mask) for t in range(count)])


def once_kernel(*refs):
    pass


def once(values, *after):
    return pl.pallas_call(
        once_kernel,
        out_shape=[shape(value.shape, value.dtype) for value in values],
        in_specs=[ANYWHERE] * (len(values) + len(after)),
        out_specs=[ANYWHERE] * len(values),
        input_output_aliases={i: i for i in range(len(values))},
        compiler_params=params(1),
        cost_estimate=cost(0, 0),
        name="once",
    )(*values, *after)


def route_kernel(count, layers, slot_hbm, row_ref, own_ref, y_ref, *rest):
    target_ref, out_refs = rest[-3 - layers], rest[-2 - layers : -2]
    slot_ref, slot_sem = rest[-2:]
    rows, width = own_ref.shape
    me = lax.axis_index("tensor")
    fetch = pltpu.make_async_copy(slot_hbm, slot_ref, slot_sem)
    fetch.start()
    fetch.wait()
    ids = row_ref[...]
    owner = jnp.zeros_like(ids)
    for a in range(slot_ref.shape[0]):
        owner = jnp.where(ids == a, slot_ref[a], owner)
    hot = (lax.broadcasted_iota(jnp.int32, (count, rows), 0) == owner).astype(jnp.float32)
    earlier = (
        lax.broadcasted_iota(jnp.int32, (rows, rows), 0)
        < lax.broadcasted_iota(jnp.int32, (rows, rows), 1)
    ).astype(jnp.bfloat16)
    ahead = dot(hot.astype(jnp.bfloat16), earlier)
    place = jnp.sum(ahead * hot, axis=0, keepdims=True).astype(jnp.int32)
    target = owner * CAP + place
    target_ref[...] = target
    j = lax.broadcasted_iota(jnp.int32, (2 * CAP, rows), 0)
    for k in range(layers):
        slots = (me ^ (4 * k) ^ (j // CAP)) * CAP + j % CAP
        select = (slots == target).astype(jnp.bfloat16)
        out_refs[k][:, :width] = dot(select, own_ref[...]).astype(jnp.bfloat16)
        out_refs[k][:, width:] = dot(select, y_ref[...]).astype(jnp.bfloat16)


def route(adapter_slot, row_adapter, own, y, *after):
    rows, width = own.shape
    count = lax.axis_size("tensor")
    layers = count // 4
    found = pl.pallas_call(
        functools.partial(route_kernel, count, layers),
        out_shape=[shape((1, rows), jnp.int32)] + [shape((2 * CAP, 2 * width))] * layers,
        in_specs=[IN_HBM] + [IN_VMEM] * 3 + [ANYWHERE] * len(after),
        out_specs=[IN_VMEM] * (layers + 1),
        scratch_shapes=[pltpu.SMEM(adapter_slot.shape, jnp.int32), DMA(())],
        compiler_params=params(16),
        cost_estimate=cost(8 * layers * CAP * rows * width, 16 * layers * CAP * width),
        name="route",
    )(adapter_slot, row_adapter[None, :], own, y, *after)
    return found[0], found[1:]


def product_kernel(groups, attended_hbm, weight_hbm, *refs):
    token_ref, attended_ref, weight_ref, sems = refs[-4:]
    chips = [m for group in groups for m in group]
    width = weight_ref.shape[2] // 2
    me = lax.axis_index("tensor")
    core, chip = me % 2, me // 2
    fetches = [pltpu.make_async_copy(attended_hbm, attended_ref, sems.at[len(chips)])]
    for i, m in enumerate(chips):
        start = pl.multiple_of((chip ^ m) * 2 * width, 2 * width)
        fetches.append(
            pltpu.make_async_copy(weight_hbm.at[:, pl.ds(start, 2 * width)], weight_ref.at[i], sems.at[i])
        )
    for fetch in fetches:
        fetch.start()
    token_ref[...] = jnp.zeros(token_ref.shape, token_ref.dtype)
    fetches[0].wait()
    there = pl.ds(pl.multiple_of((1 - core) * width, width), width)
    here = pl.ds(pl.multiple_of(core * width, width), width)
    at = 0
    for g, group in enumerate(groups):
        away_ref, stay_ref = refs[2 * g : 2 * g + 2]
        for i in range(len(group)):
            fetches[at + 1].wait()
            away_ref[i] = dot(attended_ref[...], weight_ref[at, :, there]).astype(jnp.bfloat16)
            stay_ref[i] = dot(attended_ref[...], weight_ref[at, :, here])
            at += 1


def product(attended, out_weight, groups, mib):
    rows, depth = attended.shape
    width = out_weight.shape[1] // lax.axis_size("tensor")
    n = sum(len(group) for group in groups)
    out_shape = []
    for group in groups:
        out_shape.append(shape((len(group), rows, width)))
        out_shape.append(shape((len(group), rows, width), jnp.float32))
    out_shape.append(shape((8, 128), jnp.float32))
    return pl.pallas_call(
        functools.partial(product_kernel, groups),
        out_shape=out_shape,
        in_specs=[IN_HBM, IN_HBM],
        out_specs=[IN_VMEM] * len(out_shape),
        scratch_shapes=[
            pltpu.VMEM((rows, depth), jnp.bfloat16),
            pltpu.VMEM((n, depth, 2 * width), jnp.bfloat16),
            DMA((n + 1,)),
        ],
        compiler_params=params(mib),
        cost_estimate=cost(4 * n * rows * depth * width, n * (4 * depth * width + 6 * rows * width)),
        name="product",
    )(attended, out_weight)


def shrink_kernel(distances, down_ref, other_ref, *refs):
    arrived_refs, out_ref = refs[: len(distances)], refs[-1]
    me = lax.axis_index("tensor")
    width = arrived_refs[0].shape[1] // 2
    over = (((1,), (1,)), ((), ()))
    for part, weights_ref in enumerate((down_ref, other_ref)):
        total = jnp.zeros((CAP, down_ref.shape[0]), jnp.float32)
        for k, arrived_ref in zip(distances, arrived_refs):
            for side in range(2):
                block = pl.ds(pl.multiple_of((me ^ (4 * k + 2 * side)) * width, width), width)
                total += lax.dot_general(
                    arrived_ref[part * CAP : (part + 1) * CAP, side * width : (side + 1) * width],
                    weights_ref[:, block],
                    over,
                    preferred_element_type=jnp.float32,
                )
        out_ref[part * CAP : (part + 1) * CAP, :] = total


def shrink(down, other, arrived, *after):
    return pl.pallas_call(
        functools.partial(shrink_kernel, tuple(arrived)),
        out_shape=shape((2 * CAP, down.shape[0]), jnp.float32),
        in_specs=[IN_VMEM] * (2 + len(arrived)) + [ANYWHERE] * len(after),
        out_specs=IN_VMEM,
        compiler_params=params(16),
        cost_estimate=cost(40 * 10**9, 4 * down.size),
        name="shrink",
    )(down, other, *arrived.values(), *after)


def grow_kernel(groups, mine_ref, other_ref, up_ref, up_other_ref, *refs):
    out_refs = refs[-len(groups) :]
    me = lax.axis_index("tensor")
    own = (mine_ref[:CAP, :] + other_ref[CAP:, :]).astype(jnp.bfloat16)
    others = (mine_ref[CAP:, :] + other_ref[:CAP, :]).astype(jnp.bfloat16)
    for masks, out_ref in zip(groups, out_refs):
        width = out_ref.shape[2]
        for i, mask in enumerate(masks):
            block = pl.ds(pl.multiple_of((me ^ mask) * width, width), width)
            out_ref[i, :CAP, :] = dot(own, up_ref[:, block]).astype(jnp.bfloat16)
            out_ref[i, CAP:, :] = dot(others, up_other_ref[:, block]).astype(jnp.bfloat16)


def grow(mine, other, up, up_other, groups, *after):
    width = up.shape[1] // lax.axis_size("tensor")
    return pl.pallas_call(
        functools.partial(grow_kernel, groups),
        out_shape=[shape((len(masks), 2 * CAP, width)) for masks in groups],
        in_specs=[IN_VMEM] * 4 + [ANYWHERE] * len(after),
        out_specs=[IN_VMEM] * len(groups),
        compiler_params=params(16),
        cost_estimate=cost(4 * CAP * up.size, 4 * up.size),
        name="grow",
    )(mine, other, up, up_other, *after)


def join_kernel(terms, target_ref, *refs):
    out_refs = refs[-len(terms) :]
    rows = target_ref.shape[1]
    me = lax.axis_index("tensor")
    j = lax.broadcasted_iota(jnp.int32, (2 * CAP, rows), 0)
    picks = {}
    for (blocks, grown), out_ref in zip(terms, out_refs):
        total = jnp.zeros(out_ref.shape, jnp.float32)
        for at, i in blocks:
            total += refs[at][i].astype(jnp.float32)
        for at, i, mask in grown:
            if mask not in picks:
                slots = (me ^ mask ^ (j // CAP)) * CAP + j % CAP
                picks[mask] = (slots == target_ref[...]).astype(jnp.bfloat16)
            total += lax.dot_general(
                picks[mask], refs[at][i], (((0,), (0,)), ((), ())), preferred_element_type=jnp.float32
            )
        out_ref[...] = total.astype(out_ref.dtype)


def join(target, operands, terms, dtype):
    rows, width = target.shape[1], operands[0].shape[2]
    n = len(terms)
    return pl.pallas_call(
        functools.partial(join_kernel, terms),
        out_shape=[shape((rows, width), dtype)] * n,
        in_specs=[IN_VMEM] * (1 + len(operands)),
        out_specs=[IN_VMEM] * n,
        compiler_params=params(24),
        cost_estimate=cost(4 * n * CAP * rows * width, 10 * n * rows * width),
        name="join",
    )(target, *operands)


def gather_kernel(sum_ref, came_ref, out_ref):
    out_ref[...] = sum_ref[...] + came_ref[...].astype(jnp.float32)


def gather(total, came):
    return pl.pallas_call(
        gather_kernel,
        out_shape=shape(total.shape, jnp.float32),
        in_specs=[IN_VMEM] * 2,
        out_specs=IN_VMEM,
        compiler_params=params(16),
        cost_estimate=cost(total.size, 10 * total.size),
        name="gather",
    )(total, came)


def staged(attended, out_weight, adapter_down, adapter_up, row_adapter, adapter_slot):
    f32, bf16 = jnp.float32, jnp.bfloat16
    up, down = adapter_up[0], jnp.swapaxes(adapter_down, 1, 2)[0]
    from_y = swap(attended, 2)
    down_other, up_other = swap(down, 1), swap(up, 1)
    firsts, chips = (7, 6, 5), (4, 3, 2, 1, 0)
    away_first, stay_first, away, stay, token = product(attended, out_weight, (firsts, chips), 44)
    (away_first,) = once((away_first,), from_y)
    came_first = swap(away_first, 1)
    first = [stay_first[i] + came_first[i].astype(f32) for i in range(3)]
    target, outgoing = route(adapter_slot, row_adapter, attended, from_y, token, down_other, up_other)
    arrived = {k: swap(outgoing[k], 4 * k) for k in (2, 3, 1)}
    arrived[0] = outgoing[0]
    go3 = first[0].astype(bf16)
    y3 = swap(go3, 2)
    (go2,) = once((first[2].astype(bf16),), go3)
    y2 = swap(go2, 2)[None]
    z3 = swap((first[1] + y3.astype(f32)).astype(bf16), 4)[None]
    (away,) = once((away,), target)
    came = swap(away, 1)
    go1 = (stay[1] + came[1].astype(f32)).astype(bf16)
    y1 = swap(go1, 2)[None]
    mine = shrink(down, down_other, arrived)
    groups = ((8, 4, 2, 0), (10, 6), (12,), (14,))
    here, over2, over4, over6 = grow(mine, swap(mine, 1), up, up_other, groups, came, y2)
    over6, over4, over2 = swap(over6, 6), swap(over4, 4), swap(over2, 2)
    (ready2,) = join(target, [stay, came, z3, y2], ((((0, 0), (1, 0), (2, 0), (3, 0)), ()),), f32)
    (sum2,) = join(
        target,
        [ready2[None], over6, over4, over2, here],
        ((((0, 0),), ((1, 0, 6), (2, 0, 4), (3, 0, 2), (4, 0, 0))),),
        bf16,
    )
    z2 = swap(sum2, 8)

    def blocks(m):
        return ((0, chips.index(m)), (1, chips.index(m))), ((2, (4, 2, 1, 0).index(m), 0),)

    sums, own = blocks(2)
    (sum1,) = join(
        target, [stay, came, here, over2, y1, sum2], ((sums + ((4, 0),), own + ((3, 1, 2),)),), bf16
    )
    z1 = swap(sum1, 4)
    (go0,) = join(target, [stay, came, here, sum1], (blocks(1),), bf16)
    y0 = swap(go0, 2)
    (side0,) = join(target, [stay, came, here], (blocks(0),), f32)
    total = gather(gather(side0, z2), z1) + y0.astype(f32)
    return total.astype(bf16)


def general(attended, out_weight, adapter_down, adapter_up, row_adapter, adapter_slot):
    tensor_size = lax.axis_size("tensor")
    device = lax.axis_index("tensor")
    row_count = attended.shape[0]
    held_count = adapter_down.shape[0]
    storage = adapter_slot[row_adapter]
    partial_value = jnp.dot(attended, out_weight, preferred_element_type=jnp.float32)
    base_out = lax.psum_scatter(partial_value, "tensor", scatter_dimension=1, tiled=True)
    owner_of = storage // held_count
    local_index = storage % held_count
    owner_hot = (owner_of[:, None] == jnp.arange(tensor_size, dtype=jnp.int32)[None, :]).astype(
        jnp.int32
    )
    position = jnp.sum(jnp.cumsum(owner_hot, axis=0) * owner_hot, axis=1) - 1
    target = owner_of * CAP + position
    slot_row = (
        jnp.full((tensor_size * CAP,), row_count, jnp.int32)
        .at[target]
        .set(jnp.arange(row_count, dtype=jnp.int32))
    )
    padded = jnp.concatenate([attended, jnp.zeros((1, attended.shape[1]), attended.dtype)], axis=0)
    outgoing = padded[slot_row]
    arrived = lax.all_to_all(outgoing, "tensor", split_axis=0, concat_axis=1, tiled=True)
    own_slots = lax.dynamic_slice_in_dim(slot_row, device * CAP, CAP)
    slot_local = jnp.concatenate([local_index, jnp.zeros((1,), jnp.int32)])[own_slots]
    selector = (slot_local[None, :] == jnp.arange(held_count, dtype=jnp.int32)[:, None]).astype(
        jnp.float32
    )
    all_shrunk = jnp.einsum(
        "cd,adk->ack", arrived, adapter_down, preferred_element_type=jnp.float32
    )
    shrunk = jnp.sum(all_shrunk * selector[:, :, None], axis=0).astype(jnp.bfloat16)
    picked = (selector[:, :, None] * shrunk[None].astype(jnp.float32)).astype(jnp.bfloat16)
    expanded = jnp.einsum(
        "ack,akd->cd", picked, adapter_up, preferred_element_type=jnp.float32
    ).astype(jnp.bfloat16)
    returned = lax.all_to_all(expanded, "tensor", split_axis=1, concat_axis=0, tiled=True)
    delta_out = returned[target]
    return (base_out + delta_out.astype(jnp.float32)).astype(jnp.bfloat16)


def shards(*arrays):
    if lax.axis_size("tensor") == 16 and arrays[2].shape[0] == 1:
        return staged(*arrays)
    return general(*arrays)


def solution(mesh):
    placed = (
        P("groups", "tensor"),
        P("tensor", None),
        P(("groups", "tensor"), None, None),
        P(("groups", "tensor"), None, None),
        P("groups"),
        P("groups"),
    )
    return jax.shard_map(
        shards, mesh=mesh, in_specs=placed, out_specs=P("groups", "tensor"), check_vma=False
    )
```

```python
import functools

import jax
import jax.numpy as jnp
from jax import lax
from jax.experimental import pallas as pl
from jax.experimental.pallas import tpu as pltpu
from jax.sharding import PartitionSpec as P

CAP = 32
IN_VMEM = pl.BlockSpec(memory_space=pltpu.VMEM)
IN_HBM = pl.BlockSpec(memory_space=pltpu.HBM)
ANYWHERE = pl.BlockSpec(memory_space=pl.ANY)
DMA = pltpu.SemaphoreType.DMA


def params(mib):
    return pltpu.CompilerParams(vmem_limit_bytes=mib * 1024 * 1024)


def cost(flops, moved):
    return pl.CostEstimate(flops=flops, bytes_accessed=moved, transcendentals=0)


def shape(dims, dtype=jnp.bfloat16):
    return jax.ShapeDtypeStruct(dims, dtype)


def dot(a, b):
    return jnp.dot(a, b, preferred_element_type=jnp.float32)


def swap(value, mask):
    count = lax.axis_size("tensor")
    return lax.ppermute(value, "tensor", [(t, t ^ mask) for t in range(count)])


def once_kernel(*refs):
    pass


def once(values, *after):
    return pl.pallas_call(
        once_kernel,
        out_shape=[shape(value.shape, value.dtype) for value in values],
        in_specs=[ANYWHERE] * (len(values) + len(after)),
        out_specs=[ANYWHERE] * len(values),
        input_output_aliases={i: i for i in range(len(values))},
        compiler_params=params(1),
        cost_estimate=cost(0, 0),
        name="once",
    )(*values, *after)


def route_kernel(count, layers, slot_hbm, row_ref, own_ref, y_ref, *rest):
    target_ref, out_refs = rest[-3 - layers], rest[-2 - layers : -2]
    slot_ref, slot_sem = rest[-2:]
    rows, width = own_ref.shape
    me = lax.axis_index("tensor")
    fetch = pltpu.make_async_copy(slot_hbm, slot_ref, slot_sem)
    fetch.start()
    fetch.wait()
    ids = row_ref[...]
    owner = jnp.zeros_like(ids)
    for a in range(slot_ref.shape[0]):
        owner = jnp.where(ids == a, slot_ref[a], owner)
    hot = (lax.broadcasted_iota(jnp.int32, (count, rows), 0) == owner).astype(jnp.float32)
    earlier = (
        lax.broadcasted_iota(jnp.int32, (rows, rows), 0)
        < lax.broadcasted_iota(jnp.int32, (rows, rows), 1)
    ).astype(jnp.bfloat16)
    ahead = dot(hot.astype(jnp.bfloat16), earlier)
    place = jnp.sum(ahead * hot, axis=0, keepdims=True).astype(jnp.int32)
    target = owner * CAP + place
    target_ref[...] = target
    j = lax.broadcasted_iota(jnp.int32, (2 * CAP, rows), 0)
    for k in range(layers):
        slots = (me ^ (4 * k) ^ (j // CAP)) * CAP + j % CAP
        select = (slots == target).astype(jnp.bfloat16)
        out_refs[k][:, :width] = dot(select, own_ref[...]).astype(jnp.bfloat16)
        out_refs[k][:, width:] = dot(select, y_ref[...]).astype(jnp.bfloat16)


def route(adapter_slot, row_adapter, own, y, *after):
    rows, width = own.shape
    count = lax.axis_size("tensor")
    layers = count // 4
    found = pl.pallas_call(
        functools.partial(route_kernel, count, layers),
        out_shape=[shape((1, rows), jnp.int32)] + [shape((2 * CAP, 2 * width))] * layers,
        in_specs=[IN_HBM] + [IN_VMEM] * 3 + [ANYWHERE] * len(after),
        out_specs=[IN_VMEM] * (layers + 1),
        scratch_shapes=[pltpu.SMEM(adapter_slot.shape, jnp.int32), DMA(())],
        compiler_params=params(16),
        cost_estimate=cost(8 * layers * CAP * rows * width, 16 * layers * CAP * width),
        name="route",
    )(adapter_slot, row_adapter[None, :], own, y, *after)
    return found[0], found[1:]


def product_kernel(groups, attended_hbm, weight_hbm, *refs):
    token_ref, attended_ref, weight_ref, sems = refs[-4:]
    chips = [m for group in groups for m in group]
    width = weight_ref.shape[2] // 2
    me = lax.axis_index("tensor")
    core, chip = me % 2, me // 2
    fetches = [pltpu.make_async_copy(attended_hbm, attended_ref, sems.at[len(chips)])]
    for i, m in enumerate(chips):
        start = pl.multiple_of((chip ^ m) * 2 * width, 2 * width)
        fetches.append(
            pltpu.make_async_copy(weight_hbm.at[:, pl.ds(start, 2 * width)], weight_ref.at[i], sems.at[i])
        )
    for fetch in fetches:
        fetch.start()
    token_ref[...] = jnp.zeros(token_ref.shape, token_ref.dtype)
    fetches[0].wait()
    there = pl.ds(pl.multiple_of((1 - core) * width, width), width)
    here = pl.ds(pl.multiple_of(core * width, width), width)
    at = 0
    for g, group in enumerate(groups):
        away_ref, stay_ref = refs[2 * g : 2 * g + 2]
        for i in range(len(group)):
            fetches[at + 1].wait()
            away_ref[i] = dot(attended_ref[...], weight_ref[at, :, there]).astype(jnp.bfloat16)
            stay_ref[i] = dot(attended_ref[...], weight_ref[at, :, here])
            at += 1


def product(attended, out_weight, groups, mib):
    rows, depth = attended.shape
    width = out_weight.shape[1] // lax.axis_size("tensor")
    n = sum(len(group) for group in groups)
    out_shape = []
    for group in groups:
        out_shape.append(shape((len(group), rows, width)))
        out_shape.append(shape((len(group), rows, width), jnp.float32))
    out_shape.append(shape((8, 128), jnp.float32))
    return pl.pallas_call(
        functools.partial(product_kernel, groups),
        out_shape=out_shape,
        in_specs=[IN_HBM, IN_HBM],
        out_specs=[IN_VMEM] * len(out_shape),
        scratch_shapes=[
            pltpu.VMEM((rows, depth), jnp.bfloat16),
            pltpu.VMEM((n, depth, 2 * width), jnp.bfloat16),
            DMA((n + 1,)),
        ],
        compiler_params=params(mib),
        cost_estimate=cost(4 * n * rows * depth * width, n * (4 * depth * width + 6 * rows * width)),
        name="product",
    )(attended, out_weight)


def shrink_kernel(distances, down_ref, other_ref, *refs):
    arrived_refs, out_ref = refs[: len(distances)], refs[-1]
    me = lax.axis_index("tensor")
    width = arrived_refs[0].shape[1] // 2
    over = (((1,), (1,)), ((), ()))
    for part, weights_ref in enumerate((down_ref, other_ref)):
        total = jnp.zeros((CAP, down_ref.shape[0]), jnp.float32)
        for k, arrived_ref in zip(distances, arrived_refs):
            for side in range(2):
                block = pl.ds(pl.multiple_of((me ^ (4 * k + 2 * side)) * width, width), width)
                total += lax.dot_general(
                    arrived_ref[part * CAP : (part + 1) * CAP, side * width : (side + 1) * width],
                    weights_ref[:, block],
                    over,
                    preferred_element_type=jnp.float32,
                )
        out_ref[part * CAP : (part + 1) * CAP, :] = total


def shrink(down, other, arrived, *after):
    return pl.pallas_call(
        functools.partial(shrink_kernel, tuple(arrived)),
        out_shape=shape((2 * CAP, down.shape[0]), jnp.float32),
        in_specs=[IN_VMEM] * (2 + len(arrived)) + [ANYWHERE] * len(after),
        out_specs=IN_VMEM,
        compiler_params=params(16),
        cost_estimate=cost(40 * 10**9, 4 * down.size),
        name="shrink",
    )(down, other, *arrived.values(), *after)


def grow_kernel(groups, mine_ref, other_ref, up_ref, up_other_ref, *refs):
    out_refs = refs[-len(groups) :]
    me = lax.axis_index("tensor")
    own = (mine_ref[:CAP, :] + other_ref[CAP:, :]).astype(jnp.bfloat16)
    others = (mine_ref[CAP:, :] + other_ref[:CAP, :]).astype(jnp.bfloat16)
    for masks, out_ref in zip(groups, out_refs):
        width = out_ref.shape[2]
        for i, mask in enumerate(masks):
            block = pl.ds(pl.multiple_of((me ^ mask) * width, width), width)
            out_ref[i, :CAP, :] = dot(own, up_ref[:, block]).astype(jnp.bfloat16)
            out_ref[i, CAP:, :] = dot(others, up_other_ref[:, block]).astype(jnp.bfloat16)


def grow(mine, other, up, up_other, groups, *after):
    width = up.shape[1] // lax.axis_size("tensor")
    return pl.pallas_call(
        functools.partial(grow_kernel, groups),
        out_shape=[shape((len(masks), 2 * CAP, width)) for masks in groups],
        in_specs=[IN_VMEM] * 4 + [ANYWHERE] * len(after),
        out_specs=[IN_VMEM] * len(groups),
        compiler_params=params(16),
        cost_estimate=cost(4 * CAP * up.size, 4 * up.size),
        name="grow",
    )(mine, other, up, up_other, *after)


def join_kernel(terms, target_ref, *refs):
    out_refs = refs[-len(terms) :]
    rows = target_ref.shape[1]
    me = lax.axis_index("tensor")
    j = lax.broadcasted_iota(jnp.int32, (2 * CAP, rows), 0)
    picks = {}
    for (blocks, grown), out_ref in zip(terms, out_refs):
        total = jnp.zeros(out_ref.shape, jnp.float32)
        for at, i in blocks:
            total += refs[at][i].astype(jnp.float32)
        for at, i, mask in grown:
            if mask not in picks:
                slots = (me ^ mask ^ (j // CAP)) * CAP + j % CAP
                picks[mask] = (slots == target_ref[...]).astype(jnp.bfloat16)
            total += lax.dot_general(
                picks[mask], refs[at][i], (((0,), (0,)), ((), ())), preferred_element_type=jnp.float32
            )
        out_ref[...] = total.astype(out_ref.dtype)


def join(target, operands, terms, dtype):
    rows, width = target.shape[1], operands[0].shape[2]
    n = len(terms)
    return pl.pallas_call(
        functools.partial(join_kernel, terms),
        out_shape=[shape((rows, width), dtype)] * n,
        in_specs=[IN_VMEM] * (1 + len(operands)),
        out_specs=[IN_VMEM] * n,
        compiler_params=params(24),
        cost_estimate=cost(4 * n * CAP * rows * width, 10 * n * rows * width),
        name="join",
    )(target, *operands)


def gather_kernel(sum_ref, came_ref, out_ref):
    out_ref[...] = sum_ref[...] + came_ref[...].astype(jnp.float32)


def gather(total, came):
    return pl.pallas_call(
        gather_kernel,
        out_shape=shape(total.shape, jnp.float32),
        in_specs=[IN_VMEM] * 2,
        out_specs=IN_VMEM,
        compiler_params=params(16),
        cost_estimate=cost(total.size, 10 * total.size),
        name="gather",
    )(total, came)


def staged(attended, out_weight, adapter_down, adapter_up, row_adapter, adapter_slot):
    f32, bf16 = jnp.float32, jnp.bfloat16
    up, down = adapter_up[0], jnp.swapaxes(adapter_down, 1, 2)[0]
    from_y = swap(attended, 2)
    down_other, up_other = swap(down, 1), swap(up, 1)
    firsts, chips = (7, 6, 5), (4, 3, 2, 1, 0)
    away_first, stay_first, away, stay, token = product(attended, out_weight, (firsts, chips), 44)
    (away_first,) = once((away_first,), from_y)
    came_first = swap(away_first, 1)
    first = [stay_first[i] + came_first[i].astype(f32) for i in range(3)]
    target, outgoing = route(adapter_slot, row_adapter, attended, from_y, token, came_first, down_other, up_other)
    arrived = {k: swap(outgoing[k], 4 * k) for k in (2, 3, 1)}
    arrived[0] = outgoing[0]
    go3 = first[0].astype(bf16)
    y3 = swap(go3, 2)
    (go2,) = once((first[2].astype(bf16),), go3)
    y2 = swap(go2, 2)[None]
    z3 = swap((first[1] + y3.astype(f32)).astype(bf16), 4)[None]
    (away,) = once((away,), target)
    came = swap(away, 1)
    go1 = (stay[1] + came[1].astype(f32)).astype(bf16)
    y1 = swap(go1, 2)[None]
    mine = shrink(down, down_other, arrived)
    groups = ((8, 4, 2, 0), (10, 6), (12,), (14,))
    here, over2, over4, over6 = grow(mine, swap(mine, 1), up, up_other, groups, came, y2)
    over6, over4, over2 = swap(over6, 6), swap(over4, 4), swap(over2, 2)
    (ready2,) = join(target, [stay, came, z3, y2], ((((0, 0), (1, 0), (2, 0), (3, 0)), ()),), f32)
    (sum2,) = join(
        target,
        [ready2[None], over6, over4, over2, here],
        ((((0, 0),), ((1, 0, 6), (2, 0, 4), (3, 0, 2), (4, 0, 0))),),
        bf16,
    )
    z2 = swap(sum2, 8)

    def blocks(m):
        return ((0, chips.index(m)), (1, chips.index(m))), ((2, (4, 2, 1, 0).index(m), 0),)

    sums, own = blocks(2)
    (sum1,) = join(
        target, [stay, came, here, over2, y1, sum2], ((sums + ((4, 0),), own + ((3, 1, 2),)),), bf16
    )
    z1 = swap(sum1, 4)
    (go0,) = join(target, [stay, came, here, sum1], (blocks(1),), bf16)
    y0 = swap(go0, 2)
    (side0,) = join(target, [stay, came, here], (blocks(0),), f32)
    total = gather(gather(side0, z2), z1) + y0.astype(f32)
    return total.astype(bf16)


def general(attended, out_weight, adapter_down, adapter_up, row_adapter, adapter_slot):
    tensor_size = lax.axis_size("tensor")
    device = lax.axis_index("tensor")
    row_count = attended.shape[0]
    held_count = adapter_down.shape[0]
    storage = adapter_slot[row_adapter]
    partial_value = jnp.dot(attended, out_weight, preferred_element_type=jnp.float32)
    base_out = lax.psum_scatter(partial_value, "tensor", scatter_dimension=1, tiled=True)
    owner_of = storage // held_count
    local_index = storage % held_count
    owner_hot = (owner_of[:, None] == jnp.arange(tensor_size, dtype=jnp.int32)[None, :]).astype(
        jnp.int32
    )
    position = jnp.sum(jnp.cumsum(owner_hot, axis=0) * owner_hot, axis=1) - 1
    target = owner_of * CAP + position
    slot_row = (
        jnp.full((tensor_size * CAP,), row_count, jnp.int32)
        .at[target]
        .set(jnp.arange(row_count, dtype=jnp.int32))
    )
    padded = jnp.concatenate([attended, jnp.zeros((1, attended.shape[1]), attended.dtype)], axis=0)
    outgoing = padded[slot_row]
    arrived = lax.all_to_all(outgoing, "tensor", split_axis=0, concat_axis=1, tiled=True)
    own_slots = lax.dynamic_slice_in_dim(slot_row, device * CAP, CAP)
    slot_local = jnp.concatenate([local_index, jnp.zeros((1,), jnp.int32)])[own_slots]
    selector = (slot_local[None, :] == jnp.arange(held_count, dtype=jnp.int32)[:, None]).astype(
        jnp.float32
    )
    all_shrunk = jnp.einsum(
        "cd,adk->ack", arrived, adapter_down, preferred_element_type=jnp.float32
    )
    shrunk = jnp.sum(all_shrunk * selector[:, :, None], axis=0).astype(jnp.bfloat16)
    picked = (selector[:, :, None] * shrunk[None].astype(jnp.float32)).astype(jnp.bfloat16)
    expanded = jnp.einsum(
        "ack,akd->cd", picked, adapter_up, preferred_element_type=jnp.float32
    ).astype(jnp.bfloat16)
    returned = lax.all_to_all(expanded, "tensor", split_axis=1, concat_axis=0, tiled=True)
    delta_out = returned[target]
    return (base_out + delta_out.astype(jnp.float32)).astype(jnp.bfloat16)


def shards(*arrays):
    if lax.axis_size("tensor") == 16 and arrays[2].shape[0] == 1:
        return staged(*arrays)
    return general(*arrays)


def solution(mesh):
    placed = (
        P("groups", "tensor"),
        P("tensor", None),
        P(("groups", "tensor"), None, None),
        P(("groups", "tensor"), None, None),
        P("groups"),
        P("groups"),
    )
    return jax.shard_map(
        shards, mesh=mesh, in_specs=placed, out_specs=P("groups", "tensor"), check_vma=False
    )
```

```python
import functools

import jax
import jax.numpy as jnp
from jax import lax
from jax.experimental import pallas as pl
from jax.experimental.pallas import tpu as pltpu
from jax.sharding import PartitionSpec as P

CAP = 32
IN_VMEM = pl.BlockSpec(memory_space=pltpu.VMEM)
IN_HBM = pl.BlockSpec(memory_space=pltpu.HBM)
ANYWHERE = pl.BlockSpec(memory_space=pl.ANY)
DMA = pltpu.SemaphoreType.DMA


def params(mib):
    return pltpu.CompilerParams(vmem_limit_bytes=mib * 1024 * 1024)


def cost(flops, moved):
    return pl.CostEstimate(flops=flops, bytes_accessed=moved, transcendentals=0)


def shape(dims, dtype=jnp.bfloat16):
    return jax.ShapeDtypeStruct(dims, dtype)


def dot(a, b):
    return jnp.dot(a, b, preferred_element_type=jnp.float32)


def swap(value, mask):
    count = lax.axis_size("tensor")
    return lax.ppermute(value, "tensor", [(t, t ^ mask) for t in range(count)])


def once_kernel(*refs):
    pass


def once(values, *after):
    return pl.pallas_call(
        once_kernel,
        out_shape=[shape(value.shape, value.dtype) for value in values],
        in_specs=[ANYWHERE] * (len(values) + len(after)),
        out_specs=[ANYWHERE] * len(values),
        input_output_aliases={i: i for i in range(len(values))},
        compiler_params=params(1),
        cost_estimate=cost(0, 0),
        name="once",
    )(*values, *after)


def route_kernel(count, layers, slot_hbm, row_ref, own_ref, y_ref, *rest):
    target_ref, out_refs = rest[-3 - layers], rest[-2 - layers : -2]
    slot_ref, slot_sem = rest[-2:]
    rows, width = own_ref.shape
    me = lax.axis_index("tensor")
    fetch = pltpu.make_async_copy(slot_hbm, slot_ref, slot_sem)
    fetch.start()
    fetch.wait()
    ids = row_ref[...]
    owner = jnp.zeros_like(ids)
    for a in range(slot_ref.shape[0]):
        owner = jnp.where(ids == a, slot_ref[a], owner)
    hot = (lax.broadcasted_iota(jnp.int32, (count, rows), 0) == owner).astype(jnp.float32)
    earlier = (
        lax.broadcasted_iota(jnp.int32, (rows, rows), 0)
        < lax.broadcasted_iota(jnp.int32, (rows, rows), 1)
    ).astype(jnp.bfloat16)
    ahead = dot(hot.astype(jnp.bfloat16), earlier)
    place = jnp.sum(ahead * hot, axis=0, keepdims=True).astype(jnp.int32)
    target = owner * CAP + place
    target_ref[...] = target
    j = lax.broadcasted_iota(jnp.int32, (2 * CAP, rows), 0)
    for k in range(layers):
        slots = (me ^ (4 * k) ^ (j // CAP)) * CAP + j % CAP
        select = (slots == target).astype(jnp.bfloat16)
        out_refs[k][:, :width] = dot(select, own_ref[...]).astype(jnp.bfloat16)
        out_refs[k][:, width:] = dot(select, y_ref[...]).astype(jnp.bfloat16)


def route(adapter_slot, row_adapter, own, y, *after):
    rows, width = own.shape
    count = lax.axis_size("tensor")
    layers = count // 4
    found = pl.pallas_call(
        functools.partial(route_kernel, count, layers),
        out_shape=[shape((1, rows), jnp.int32)] + [shape((2 * CAP, 2 * width))] * layers,
        in_specs=[IN_HBM] + [IN_VMEM] * 3 + [ANYWHERE] * len(after),
        out_specs=[IN_VMEM] * (layers + 1),
        scratch_shapes=[pltpu.SMEM(adapter_slot.shape, jnp.int32), DMA(())],
        compiler_params=params(16),
        cost_estimate=cost(8 * layers * CAP * rows * width, 16 * layers * CAP * width),
        name="route",
    )(adapter_slot, row_adapter[None, :], own, y, *after)
    return found[0], found[1:]


def product_kernel(groups, attended_hbm, weight_hbm, *refs):
    token_ref, attended_ref, weight_ref, sems = refs[-4:]
    chips = [m for group in groups for m in group]
    width = weight_ref.shape[2] // 2
    me = lax.axis_index("tensor")
    core, chip = me % 2, me // 2
    fetches = [pltpu.make_async_copy(attended_hbm, attended_ref, sems.at[len(chips)])]
    for i, m in enumerate(chips):
        start = pl.multiple_of((chip ^ m) * 2 * width, 2 * width)
        fetches.append(
            pltpu.make_async_copy(weight_hbm.at[:, pl.ds(start, 2 * width)], weight_ref.at[i], sems.at[i])
        )
    for fetch in fetches:
        fetch.start()
    token_ref[...] = jnp.zeros(token_ref.shape, token_ref.dtype)
    fetches[0].wait()
    there = pl.ds(pl.multiple_of((1 - core) * width, width), width)
    here = pl.ds(pl.multiple_of(core * width, width), width)
    at = 0
    for g, group in enumerate(groups):
        away_ref, stay_ref = refs[2 * g : 2 * g + 2]
        for i in range(len(group)):
            fetches[at + 1].wait()
            away_ref[i] = dot(attended_ref[...], weight_ref[at, :, there]).astype(jnp.bfloat16)
            stay_ref[i] = dot(attended_ref[...], weight_ref[at, :, here])
            at += 1


def product(attended, out_weight, groups, mib):
    rows, depth = attended.shape
    width = out_weight.shape[1] // lax.axis_size("tensor")
    n = sum(len(group) for group in groups)
    out_shape = []
    for group in groups:
        out_shape.append(shape((len(group), rows, width)))
        out_shape.append(shape((len(group), rows, width), jnp.float32))
    out_shape.append(shape((8, 128), jnp.float32))
    return pl.pallas_call(
        functools.partial(product_kernel, groups),
        out_shape=out_shape,
        in_specs=[IN_HBM, IN_HBM],
        out_specs=[IN_VMEM] * len(out_shape),
        scratch_shapes=[
            pltpu.VMEM((rows, depth), jnp.bfloat16),
            pltpu.VMEM((n, depth, 2 * width), jnp.bfloat16),
            DMA((n + 1,)),
        ],
        compiler_params=params(mib),
        cost_estimate=cost(4 * n * rows * depth * width, n * (4 * depth * width + 6 * rows * width)),
        name="product",
    )(attended, out_weight)


def shrink_kernel(distances, down_ref, other_ref, *refs):
    arrived_refs, out_ref = refs[: len(distances)], refs[-1]
    me = lax.axis_index("tensor")
    width = arrived_refs[0].shape[1] // 2
    over = (((1,), (1,)), ((), ()))
    for part, weights_ref in enumerate((down_ref, other_ref)):
        total = jnp.zeros((CAP, down_ref.shape[0]), jnp.float32)
        for k, arrived_ref in zip(distances, arrived_refs):
            for side in range(2):
                block = pl.ds(pl.multiple_of((me ^ (4 * k + 2 * side)) * width, width), width)
                total += lax.dot_general(
                    arrived_ref[part * CAP : (part + 1) * CAP, side * width : (side + 1) * width],
                    weights_ref[:, block],
                    over,
                    preferred_element_type=jnp.float32,
                )
        out_ref[part * CAP : (part + 1) * CAP, :] = total


def shrink(down, other, arrived, *after):
    return pl.pallas_call(
        functools.partial(shrink_kernel, tuple(arrived)),
        out_shape=shape((2 * CAP, down.shape[0]), jnp.float32),
        in_specs=[IN_VMEM] * (2 + len(arrived)) + [ANYWHERE] * len(after),
        out_specs=IN_VMEM,
        compiler_params=params(16),
        cost_estimate=cost(40 * 10**9, 4 * down.size),
        name="shrink",
    )(down, other, *arrived.values(), *after)


def grow_kernel(groups, mine_ref, other_ref, up_ref, up_other_ref, *refs):
    out_refs = refs[-len(groups) :]
    me = lax.axis_index("tensor")
    own = (mine_ref[:CAP, :] + other_ref[CAP:, :]).astype(jnp.bfloat16)
    others = (mine_ref[CAP:, :] + other_ref[:CAP, :]).astype(jnp.bfloat16)
    for masks, out_ref in zip(groups, out_refs):
        width = out_ref.shape[2]
        for i, mask in enumerate(masks):
            block = pl.ds(pl.multiple_of((me ^ mask) * width, width), width)
            out_ref[i, :CAP, :] = dot(own, up_ref[:, block]).astype(jnp.bfloat16)
            out_ref[i, CAP:, :] = dot(others, up_other_ref[:, block]).astype(jnp.bfloat16)


def grow(mine, other, up, up_other, groups, *after):
    width = up.shape[1] // lax.axis_size("tensor")
    return pl.pallas_call(
        functools.partial(grow_kernel, groups),
        out_shape=[shape((len(masks), 2 * CAP, width)) for masks in groups],
        in_specs=[IN_VMEM] * 4 + [ANYWHERE] * len(after),
        out_specs=[IN_VMEM] * len(groups),
        compiler_params=params(16),
        cost_estimate=cost(4 * CAP * up.size, 4 * up.size),
        name="grow",
    )(mine, other, up, up_other, *after)


def join_kernel(terms, target_ref, *refs):
    out_refs = refs[-len(terms) :]
    rows = target_ref.shape[1]
    me = lax.axis_index("tensor")
    j = lax.broadcasted_iota(jnp.int32, (2 * CAP, rows), 0)
    picks = {}
    for (blocks, grown), out_ref in zip(terms, out_refs):
        total = jnp.zeros(out_ref.shape, jnp.float32)
        for at, i in blocks:
            total += refs[at][i].astype(jnp.float32)
        for at, i, mask in grown:
            if mask not in picks:
                slots = (me ^ mask ^ (j // CAP)) * CAP + j % CAP
                picks[mask] = (slots == target_ref[...]).astype(jnp.bfloat16)
            total += lax.dot_general(
                picks[mask], refs[at][i], (((0,), (0,)), ((), ())), preferred_element_type=jnp.float32
            )
        out_ref[...] = total.astype(out_ref.dtype)


def join(target, operands, terms, dtype):
    rows, width = target.shape[1], operands[0].shape[2]
    n = len(terms)
    return pl.pallas_call(
        functools.partial(join_kernel, terms),
        out_shape=[shape((rows, width), dtype)] * n,
        in_specs=[IN_VMEM] * (1 + len(operands)),
        out_specs=[IN_VMEM] * n,
        compiler_params=params(24),
        cost_estimate=cost(4 * n * CAP * rows * width, 10 * n * rows * width),
        name="join",
    )(target, *operands)


def gather_kernel(sum_ref, came_ref, out_ref):
    out_ref[...] = sum_ref[...] + came_ref[...].astype(jnp.float32)


def gather(total, came):
    return pl.pallas_call(
        gather_kernel,
        out_shape=shape(total.shape, jnp.float32),
        in_specs=[IN_VMEM] * 2,
        out_specs=IN_VMEM,
        compiler_params=params(16),
        cost_estimate=cost(total.size, 10 * total.size),
        name="gather",
    )(total, came)


def staged(attended, out_weight, adapter_down, adapter_up, row_adapter, adapter_slot):
    f32, bf16 = jnp.float32, jnp.bfloat16
    up, down = adapter_up[0], jnp.swapaxes(adapter_down, 1, 2)[0]
    from_y = swap(attended, 2)
    down_other, up_other = swap(down, 1), swap(up, 1)
    firsts, chips = (7, 6, 5), (4, 3, 2, 1, 0)
    away_first, stay_first, away, stay, token = product(attended, out_weight, (firsts, chips), 44)
    (away_first,) = once((away_first,), from_y)
    came_first = swap(away_first, 1)
    first = [stay_first[i] + came_first[i].astype(f32) for i in range(3)]
    target, outgoing = route(adapter_slot, row_adapter, attended, from_y, token, down_other, up_other)
    arrived = {k: swap(outgoing[k], 4 * k) for k in (1, 3, 2)}
    arrived[0] = outgoing[0]
    go3 = first[0].astype(bf16)
    y3 = swap(go3, 2)
    (go2,) = once((first[2].astype(bf16),), go3)
    y2 = swap(go2, 2)[None]
    z3 = swap((first[1] + y3.astype(f32)).astype(bf16), 4)[None]
    (away,) = once((away,), target)
    came = swap(away, 1)
    go1 = (stay[1] + came[1].astype(f32)).astype(bf16)
    y1 = swap(go1, 2)[None]
    mine = shrink(down, down_other, arrived)
    groups = ((8, 4, 2, 0), (10, 6), (12,), (14,))
    here, over2, over4, over6 = grow(mine, swap(mine, 1), up, up_other, groups, came, y2)
    over6, over4, over2 = swap(over6, 6), swap(over4, 4), swap(over2, 2)
    (ready2,) = join(target, [stay, came, z3, y2], ((((0, 0), (1, 0), (2, 0), (3, 0)), ()),), f32)
    (sum2,) = join(
        target,
        [ready2[None], over6, over4, over2, here],
        ((((0, 0),), ((1, 0, 6), (2, 0, 4), (3, 0, 2), (4, 0, 0))),),
        bf16,
    )
    z2 = swap(sum2, 8)

    def blocks(m):
        return ((0, chips.index(m)), (1, chips.index(m))), ((2, (4, 2, 1, 0).index(m), 0),)

    sums, own = blocks(2)
    (sum1,) = join(
        target, [stay, came, here, over2, y1, sum2], ((sums + ((4, 0),), own + ((3, 1, 2),)),), bf16
    )
    z1 = swap(sum1, 4)
    (go0,) = join(target, [stay, came, here, sum1], (blocks(1),), bf16)
    y0 = swap(go0, 2)
    (side0,) = join(target, [stay, came, here], (blocks(0),), f32)
    total = gather(gather(side0, z2), z1) + y0.astype(f32)
    return total.astype(bf16)


def general(attended, out_weight, adapter_down, adapter_up, row_adapter, adapter_slot):
    tensor_size = lax.axis_size("tensor")
    device = lax.axis_index("tensor")
    row_count = attended.shape[0]
    held_count = adapter_down.shape[0]
    storage = adapter_slot[row_adapter]
    partial_value = jnp.dot(attended, out_weight, preferred_element_type=jnp.float32)
    base_out = lax.psum_scatter(partial_value, "tensor", scatter_dimension=1, tiled=True)
    owner_of = storage // held_count
    local_index = storage % held_count
    owner_hot = (owner_of[:, None] == jnp.arange(tensor_size, dtype=jnp.int32)[None, :]).astype(
        jnp.int32
    )
    position = jnp.sum(jnp.cumsum(owner_hot, axis=0) * owner_hot, axis=1) - 1
    target = owner_of * CAP + position
    slot_row = (
        jnp.full((tensor_size * CAP,), row_count, jnp.int32)
        .at[target]
        .set(jnp.arange(row_count, dtype=jnp.int32))
    )
    padded = jnp.concatenate([attended, jnp.zeros((1, attended.shape[1]), attended.dtype)], axis=0)
    outgoing = padded[slot_row]
    arrived = lax.all_to_all(outgoing, "tensor", split_axis=0, concat_axis=1, tiled=True)
    own_slots = lax.dynamic_slice_in_dim(slot_row, device * CAP, CAP)
    slot_local = jnp.concatenate([local_index, jnp.zeros((1,), jnp.int32)])[own_slots]
    selector = (slot_local[None, :] == jnp.arange(held_count, dtype=jnp.int32)[:, None]).astype(
        jnp.float32
    )
    all_shrunk = jnp.einsum(
        "cd,adk->ack", arrived, adapter_down, preferred_element_type=jnp.float32
    )
    shrunk = jnp.sum(all_shrunk * selector[:, :, None], axis=0).astype(jnp.bfloat16)
    picked = (selector[:, :, None] * shrunk[None].astype(jnp.float32)).astype(jnp.bfloat16)
    expanded = jnp.einsum(
        "ack,akd->cd", picked, adapter_up, preferred_element_type=jnp.float32
    ).astype(jnp.bfloat16)
    returned = lax.all_to_all(expanded, "tensor", split_axis=1, concat_axis=0, tiled=True)
    delta_out = returned[target]
    return (base_out + delta_out.astype(jnp.float32)).astype(jnp.bfloat16)


def shards(*arrays):
    if lax.axis_size("tensor") == 16 and arrays[2].shape[0] == 1:
        return staged(*arrays)
    return general(*arrays)


def solution(mesh):
    placed = (
        P("groups", "tensor"),
        P("tensor", None),
        P(("groups", "tensor"), None, None),
        P(("groups", "tensor"), None, None),
        P("groups"),
        P("groups"),
    )
    return jax.shard_map(
        shards, mesh=mesh, in_specs=placed, out_specs=P("groups", "tensor"), check_vma=False
    )
```
